32 devices in a mesh: grp: 4 (over z), ctx: 8 (over y, x, core).
Axes of the slice: x: 2, y: 2, z: 4, core: 2. Of those that a mesh axis runs over, the one named last changes fastest.
Arguments:
- inputs: bfloat16 [2, 4, 512, 1152], P(None, 'grp', 'ctx'), may hold values from -6 to 6
- segments: int32 [2, 4, 512], P(None, 'grp', 'ctx'), may hold values from 0 to 16, as said below
- query_weight: bfloat16 [1327104], P(('grp', 'ctx')), may hold values from -0.1875 to 0.1875
- key_weight: bfloat16 [442368], P(('grp', 'ctx')), may hold values from -0.1875 to 0.1875
- value_weight: bfloat16 [442368], P(('grp', 'ctx')), may hold values from -0.1875 to 0.1875
- output_weight: bfloat16 [1327104], P(('grp', 'ctx')), may hold values from -3 to 3
- gate_weight: bfloat16 [3538944], P(('grp', 'ctx')), may hold values from -0.1875 to 0.1875
- up_weight: bfloat16 [3538944], P(('grp', 'ctx')), may hold values from -0.1875 to 0.1875
- down_weight: bfloat16 [3538944], P(('grp', 'ctx')), may hold values from -0.109375 to 0.109375
- norm_gain_pair: bfloat16 [2304], P(('grp', 'ctx')), may hold values from 0.5 to 1.5
- cotangent: bfloat16 [2, 4, 512, 1152], P(None, 'grp', 'ctx'), may hold values from -6 to 6
Outputs:
- outputs: bfloat16 [2, 4, 512, 1152], P(None, 'grp', 'ctx')
- input_grad: bfloat16 [2, 4, 512, 1152], P(None, 'grp', 'ctx')
- grad_query: float32 [1327104], P(('grp', 'ctx'))
- grad_key: float32 [442368], P(('grp', 'ctx'))
- grad_value: float32 [442368], P(('grp', 'ctx'))
- grad_output: float32 [1327104], P(('grp', 'ctx'))
- grad_gate: float32 [3538944], P(('grp', 'ctx'))
- grad_up: float32 [3538944], P(('grp', 'ctx'))
- grad_down: float32 [3538944], P(('grp', 'ctx'))
- grad_gains: float32 [2304], P(('grp', 'ctx'))
The draws below stay inside these ranges and needn't reach their ends.
Inputs may be any that keep to these rules, and one draw needn't show every extreme that they name: `segments`: segment numbers never fall along a packed sequence.
All inputs are finite; a program needn't handle non-finite values.
Results may differ from the reference program's by a relative error of at most 0.019.
Values may be sent and summed in bfloat16 or wider, within the bound.
No kernel may reach another device: no remote copies, remote signals or barrier semaphores. Data moves between devices by JAX's collectives and lax.ppermute only.
A program may use at most 256 MiB of HBM per device.

```python
import jax
import jax.numpy as jnp
from jax import lax

MODEL_WIDTH = 1152
QUERY_HEADS = 18
KEY_HEADS = 6
HEAD_SIZE = 64
HIDDEN_UNITS = 3072
MICRO = 2
TOK = 64
SEQS = 4
LENGTH = 512


def draw_segments(key, part):
    key = jax.random.fold_in(key, 7)
    first_key, second_key, third_key, fourth_key = jax.random.split(key, 4)
    cut_raw = jax.random.randint(first_key, (MICRO, SEQS, 16), 0, 32)
    cuts = LENGTH * cut_raw * cut_raw * cut_raw // 32768
    places = jnp.arange(LENGTH, dtype=jnp.int32)
    heavy = jnp.sum((cuts[:, :, None, :] <= places[None, None, :, None]).astype(jnp.int32), axis=-1)
    chosen = jax.random.randint(second_key, (SEQS,), 0, MICRO)
    tail = jax.random.randint(third_key, (MICRO, SEQS), 1, TOK)
    head = jax.random.randint(fourth_key, (MICRO, SEQS), 1, TOK)
    after_head = (places[None, None, :] >= head[:, :, None]).astype(jnp.int32)
    in_tail = (places[None, None, :] >= LENGTH - tail[:, :, None]).astype(jnp.int32)
    single = after_head + in_tail
    picked = jnp.arange(MICRO, dtype=jnp.int32)[:, None, None] == chosen[None, :, None]
    return jnp.where(picked, single, heavy).astype(jnp.int32)


def shard_levels(stream_key, extent, cuts, low, high):
    gain, own = 1.0, jax.random.fold_in(stream_key, 6)
    for position, shards_of in cuts:
        heights = jnp.exp(jax.random.uniform(jax.random.fold_in(own, position), (shards_of,), jnp.float32, low / len(cuts), high / len(cuts)))
        gain = gain * jnp.repeat(heights, extent[position] // shards_of).reshape([-1 if axis == position else 1 for axis in range(len(extent))])
    return gain


def bell_draw(key, shape, deviation, reach, cuts=(), kind=jnp.bfloat16):
    loudness = shard_levels(key, shape, cuts, -0.22, 0.18) if cuts else 1.0
    entries = jax.random.normal(key, shape, jnp.float32) * deviation * loudness
    return jnp.minimum(jnp.maximum(entries, -reach), reach).astype(kind)


def setup_inputs(seed: int = 0) -> dict:
    keys = jax.random.split(jax.random.key(seed), 12)
    return {
        "inputs": bell_draw(keys[0], (MICRO, SEQS, LENGTH, MODEL_WIDTH), 1.0, 6.0, ((1, 4), (2, 8))),
        "segments": draw_segments(jax.random.fold_in(keys[11], 71), 0),
        "query_weight": bell_draw(keys[2], (MODEL_WIDTH * QUERY_HEADS * HEAD_SIZE,), MODEL_WIDTH ** -0.5, 0.1875, ((0, 32),)),
        "key_weight": bell_draw(keys[3], (MODEL_WIDTH * KEY_HEADS * HEAD_SIZE,), MODEL_WIDTH ** -0.5, 0.1875, ((0, 32),)),
        "value_weight": bell_draw(keys[4], (MODEL_WIDTH * KEY_HEADS * HEAD_SIZE,), MODEL_WIDTH ** -0.5, 0.1875, ((0, 32),)),
        "output_weight": bell_draw(keys[5], (QUERY_HEADS * HEAD_SIZE * MODEL_WIDTH,), (max(QUERY_HEADS * HEAD_SIZE // 256, 1)) ** -0.5, 3.0, ((0, 32),)),
        "gate_weight": bell_draw(keys[6], (MODEL_WIDTH * HIDDEN_UNITS,), MODEL_WIDTH ** -0.5, 0.1875, ((0, 32),)),
        "up_weight": bell_draw(keys[7], (MODEL_WIDTH * HIDDEN_UNITS,), MODEL_WIDTH ** -0.5, 0.1875, ((0, 32),)),
        "down_weight": bell_draw(keys[8], (HIDDEN_UNITS * MODEL_WIDTH,), HIDDEN_UNITS ** -0.5, 0.109375, ((0, 32),)),
        "norm_gain_pair": jnp.clip(1.0 + 0.1 * jax.random.normal(keys[9], (2 * MODEL_WIDTH,), jnp.float32), 0.5, 1.5).astype(jnp.bfloat16),
        "cotangent": bell_draw(keys[10], (MICRO, SEQS, LENGTH, MODEL_WIDTH), 1.0, 6.0, ((1, 4), (2, 8))),
    }


HIGH = lax.Precision.HIGHEST
EPS = 1e-05
THETA = 10000.0
NEGATIVE_LARGE = -1e+30

@jax.custom_vjp
def reduced_precision(v):
    return lax.optimization_barrier(v.astype(jnp.bfloat16)).astype(jnp.float32)

@jax.custom_vjp
def reduced_backward(v):
    return v

def low_keep(v):
    return (reduced_precision(v), None)

def low_pass(kept, grad):
    return (grad,)

def back_keep(v):
    return (v, None)

def back_low(kept, grad):
    return (reduced_precision(grad),)
reduced_precision.defvjp(low_keep, low_pass)
reduced_backward.defvjp(back_keep, back_low)

def matrix_product(left, right):
    return jnp.dot(left, right, precision=HIGH, preferred_element_type=jnp.float32)

def rope_tables(token_length):
    half = HEAD_SIZE // 2
    freq = THETA ** (-jnp.arange(half, dtype=jnp.float32) * 2.0 / HEAD_SIZE)
    angle = jnp.arange(token_length, dtype=jnp.float32)[:, None] * freq[None, :]
    return (jnp.cos(angle)[:, None, :], jnp.sin(angle)[:, None, :])

def rotary_apply(value_rows, cosine_table, sine_table):
    half = value_rows.shape[-1] // 2
    first = value_rows[..., :half]
    second = value_rows[..., half:]
    return jnp.concatenate([first * cosine_table - second * sine_table, second * cosine_table + first * sine_table], -1)

def layer_seq(xrow, seg_row, weight_matrices):
    query_weight, key_weight, value_weight, output_weight, gate_weight, up_weight, down_weight, gains = weight_matrices
    token_length = xrow.shape[0]
    query_groups = QUERY_HEADS // KEY_HEADS
    scale = HEAD_SIZE ** (-0.5)
    gain_one = gains[:MODEL_WIDTH]
    gain_two = gains[MODEL_WIDTH:]
    normed = xrow * lax.rsqrt(lax.optimization_barrier(jnp.mean(xrow * xrow, axis=-1, keepdims=True)) + EPS)
    activated_hidden = reduced_precision(normed * gain_one)
    cosine_table, sine_table = rope_tables(token_length)
    query = reduced_precision(rotary_apply(reduced_backward(matrix_product(activated_hidden, query_weight)).reshape(token_length, QUERY_HEADS, HEAD_SIZE), cosine_table, sine_table))
    key_rows = reduced_precision(rotary_apply(reduced_backward(matrix_product(activated_hidden, key_weight)).reshape(token_length, KEY_HEADS, HEAD_SIZE), cosine_table, sine_table))
    value_rows = reduced_precision(reduced_backward(matrix_product(activated_hidden, value_weight))).reshape(token_length, KEY_HEADS, HEAD_SIZE)
    block_tile = min(512, token_length)
    places = jnp.arange(token_length, dtype=jnp.int32)

    def attend(args):
        query_block, qplace, qseg = args
        grouped_queries = query_block.reshape(block_tile, KEY_HEADS, query_groups, HEAD_SIZE)
        scores = reduced_backward(jnp.einsum('tkgd,nkd->kgtn', grouped_queries, key_rows, precision=HIGH) * scale)
        mask = (places[None, :] <= qplace[:, None]) & (seg_row[None, :] == qseg[:, None])
        scores = jnp.where(mask, scores, NEGATIVE_LARGE)
        best = lax.optimization_barrier(jnp.max(scores, axis=-1, keepdims=True))
        expo = jnp.exp(scores - best)
        probs = reduced_precision(expo / lax.optimization_barrier(jnp.sum(expo, axis=-1, keepdims=True)))
        mixed = jnp.einsum('kgtn,nkd->tkgd', probs, value_rows, precision=HIGH)
        return mixed.reshape(block_tile, QUERY_HEADS * HEAD_SIZE)
    attended = lax.map(jax.checkpoint(attend), (query.reshape(token_length // block_tile, block_tile, QUERY_HEADS, HEAD_SIZE), places.reshape(-1, block_tile), seg_row.reshape(-1, block_tile)))
    attended = reduced_precision(reduced_backward(attended.reshape(token_length, QUERY_HEADS * HEAD_SIZE)))
    residual = xrow + reduced_backward(matrix_product(attended, output_weight))
    normed_two = residual * lax.rsqrt(lax.optimization_barrier(jnp.mean(residual * residual, axis=-1, keepdims=True)) + EPS)
    mixed = reduced_precision(normed_two * gain_two)
    gate = reduced_backward(matrix_product(mixed, gate_weight))
    upper = reduced_backward(matrix_product(mixed, up_weight))
    hidden = reduced_precision(jax.nn.silu(gate) * upper)
    return residual + reduced_backward(matrix_product(hidden, down_weight))

def forward(segments, inputs, query_weight, key_weight, value_weight, output_weight, gate_weight, up_weight, down_weight, norm_gain_pair):
    weight_matrices = (query_weight.reshape(MODEL_WIDTH, QUERY_HEADS * HEAD_SIZE), key_weight.reshape(MODEL_WIDTH, KEY_HEADS * HEAD_SIZE), value_weight.reshape(MODEL_WIDTH, KEY_HEADS * HEAD_SIZE), output_weight.reshape(QUERY_HEADS * HEAD_SIZE, MODEL_WIDTH), gate_weight.reshape(MODEL_WIDTH, HIDDEN_UNITS), up_weight.reshape(MODEL_WIDTH, HIDDEN_UNITS), down_weight.reshape(HIDDEN_UNITS, MODEL_WIDTH), norm_gain_pair)
    token_rows = inputs.reshape(MICRO * SEQS, LENGTH, MODEL_WIDTH)
    seg_rows = segments.reshape(MICRO * SEQS, LENGTH)

    def one_row(args):
        return layer_seq(args[0], args[1], weight_matrices)
    result = lax.map(jax.checkpoint(one_row), (token_rows, seg_rows))
    return result.reshape(inputs.shape)

def reference(inputs, segments, query_weight, key_weight, value_weight, output_weight, gate_weight, up_weight, down_weight, norm_gain_pair, cotangent):
    floats = [a.astype(jnp.float32) for a in (inputs, query_weight, key_weight, value_weight, output_weight, gate_weight, up_weight, down_weight, norm_gain_pair)]
    result, pullback = jax.vjp(lambda *args: forward(segments, *args), *floats)
    grads = pullback(cotangent.astype(jnp.float32))
    return (result.astype(jnp.bfloat16), grads[0].astype(jnp.bfloat16), grads[1], grads[2], grads[3], grads[4], grads[5], grads[6], grads[7], grads[8])
```

```python
import jax
import jax.numpy as jnp
from jax import lax
from jax.experimental import pallas as pl
from jax.experimental.pallas import tpu as pltpu
from jax.sharding import PartitionSpec as P

MODEL_WIDTH = 1152
QUERY_HEADS = 18
KEY_HEADS = 6
HEAD_SIZE = 64
HIDDEN_UNITS = 3072
MICRO = 2


EPS = 1e-05
THETA = 10000.0
NEGATIVE_LARGE = -1e30


def rope_parts(positions):
    half = HEAD_SIZE // 2
    freq = THETA ** (-jnp.arange(half, dtype=jnp.float32) * 2.0 / HEAD_SIZE)
    angle = positions.astype(jnp.float32)[:, None] * freq[None, :]
    return (jnp.cos(angle)[:, None, :], jnp.sin(angle)[:, None, :])


def rotary_apply(value_rows, cosine_table, sine_table, sign):
    half = value_rows.shape[-1] // 2
    first = value_rows[..., :half]
    second = value_rows[..., half:]
    return jnp.concatenate(
        [
            first * cosine_table - sign * second * sine_table,
            second * cosine_table + sign * first * sine_table,
        ],
        -1,
    )


def shape_weights(full_precision):
    return (
        full_precision[0].reshape(MODEL_WIDTH, QUERY_HEADS * HEAD_SIZE),
        full_precision[1].reshape(MODEL_WIDTH, KEY_HEADS * HEAD_SIZE),
        full_precision[2].reshape(MODEL_WIDTH, KEY_HEADS * HEAD_SIZE),
        full_precision[3].reshape(QUERY_HEADS * HEAD_SIZE, MODEL_WIDTH),
        full_precision[4].reshape(MODEL_WIDTH, HIDDEN_UNITS),
        full_precision[5].reshape(MODEL_WIDTH, HIDDEN_UNITS),
        full_precision[6].reshape(HIDDEN_UNITS, MODEL_WIDTH),
        full_precision[7],
    )


def allowed(key_pos, key_seg, query_pos, query_seg):
    return (key_pos[None, :] <= query_pos[:, None]) & (key_seg[None, :] == query_seg[:, None])


def online_step(
    state, grouped_queries, key_block, value_block, pblock, sblock, query_pos, query_seg
):
    best, total, accum = state
    block_span = key_block.shape[0]
    key_head_rows = key_block.reshape(block_span, KEY_HEADS, HEAD_SIZE)
    value_head_rows = value_block.reshape(block_span, KEY_HEADS, HEAD_SIZE)
    scores = jnp.einsum(
        "tkgd,nkd->kgtn", grouped_queries, key_head_rows, preferred_element_type=jnp.float32
    ) * HEAD_SIZE ** (-0.5)
    mask = allowed(pblock, sblock, query_pos, query_seg)[None, None]
    scores = jnp.where(mask, scores, NEGATIVE_LARGE)
    new_best = jnp.maximum(best, jnp.max(scores, axis=-1))
    factor = jnp.exp(best - new_best)
    expo = jnp.where(mask, jnp.exp(scores - new_best[..., None]), 0.0)
    total = total * factor + jnp.sum(expo, axis=-1)
    accum = accum * factor[..., None] + jnp.einsum(
        "kgtn,nkd->kgtd",
        expo.astype(jnp.bfloat16),
        value_head_rows,
        preferred_element_type=jnp.float32,
    )
    return (new_best, total, accum)


def guarded_step(
    state, grouped_queries, key_block, value_block, pblock, sblock, query_pos, query_seg
):

    def guarded_work(current):
        return online_step(
            current, grouped_queries, key_block, value_block, pblock, sblock, query_pos, query_seg
        )

    def guarded_leave(current):
        return current

    return lax.cond(pblock[0] <= query_pos[-1], guarded_work, guarded_leave, state)


def online_blocks(
    carry, grouped_queries, key_rows, value_rows, key_pos, key_seg, query_pos, query_seg
):
    count = key_rows.shape[0]
    block_size = 512 if count > 512 and count % 512 == 0 else count
    if block_size == count:
        return guarded_step(
            carry, grouped_queries, key_rows, value_rows, key_pos, key_seg, query_pos, query_seg
        )

    def step(state, block_tile):
        return (
            guarded_step(
                state,
                grouped_queries,
                block_tile[0],
                block_tile[1],
                block_tile[2],
                block_tile[3],
                query_pos,
                query_seg,
            ),
            None,
        )

    block_tiles = (
        key_rows.reshape(-1, block_size, key_rows.shape[1]),
        value_rows.reshape(-1, block_size, value_rows.shape[1]),
        key_pos.reshape(-1, block_size),
        key_seg.reshape(-1, block_size),
    )
    carry, _ = lax.scan(step, carry, block_tiles)
    return carry


def forward_rows(xrow, seg_row, query_seg, positions, cosine_table, sine_table, weight_matrices):
    (
        query_weight,
        key_weight,
        value_weight,
        output_weight,
        gate_weight,
        up_weight,
        down_weight,
        gains,
    ) = weight_matrices
    token_rows = xrow.shape[0]
    query_groups = QUERY_HEADS // KEY_HEADS
    gain_one = gains[:MODEL_WIDTH].astype(jnp.float32)
    gain_two = gains[MODEL_WIDTH:].astype(jnp.float32)
    inv_one = lax.rsqrt(jnp.mean(xrow * xrow, axis=-1, keepdims=True) + EPS)
    normed_one = xrow * inv_one
    activated_hidden = (normed_one * gain_one).astype(jnp.bfloat16)
    query_unrotated = jnp.dot(
        activated_hidden, query_weight, preferred_element_type=jnp.float32
    ).reshape(token_rows, QUERY_HEADS, HEAD_SIZE)
    key_unrotated = jnp.dot(
        activated_hidden, key_weight, preferred_element_type=jnp.float32
    ).reshape(token_rows, KEY_HEADS, HEAD_SIZE)
    value_raw = jnp.dot(activated_hidden, value_weight, preferred_element_type=jnp.float32)
    grouped_queries = (
        rotary_apply(query_unrotated, cosine_table, sine_table, 1.0)
        .astype(jnp.bfloat16)
        .reshape(token_rows, KEY_HEADS, query_groups, HEAD_SIZE)
    )
    key_rows = (
        rotary_apply(key_unrotated, cosine_table, sine_table, 1.0)
        .astype(jnp.bfloat16)
        .reshape(token_rows, KEY_HEADS * HEAD_SIZE)
    )
    value_rows = value_raw.astype(jnp.bfloat16)
    start_state = (
        jnp.full((KEY_HEADS, query_groups, token_rows), NEGATIVE_LARGE, jnp.float32),
        jnp.zeros((KEY_HEADS, query_groups, token_rows), jnp.float32),
        jnp.zeros((KEY_HEADS, query_groups, token_rows, HEAD_SIZE), jnp.float32),
    )
    piece = (
        lax.all_gather(key_rows, "ctx", axis=0, tiled=True),
        lax.all_gather(value_rows, "ctx", axis=0, tiled=True),
    )
    count = piece[0].shape[0]
    key_pos = jnp.arange(count, dtype=jnp.int32)
    best, total, accum = online_blocks(
        start_state, grouped_queries, piece[0], piece[1], key_pos, seg_row, positions, query_seg
    )
    attn = accum / total[..., None]
    lse = best + jnp.log(total)
    attn_low = (
        jnp.transpose(attn, (2, 0, 1, 3))
        .reshape(token_rows, QUERY_HEADS * HEAD_SIZE)
        .astype(jnp.bfloat16)
    )
    residual = xrow + jnp.dot(attn_low, output_weight, preferred_element_type=jnp.float32)
    inv_two = lax.rsqrt(jnp.mean(residual * residual, axis=-1, keepdims=True) + EPS)
    normed_two = residual * inv_two
    mixed = (normed_two * gain_two).astype(jnp.bfloat16)
    gate = jnp.dot(mixed, gate_weight, preferred_element_type=jnp.float32)
    upper = jnp.dot(mixed, up_weight, preferred_element_type=jnp.float32)
    hidden = (jax.nn.silu(gate) * upper).astype(jnp.bfloat16)
    result = residual + jnp.dot(hidden, down_weight, preferred_element_type=jnp.float32)
    kept = (
        inv_one,
        normed_one,
        activated_hidden,
        grouped_queries,
        key_rows,
        value_rows,
        attn,
        lse,
        attn_low,
        inv_two,
        normed_two,
        mixed,
        gate,
        upper,
        hidden,
    )
    return (result, kept)


def backward_rows(
    dout, seg_row, query_seg, positions, cosine_table, sine_table, weight_matrices, kept
):
    (
        query_weight,
        key_weight,
        value_weight,
        output_weight,
        gate_weight,
        up_weight,
        down_weight,
        gains,
    ) = weight_matrices
    (
        inv_one,
        normed_one,
        activated_hidden,
        grouped_queries,
        key_rows,
        value_rows,
        attn,
        lse,
        attn_low,
        inv_two,
        normed_two,
        mixed,
        gate,
        upper,
        hidden,
    ) = kept
    token_rows = dout.shape[0]
    query_groups = QUERY_HEADS // KEY_HEADS
    scale = HEAD_SIZE ** (-0.5)
    gain_one = gains[:MODEL_WIDTH].astype(jnp.float32)
    gain_two = gains[MODEL_WIDTH:].astype(jnp.float32)
    dout_low = dout.astype(jnp.bfloat16)
    grad_down = jnp.einsum("tf,td->fd", hidden, dout_low, preferred_element_type=jnp.float32)
    grad_hidden = jnp.einsum("td,fd->tf", dout_low, down_weight, preferred_element_type=jnp.float32)
    sigma = jax.nn.sigmoid(gate)
    grad_gate_act = (grad_hidden * upper * (sigma + gate * sigma * (1.0 - sigma))).astype(
        jnp.bfloat16
    )
    grad_up_act = (grad_hidden * (gate * sigma)).astype(jnp.bfloat16)
    grad_gate = jnp.einsum("te,tf->ef", mixed, grad_gate_act, preferred_element_type=jnp.float32)
    grad_up = jnp.einsum("te,tf->ef", mixed, grad_up_act, preferred_element_type=jnp.float32)
    grad_mixed = jnp.einsum(
        "tf,ef->te", grad_gate_act, gate_weight, preferred_element_type=jnp.float32
    ) + jnp.einsum("tf,ef->te", grad_up_act, up_weight, preferred_element_type=jnp.float32)
    grad_gain_two = jnp.sum(grad_mixed * normed_two, axis=0)
    scaled_two = grad_mixed * gain_two
    grad_res = dout + inv_two * (
        scaled_two - normed_two * jnp.mean(scaled_two * normed_two, axis=-1, keepdims=True)
    )
    grad_branch = grad_res.astype(jnp.bfloat16)
    grad_output = jnp.einsum("te,td->ed", attn_low, grad_branch, preferred_element_type=jnp.float32)
    attention_gradient = jnp.einsum(
        "td,ed->te", grad_branch, output_weight, preferred_element_type=jnp.float32
    )
    attention_gradient_reduced = attention_gradient.astype(jnp.bfloat16).reshape(
        token_rows, KEY_HEADS, query_groups, HEAD_SIZE
    )
    delta = jnp.einsum("tkgd,kgtd->kgt", attention_gradient_reduced.astype(jnp.float32), attn)
    key_rows_total, value_rows_total = (
        lax.all_gather(key_rows, "ctx", axis=0, tiled=True),
        lax.all_gather(value_rows, "ctx", axis=0, tiled=True),
    )
    token_length = key_rows_total.shape[0]
    block_size = min(512, token_length)

    def reverse_block_step(grad_query, block_tile):
        key_block, value_block, pblock, sblock = block_tile

        def reverse_work(current):
            key_head_rows = key_block.reshape(block_size, KEY_HEADS, HEAD_SIZE)
            value_head_rows = value_block.reshape(block_size, KEY_HEADS, HEAD_SIZE)
            scores = (
                jnp.einsum(
                    "tkgd,nkd->kgtn",
                    grouped_queries,
                    key_head_rows,
                    preferred_element_type=jnp.float32,
                )
                * scale
            )
            mask = allowed(pblock, sblock, positions, query_seg)[None, None]
            probs = jnp.where(mask, jnp.exp(scores - lse[..., None]), 0.0)
            grad_probs = jnp.einsum(
                "tkgd,nkd->kgtn",
                attention_gradient_reduced,
                value_head_rows,
                preferred_element_type=jnp.float32,
            )
            grad_scores = (probs * (grad_probs - delta[..., None])).astype(jnp.bfloat16)
            updated_state = current + jnp.einsum(
                "kgtn,nkd->tkgd", grad_scores, key_head_rows, preferred_element_type=jnp.float32
            )
            key_gradient_term = (
                jnp.einsum(
                    "kgtn,tkgd->nkd",
                    grad_scores,
                    grouped_queries,
                    preferred_element_type=jnp.float32,
                )
                * scale
            )
            value_gradient_term = jnp.einsum(
                "kgtn,tkgd->nkd",
                probs.astype(jnp.bfloat16),
                attention_gradient_reduced,
                preferred_element_type=jnp.float32,
            )
            return (
                updated_state,
                (
                    key_gradient_term.reshape(block_size, KEY_HEADS * HEAD_SIZE),
                    value_gradient_term.reshape(block_size, KEY_HEADS * HEAD_SIZE),
                ),
            )

        def reverse_leave(current):
            empty_state = jnp.zeros((block_size, KEY_HEADS * HEAD_SIZE), jnp.float32)
            return (current, (empty_state, empty_state))

        return lax.cond(pblock[0] <= positions[-1], reverse_work, reverse_leave, grad_query)

    places = jnp.arange(token_length, dtype=jnp.int32)
    block_tiles = (
        key_rows_total.reshape(-1, block_size, KEY_HEADS * HEAD_SIZE),
        value_rows_total.reshape(-1, block_size, KEY_HEADS * HEAD_SIZE),
        places.reshape(-1, block_size),
        seg_row.reshape(-1, block_size),
    )
    grad_query_rot, (key_gradient_terms, value_gradient_terms) = lax.scan(
        reverse_block_step,
        jnp.zeros((token_rows, KEY_HEADS, query_groups, HEAD_SIZE), jnp.float32),
        block_tiles,
    )
    key_gradient_rows, grad_values = (
        lax.psum_scatter(
            key_gradient_terms.reshape(token_length, KEY_HEADS * HEAD_SIZE),
            "ctx",
            scatter_dimension=0,
            tiled=True,
        ),
        lax.psum_scatter(
            value_gradient_terms.reshape(token_length, KEY_HEADS * HEAD_SIZE),
            "ctx",
            scatter_dimension=0,
            tiled=True,
        ),
    )
    grad_q_low = (
        rotary_apply(
            (grad_query_rot * scale).reshape(token_rows, QUERY_HEADS, HEAD_SIZE),
            cosine_table,
            sine_table,
            -1.0,
        )
        .astype(jnp.bfloat16)
        .reshape(token_rows, QUERY_HEADS * HEAD_SIZE)
    )
    grad_k_low = (
        rotary_apply(
            key_gradient_rows.reshape(token_rows, KEY_HEADS, HEAD_SIZE),
            cosine_table,
            sine_table,
            -1.0,
        )
        .astype(jnp.bfloat16)
        .reshape(token_rows, KEY_HEADS * HEAD_SIZE)
    )
    grad_v_low = grad_values.astype(jnp.bfloat16)
    grad_wq = jnp.einsum(
        "te,tf->ef", activated_hidden, grad_q_low, preferred_element_type=jnp.float32
    )
    grad_wk = jnp.einsum(
        "te,tf->ef", activated_hidden, grad_k_low, preferred_element_type=jnp.float32
    )
    grad_wv = jnp.einsum(
        "te,tf->ef", activated_hidden, grad_v_low, preferred_element_type=jnp.float32
    )
    grad_acted = jnp.einsum(
        "tf,ef->te", grad_q_low, query_weight, preferred_element_type=jnp.float32
    )
    grad_acted = grad_acted + jnp.einsum(
        "tf,ef->te", grad_k_low, key_weight, preferred_element_type=jnp.float32
    )
    grad_acted = grad_acted + jnp.einsum(
        "tf,ef->te", grad_v_low, value_weight, preferred_element_type=jnp.float32
    )
    grad_gain_one = jnp.sum(grad_acted * normed_one, axis=0)
    scaled_one = grad_acted * gain_one
    grad_input = grad_res + inv_one * (
        scaled_one - normed_one * jnp.mean(scaled_one * normed_one, axis=-1, keepdims=True)
    )
    terms = [
        grad_wq.reshape(-1),
        grad_wk.reshape(-1),
        grad_wv.reshape(-1),
        grad_output.reshape(-1),
        grad_gate.reshape(-1),
        grad_up.reshape(-1),
        grad_down.reshape(-1),
        jnp.concatenate([grad_gain_one, grad_gain_two]),
    ]
    return (grad_input.astype(jnp.bfloat16), terms)


def local(
    inputs,
    segments,
    query_weight,
    key_weight,
    value_weight,
    output_weight,
    gate_weight,
    up_weight,
    down_weight,
    norm_gain_pair,
    cotangent,
):
    shard_rows = inputs.shape[2]
    seg_full = lax.all_gather(segments, "ctx", axis=2, tiled=True)
    positions = lax.axis_index("ctx") * shard_rows + jnp.arange(shard_rows, dtype=jnp.int32)
    cosine_table, sine_table = rope_parts(positions)
    weight_matrices = shape_weights(
        (
            lax.all_gather(query_weight, ("grp", "ctx"), axis=0, tiled=True),
            lax.all_gather(key_weight, ("grp", "ctx"), axis=0, tiled=True),
            lax.all_gather(value_weight, ("grp", "ctx"), axis=0, tiled=True),
            lax.all_gather(output_weight, ("grp", "ctx"), axis=0, tiled=True),
            lax.all_gather(gate_weight, ("grp", "ctx"), axis=0, tiled=True),
            lax.all_gather(up_weight, ("grp", "ctx"), axis=0, tiled=True),
            lax.all_gather(down_weight, ("grp", "ctx"), axis=0, tiled=True),
            lax.all_gather(norm_gain_pair, ("grp", "ctx"), axis=0, tiled=True),
        )
    )
    results = []
    saved = []
    for micro_step in range(MICRO):
        xrow = inputs[micro_step, 0].astype(jnp.float32)
        result, kept = forward_rows(
            xrow,
            seg_full[micro_step, 0],
            segments[micro_step, 0],
            positions,
            cosine_table,
            sine_table,
            weight_matrices,
        )
        results.append(result.astype(jnp.bfloat16))
        saved.append(kept)
    mats_back = shape_weights(
        (
            lax.all_gather(query_weight, ("grp", "ctx"), axis=0, tiled=True),
            lax.all_gather(key_weight, ("grp", "ctx"), axis=0, tiled=True),
            lax.all_gather(value_weight, ("grp", "ctx"), axis=0, tiled=True),
            lax.all_gather(output_weight, ("grp", "ctx"), axis=0, tiled=True),
            lax.all_gather(gate_weight, ("grp", "ctx"), axis=0, tiled=True),
            lax.all_gather(up_weight, ("grp", "ctx"), axis=0, tiled=True),
            lax.all_gather(down_weight, ("grp", "ctx"), axis=0, tiled=True),
            lax.all_gather(norm_gain_pair, ("grp", "ctx"), axis=0, tiled=True),
        )
    )
    input_grads = []
    shares = None
    totals = None
    for micro_step in range(MICRO):
        dout = cotangent[micro_step, 0].astype(jnp.float32)
        grad_input, terms = backward_rows(
            dout,
            seg_full[micro_step, 0],
            segments[micro_step, 0],
            positions,
            cosine_table,
            sine_table,
            mats_back,
            saved[micro_step],
        )
        input_grads.append(grad_input)
        totals = terms if totals is None else [a + b for a, b in zip(totals, terms)]
    shares = list(
        (
            lax.psum_scatter(totals[0], ("grp", "ctx"), scatter_dimension=0, tiled=True),
            lax.psum_scatter(totals[1], ("grp", "ctx"), scatter_dimension=0, tiled=True),
            lax.psum_scatter(totals[2], ("grp", "ctx"), scatter_dimension=0, tiled=True),
            lax.psum_scatter(totals[3], ("grp", "ctx"), scatter_dimension=0, tiled=True),
            lax.psum_scatter(totals[4], ("grp", "ctx"), scatter_dimension=0, tiled=True),
            lax.psum_scatter(totals[5], ("grp", "ctx"), scatter_dimension=0, tiled=True),
            lax.psum_scatter(totals[6], ("grp", "ctx"), scatter_dimension=0, tiled=True),
            lax.psum_scatter(totals[7], ("grp", "ctx"), scatter_dimension=0, tiled=True),
        )
    )
    outputs = jnp.stack(results)[:, None]
    input_grad = jnp.stack(input_grads)[:, None]
    return (
        outputs,
        input_grad,
        shares[0],
        shares[1],
        shares[2],
        shares[3],
        shares[4],
        shares[5],
        shares[6],
        shares[7],
    )


W = MODEL_WIDTH
HG = QUERY_HEADS // KEY_HEADS * HEAD_SIZE
QK = HG + HEAD_SIZE
SLAB = 384
QKV = HG + 2 * HEAD_SIZE
OUT = W // 8
BACK = 512
EDGE = 304
CHUNK = W // 32
HID = HIDDEN_UNITS // 8
SUB = HIDDEN_UNITS // 32
ROWS = 128
ALL = 8 * ROWS
POS = 64
LEN = 512
RELATIVE = (0, 2, 4, 6, 1, 3, 5, 7)
F32 = jnp.float32
BF16 = jnp.bfloat16
SCALE = HEAD_SIZE ** (-0.5)
NT = (((1,), (1,)), ((), ()))
TN = (((0,), (0,)), ((), ()))
MIB = 1024 * 1024


def pc(value, k):
    return lax.ppermute(value, "ctx", [(s, s ^ k) for s in range(8)])


def pz(value, k):
    return lax.ppermute(value, "grp", [(s, s ^ k) for s in range(4)])


def after(value, *others):
    return lax.optimization_barrier((value,) + others)[0]


def first_ctx(value):
    far = pc(value, 6)
    return [value, pc(value, 2), pc(value, 4), far]


def both_cores(mine):
    return mine + [pc(m, 1) for m in mine]


def gather_ctx(value):
    return both_cores(first_ctx(value))


def gather_grp(value):
    one = pz(value, 1)
    two = pz(value, 2)
    return (value, one, two, pz(two, 1))


def add_low(a, b):
    return (a.astype(F32) + b.astype(F32)).astype(BF16)


class Order:
    def __init__(self):
        self.last = None

    def __call__(self, values):
        return values if self.last is None else after(values, self.last)

    def then(self, result):
        self.last = jax.tree.leaves(result)[-1]
        return result

    def wait(self, values):
        return self.then(self(values))


def scatter_ctx(even, got):
    return [add_low(even[k], got[k]) for k in range(4)]


def send_ctx(sums):
    far = pc(sums[3], 6)
    return sums[0], pc(sums[1], 2), pc(sums[2], 4), far


def pick(blocks, g):
    return [lax.dynamic_index_in_dim(blocks, g ^ k, 0, keepdims=False) for k in range(4)]


def call(body, outs, *args, grid=None, in_specs=None, out_specs=None, scratch=(), flops=0, name=None):
    nbytes = sum(a.size * a.dtype.itemsize for a in args)
    nbytes += sum(o.size * o.dtype.itemsize for o in outs)
    kwargs = {}
    if grid is not None:
        kwargs = dict(grid=grid, in_specs=in_specs, out_specs=out_specs)
    else:
        kwargs = dict(
            in_specs=[
                pl.BlockSpec(memory_space=pltpu.SMEM)
                if a.dtype == jnp.int32 and a.ndim == 1
                else pl.BlockSpec(memory_space=pltpu.VMEM)
                for a in args
            ],
            out_specs=[pl.BlockSpec(memory_space=pltpu.VMEM) for _ in outs],
        )
    return pl.pallas_call(
        body,
        out_shape=outs,
        scratch_shapes=scratch,
        compiler_params=pltpu.CompilerParams(vmem_limit_bytes=56 * MIB),
        cost_estimate=pl.CostEstimate(flops=0, bytes_accessed=1, transcendentals=0),
        name=name,
        **kwargs,
    )(*args)


def sds(shape, dtype):
    return jax.ShapeDtypeStruct(shape, dtype)


def rows_of(ref, count):
    wide = ref.shape[0] // count
    return jnp.concatenate([ref[pl.ds(n, count, stride=wide), :] for n in range(wide)], 1)


def store_rows(ref, rows):
    count = rows.shape[0]
    wide = ref.shape[0] // count
    for n in range(wide):
        ref[pl.ds(n, count, stride=wide), :] = rows[:, n * 128 : (n + 1) * 128]


def pack_qkv_body(q_r, k_r, v_r, gain, out, sq, sk, sv):
    sq[...] = q_r[...].astype(F32)
    sk[...] = k_r[...].astype(F32)
    sv[...] = v_r[...].astype(F32)
    q, k, v = rows_of(sq, CHUNK), rows_of(sk, CHUNK), rows_of(sv, CHUNK)
    tail = jnp.concatenate([gain[:, n * SLAB : (n + 1) * SLAB] for n in range(3)], 0).astype(F32)
    tail = jnp.concatenate([tail, jnp.zeros((1, SLAB), F32)], 0)
    for h in range(8):
        if h < KEY_HEADS:
            rows = jnp.concatenate(
                [
                    q[:, h * HG : (h + 1) * HG],
                    k[:, h * HEAD_SIZE : (h + 1) * HEAD_SIZE],
                    v[:, h * HEAD_SIZE : (h + 1) * HEAD_SIZE],
                    jnp.zeros((CHUNK, SLAB - HG - 2 * HEAD_SIZE), F32),
                ],
                1,
            )
        else:
            rows = jnp.zeros((CHUNK, SLAB), F32)
        out[h] = jnp.concatenate([rows, tail], 0).astype(BF16)


def pack_hidden_body(gate_r, up_r, out, sg, su):
    sg[...] = gate_r[...].astype(F32)
    su[...] = up_r[...].astype(F32)
    gate, up = rows_of(sg, CHUNK), rows_of(su, CHUNK)
    for h in range(8):
        parts = [
            full[:, z * 768 + h * SUB : z * 768 + (h + 1) * SUB] for full in (gate, up) for z in range(4)
        ]
        out[h] = jnp.concatenate(parts, 1).astype(BF16)


def join_body(*refs):
    for n, block in enumerate(refs[:8]):
        refs[8][n * ROWS : (n + 1) * ROWS, :] = block[...]


def join(blocks):
    return call(join_body, [sds((ALL, W), BF16)], *blocks, name="join")[0]


def compact_body(src, out):
    out[...] = jnp.concatenate([src[h].astype(F32) for h in range(8)], 0).astype(BF16)


def output_weight_body(sc, b0, b1, b2, b3, b4, b5, b6, b7, out, rows):
    i, g = sc[0], sc[1]
    for j, b in zip(RELATIVE, (b0, b1, b2, b3, b4, b5, b6, b7)):
        for k in range(4):
            rows[i ^ j, g ^ k] = b[k].astype(F32)
    for z in range(4):
        for q in range(2):
            parts = [rows_of(rows.at[c, z], CHUNK) for c in range(4 * q, 4 * q + 4)]
            start = z * 288 + q * 144
            out[start : start + 144, :] = jnp.concatenate(parts, 0).astype(BF16)


def rotate(x, cosine, sine, sign):
    lane = lax.broadcasted_iota(jnp.int32, (1, 128), 1) % HEAD_SIZE
    first = lane < HEAD_SIZE // 2
    halves = []
    for n in range(x.shape[1] // 128):
        part = x[:, n * 128 : (n + 1) * 128]
        swapped = jnp.where(first, pltpu.roll(part, 96, 1), pltpu.roll(part, 32, 1))
        halves.append(part * cosine + sign * (swapped * sine))
    return jnp.concatenate(halves, 1)


def attend_body(
    sc, x0, x1, x2, x3, x4, x5, x6, x7, w0, w1, w2, w3, cosine, sine, pcol, prow,
    att, qk_o, v_o, acted, probs, w_o, gains, x_o,
):
    xs = (x0, x1, x2, x3, x4, x5, x6, x7)
    g = sc[1]
    sums = [jnp.zeros((3, SLAB), F32), jnp.zeros((3, SLAB), F32)]
    for k, w in enumerate((w0, w1, w2, w3)):
        z = g ^ k
        block = jnp.concatenate([w[h, :CHUNK, :].astype(F32) for h in range(8)], 0)
        w_o[pl.ds(pl.multiple_of(z * 288, 32), 288), :] = block.astype(BF16)
        rows = sum(w[h, CHUNK : CHUNK + 3, :].astype(F32) for h in range(8))
        sums[0] = sums[0] + jnp.where(z < 2, rows, 0.0)
        sums[1] = sums[1] + jnp.where(z < 2, 0.0, rows)
    gain = [jnp.concatenate([s[0:1], s[1:2], s[2:3]], 1) for s in sums]
    gains[...] = jnp.concatenate([gain[0], gain[1], jnp.zeros((6, W), F32)], 0)
    for m in range(MICRO):
        segs = []
        for b in range(8):
            src = xs[b][m * POS : (m + 1) * POS, :]
            x_o[b * ROWS + m * POS : b * ROWS + (m + 1) * POS, :] = src[:, :W]
            x = src[:, :W].astype(F32)
            inv = lax.rsqrt(jnp.mean(x * x, axis=-1, keepdims=True) + EPS)
            acted[b * ROWS + m * POS : b * ROWS + (m + 1) * POS, :] = (x * inv * gain[0]).astype(BF16)
            segs.append(src[:, W:].astype(F32))
        rows = jnp.concatenate(
            [acted[b * ROWS + m * POS : b * ROWS + (m + 1) * POS, :] for b in range(8)], 0
        )
        seg = jnp.concatenate(segs, 0)
        y = jnp.dot(rows, w_o[...], preferred_element_type=F32)
        qk = rotate(y[:, :QK], cosine[...], sine[...], 1.0).astype(BF16)
        v = y[:, QK:].astype(BF16)
        qk_o[m] = qk
        v_o[m] = v
        seg_row = jnp.transpose(seg)[0:1, :]
        mask = (prow[0:1, :] <= pcol[:, 0:1]) & (seg_row == seg[:, 0:1])
        bias = jnp.where(mask, 0.0, NEGATIVE_LARGE)
        keys = qk[:, HG:]
        for h in range(3):
            s = lax.dot_general(
                qk[:, h * HEAD_SIZE : (h + 1) * HEAD_SIZE], keys, NT, preferred_element_type=F32
            )
            s = s * SCALE + bias
            e = jnp.exp(s - jnp.max(s, axis=-1, keepdims=True))
            p = (e * (1.0 / jnp.sum(e, axis=-1, keepdims=True))).astype(BF16)
            probs[m, h] = p
            lane = m * HG + h * HEAD_SIZE
            att[:, lane : lane + HEAD_SIZE] = jnp.dot(
                p, v[:, :HEAD_SIZE], preferred_element_type=F32
            ).astype(BF16)


def project_body(sc, x, a0, a1, a2, a3, a4, a5, a6, a7, wo, gains, att_o, mixed_o, res_o, heads):
    i = sc[0]
    t = pl.program_id(0)
    for j, a in zip(RELATIVE, (a0, a1, a2, a3, a4, a5, a6, a7)):
        h = i ^ j
        for half in range(2):
            b = 2 * t + half
            q = (2 * (b & 3) + (b >> 2)) ^ j
            start = pl.multiple_of(((q & 1) * 4 + (q >> 1)) * POS, POS)
            rows = a[pl.ds(start, POS), :]
            for m in range(MICRO):
                heads[h, half * ROWS + m * POS : half * ROWS + (m + 1) * POS, :] = rows[:, m * HG : (m + 1) * HG]
    for h in range(KEY_HEADS):
        att_o[:, h * HG : (h + 1) * HG] = heads[h]
    residual = x[...].astype(F32) + jnp.dot(att_o[...], wo[...], preferred_element_type=F32)

    @pl.when(t == 0)
    def _():
        res_o[...] = residual[:ROWS]

    inv = lax.rsqrt(jnp.mean(residual * residual, axis=-1, keepdims=True) + EPS)
    mixed_o[...] = (residual * inv * gains[1:2, :]).astype(BF16)


def feed_body(
    sc, mixed_r, c, g0, g1, g2, g3, d0, d1, d2, d3, hidden_o, dgu_o, pm, pe, dn, sums, gu
):
    g = sc[1]
    t = pl.program_id(0)

    @pl.when(t == 0)
    def _():
        for k, (a, d) in enumerate(((g0, d0), (g1, d1), (g2, d2), (g3, d3))):
            z = g ^ k
            gu[pl.ds(pl.multiple_of(z * 288, 32), 288), :] = a[...]
            dn[pl.ds(pl.multiple_of(z * SUB, 32), SUB), :] = d[...]
        sums[...] = jnp.zeros((8, W), F32)

    mixed = mixed_r[...]
    y = jnp.dot(mixed, gu[...], preferred_element_type=F32)
    gate = y[:, :HID]
    up = y[:, HID:]
    sig = 1.0 / (1.0 + jnp.exp(-gate))
    silu = gate * sig
    hidden_o[...] = (silu * up).astype(BF16)
    dh = lax.dot_general(c[...], dn[...], NT, preferred_element_type=F32)
    dgate = (dh * up * (sig + silu * (1.0 - sig))).astype(BF16)
    dup = (dh * silu).astype(BF16)
    dgu = jnp.concatenate([dgate, dup], 1)
    dgu_o[...] = dgu
    dm = lax.dot_general(dgu, gu[...], NT, preferred_element_type=F32)
    sums[0:1, :] = sums[0:1, :] + jnp.sum(dm * mixed.astype(F32), axis=0, keepdims=True)
    dm = dm.astype(BF16).reshape(2, ROWS, W)

    @pl.when(t < 2)
    def _():
        pm[...] = dm

    @pl.when(t >= 2)
    def _():
        pe[...] = dm


def mid_body(a, b, d, f, c, res, gains, dres, low):
    dm = a[...].astype(F32) + b[...].astype(F32) + d[...].astype(F32) + f[...].astype(F32)
    r = res[...]
    inv = lax.rsqrt(jnp.mean(r * r, axis=-1, keepdims=True) + EPS)
    n = r * inv
    e = dm * gains[1:2, :]
    out = c[...].astype(F32) + inv * (e - n * jnp.mean(e * n, axis=-1, keepdims=True))
    dres[...] = out
    low[...] = out.astype(BF16)


def last_body(a, b, d, f, x, dres, gains, out):
    da = a[...].astype(F32) + b[...].astype(F32) + d[...].astype(F32) + f[...].astype(F32)
    r = x[...].astype(F32)
    inv = lax.rsqrt(jnp.mean(r * r, axis=-1, keepdims=True) + EPS)
    n = r * inv
    e = da * gains[0:1, :]
    out[...] = (dres[...] + inv * (e - n * jnp.mean(e * n, axis=-1, keepdims=True))).astype(BF16)


def back_body(
    sc, l0, l1, l2, l3, l4, l5, l6, l7, wo, qk_r, v_r, probs, cosine, sine, acted_t, att_t, w_slab, gains, sums,
    out, b0, b1, b2, b3, columns, dots, edge,
):
    lows = (l0, l1, l2, l3, l4, l5, l6, l7)
    i, g = sc[0], sc[1]
    place = lax.broadcasted_iota(jnp.int32, (256, W), 1) - lax.broadcasted_iota(jnp.int32, (256, W), 0)
    chosen = jnp.where(place == i * OUT, 1.0, 0.0).astype(BF16)
    for m in range(MICRO):
        rows = jnp.concatenate([lows[b][m * POS : (m + 1) * POS, :] for b in range(8)], 0)
        datt = lax.dot_general(rows, wo[...], NT, preferred_element_type=F32).astype(BF16)
        part = lax.dot_general(rows, chosen, NT, preferred_element_type=F32).astype(BF16)
        qk = qk_r[m]
        keys = qk[:, HG:]
        v = v_r[m][:, :HEAD_SIZE]
        dq = []
        dk = jnp.zeros((HEAD_SIZE, LEN), F32)
        dv = jnp.zeros((HEAD_SIZE, LEN), F32)
        for h in range(3):
            da = datt[:, h * HEAD_SIZE : (h + 1) * HEAD_SIZE]
            q = qk[:, h * HEAD_SIZE : (h + 1) * HEAD_SIZE]
            low = probs[m, h]
            p = low.astype(F32)
            dp = lax.dot_general(da, v, NT, preferred_element_type=F32)
            delta = jnp.sum(p * dp, axis=-1, keepdims=True)
            ds = (p * (dp - delta)).astype(BF16)
            dq.append(jnp.dot(ds, keys, preferred_element_type=F32))
            dk = dk + lax.dot_general(q, ds, TN, preferred_element_type=F32)
            dv = dv + lax.dot_general(da, low, TN, preferred_element_type=F32)
        dqk = jnp.concatenate(dq + [jnp.transpose(dk)], 1) * SCALE
        dqk = rotate(dqk, cosine[...], sine[...], -1.0)
        dvt = jnp.transpose(jnp.concatenate([dv, jnp.zeros((HEAD_SIZE, LEN), F32)], 0))
        full = jnp.concatenate([dqk, dvt], 1).astype(BF16)
        for b in range(8):
            out[b * ROWS + m * POS : b * ROWS + (m + 1) * POS, :] = full[b * POS : (b + 1) * POS, :]
            columns[b * ROWS + m * POS : b * ROWS + (m + 1) * POS, :] = part[b * POS : (b + 1) * POS, :]
    blocks = (b0, b1, b2, b3)
    for k in range(4):
        z = g ^ k
        start = pl.multiple_of(z * 288, 32)
        y = jnp.dot(acted_t[pl.ds(start, 288), :], out[...], preferred_element_type=F32)
        yo = jnp.dot(att_t[pl.ds(start, 288), :], columns[...], preferred_element_type=F32)
        y2 = jnp.concatenate([y[:, :QKV], yo[:, : BACK - QKV]], 1)
        blocks[k][:288, :] = y2.astype(BF16)
        dot = jnp.sum(y * w_slab[pl.ds(start, 288), :].astype(F32), axis=-1, keepdims=True)
        dots[z] = jnp.transpose(jnp.broadcast_to(dot, (288, 128)))[:8, :]
    one = jnp.concatenate([dots[z][0:1, :] for z in range(4)], 1) / gains[0:1, :]
    two = sums[0:1, :] / gains[1:2, :]
    for z in range(4):
        full = one if z < 2 else two
        at = (z % 2) * 576
        rows = jnp.concatenate([full[:, at + 72 * c : at + 72 * (c + 1)] for c in range(8)], 0)
        rows = jnp.concatenate([rows, jnp.zeros((8, BACK - 72), F32)], 1)
        edge[z] = jnp.concatenate([rows, jnp.zeros((EDGE - 288 - 8, BACK), F32)], 0)
    for k in range(4):
        blocks[k][288:, :] = edge[g ^ k].astype(BF16)


def split_back_body(a, b, d, out):
    rows = a[...].astype(F32) + b[...].astype(F32) + d[...].astype(F32)
    for h in range(8):
        block = [rows[h * CHUNK : (h + 1) * CHUNK, :], rows[288 + h : 289 + h, :], jnp.zeros((3, BACK), F32)]
        out[h] = jnp.concatenate(block, 0).astype(BF16)


def split_body(a, b, d, out):
    rows = a[...].astype(F32) + b[...].astype(F32) + d[...].astype(F32)
    for h in range(8):
        out[h] = rows[h * CHUNK : (h + 1) * CHUNK, :].astype(BF16)


def down_body(a, b, d, out):
    store_rows(out, a[...].astype(F32) + b[...].astype(F32) + d[...].astype(F32))


def unpack_back_body(src, q, k, v, o, gains):
    parts = [src[h].astype(F32) for h in range(8)]
    rows = [p[:CHUNK, :] for p in parts]
    store_rows(q, jnp.concatenate([p[:, :HG] for p in rows[:KEY_HEADS]], 1))
    store_rows(k, jnp.concatenate([p[:, HG:QK] for p in rows[:KEY_HEADS]], 1))
    store_rows(v, jnp.concatenate([p[:, QK:QKV] for p in rows[:KEY_HEADS]], 1))
    store_rows(o, jnp.concatenate([p[:, QKV : QKV + OUT] for p in rows], 1))
    gains[...] = jnp.broadcast_to(sum(p[CHUNK : CHUNK + 1, :128] for p in parts), (8, 128))


def unpack_hidden_body(src, gate, up):
    for n, out in enumerate((gate, up)):
        parts = [
            src[h, :, n * HID + z * SUB : n * HID + (z + 1) * SUB].astype(F32)
            for z in range(4)
            for h in range(8)
        ]
        store_rows(out, jnp.concatenate(parts, 1))


def fast_local(inputs, segments, wq, wk, wv, wo, wg, wu, wd, gain_pair, cotangent):
    i = lax.axis_index("ctx").astype(jnp.int32)
    g = lax.axis_index("grp").astype(jnp.int32)
    r = g * 8 + i
    sc = jnp.stack([i, g])
    x_own = inputs.reshape(ROWS, W)
    c_own = cotangent.reshape(ROWS, W)
    order = Order()

    q2, k2, v2 = wq.reshape(-1, 128), wk.reshape(-1, 128), wv.reshape(-1, 128)
    placed = lax.dynamic_update_slice(jnp.zeros((1, W), BF16), gain_pair[None, :], (0, (r % 16) * 72))
    packed = order.then(
        call(
            pack_qkv_body,
            [sds((8, 40, SLAB), BF16)],
            q2, k2, v2, placed,
            scratch=[pltpu.VMEM(a.shape, F32) for a in (q2, k2, v2)], name="pack_qkv",
        )
    )[0]
    packed = lax.all_to_all(packed, "ctx", 0, 0, tiled=True)

    x_late, seg_late = order((x_own, segments))
    seg = jnp.broadcast_to(seg_late.reshape(ROWS, 1).astype(BF16), (ROWS, 128))
    xs = first_ctx(order.then(jnp.concatenate([x_late, seg], 1)))

    wg, wu, wo, wd, i_late = order((wg, wu, wo, wd, i))
    o_own = wo.reshape(-1, 128)
    o_one, o_two = pz(o_own, 1), pz(o_own, 2)
    gate2, up2 = wg.reshape(-1, 128), wu.reshape(-1, 128)
    hid = order.then(
        call(
            pack_hidden_body,
            [sds((8, CHUNK, 2 * HID), BF16)],
            gate2, up2,
            scratch=[pltpu.VMEM(a.shape, F32) for a in (gate2, up2)], name="pack_hidden",
        )
    )[0]
    packed = order.wait(packed)
    s_one, s_two = pz(packed, 1), pz(packed, 2)
    hid = lax.all_to_all(after(hid, packed), "ctx", 0, 0, tiled=True)
    o_two = order.wait(o_two)
    o_three = pz(o_two, 1)
    xs = both_cores(order.wait(xs))
    s_one = order.wait(s_one)
    d_own = order(wd).reshape(SUB, W)
    d_one, d_two = pz(d_own, 1), pz(d_own, 2)
    o_sent = order.then(jnp.stack(order([o_own, o_one, o_two, o_three])))
    os = first_ctx(o_sent)
    s_two = order.wait(s_two)
    s_three = pz(s_two, 1)
    hid = order.then(call(compact_body, [sds((288, 2 * HID), BF16)], order(hid), name="compact"))[0]
    g_one, g_two = pz(after(hid, d_one), 1), pz(after(hid, d_one), 2)

    i_late = order(i_late)
    rel = jnp.array(RELATIVE, jnp.int32)
    positions = ((i_late ^ rel)[:, None] * POS + jnp.arange(POS, dtype=jnp.int32)[None, :]).reshape(LEN)
    half = HEAD_SIZE // 2
    freq = THETA ** (-jnp.arange(half, dtype=F32) * 2.0 / HEAD_SIZE)
    angle = positions.astype(F32)[:, None] * freq[None, :]
    cosine = jnp.tile(jnp.cos(angle), (1, 4))
    sine = jnp.sin(angle)
    sine = jnp.concatenate([-sine, sine, -sine, sine], 1)
    pcol = jnp.broadcast_to(positions.astype(F32)[:, None], (LEN, 128))
    prow = jnp.broadcast_to(positions.astype(F32)[None, :], (8, LEN))
    cosine, sine, pcol, prow = order.then((cosine, sine, pcol, prow))

    xs, slabs = order((xs, (packed, s_one, s_two, s_three)))
    att, qk, v, acted, probs, w_slab, gains, call_x = order.then(
        call(
            attend_body,
            [
                sds((LEN, 2 * HG), BF16),
                sds((MICRO, LEN, QK), BF16),
                sds((MICRO, LEN, 128), BF16),
                sds((ALL, W), BF16),
                sds((MICRO, 3, LEN, LEN), BF16),
                sds((W, SLAB), BF16),
                sds((8, W), F32),
                sds((ALL, W), BF16),
            ],
            sc, *xs, *slabs, cosine, sine, pcol, prow, name="attend",
        )
    )
    heads = first_ctx(att)
    d_two = order.wait(d_two)
    d_three = pz(d_two, 1)
    os = both_cores(order.wait(os))
    w_out = order.then(
        call(
            output_weight_body, [sds((W, W), BF16)], sc, *order(os),
            scratch=[pltpu.VMEM((8, 4, wo.size // 128, 128), F32)], name="output_weight",
        )
    )[0]
    g_one = order.wait(g_one)
    heads[1] = order.wait(heads[1])
    heads[2] = order.wait(heads[2])
    cs = first_ctx(order(c_own))
    g_two = order.wait(g_two)
    g_three = pz(g_two, 1)
    heads = both_cores(order.wait(heads))

    whole = lambda *shape: pl.BlockSpec(shape, lambda t: (0,) * len(shape))
    rowb = lambda n: pl.BlockSpec((256, n), lambda t: (t, 0))
    smem = pl.BlockSpec(memory_space=pltpu.SMEM)
    heads = order(heads)
    att_full, mixed, res_own = order.then(
        call(
            project_body,
            [sds((ALL, W), BF16), sds((ALL, W), BF16), sds((ROWS, W), F32)],
            sc, call_x, *heads, w_out, gains,
            grid=(4,),
            in_specs=[smem, rowb(W)] + [whole(LEN, 2 * HG)] * 8 + [whole(W, W), whole(8, W)],
            out_specs=[rowb(W), rowb(W), whole(ROWS, W)],
            scratch=[pltpu.VMEM((8, 256, HG), BF16)], name="project",
        )
    )
    cs = both_cores(order.wait(cs))
    att_t = order.then(jnp.transpose(order(att_full)))
    acted_t = order.then(jnp.transpose(order(acted)))
    wo_own = order.then(lax.dynamic_slice(order(w_out), (jnp.minimum(i, KEY_HEADS - 1) * HG, 0), (HG, W)))
    call_c = order.then(join(order(cs)))
    gu, dn = order(((hid, g_one, g_two, g_three), (d_own, d_one, d_two, d_three)))
    hidden, dgu, pm, pe, down, dots_two = order.then(
        call(
            feed_body,
            [
                sds((ALL, HID), BF16),
                sds((ALL, 2 * HID), BF16),
                sds((4, ROWS, W), BF16),
                sds((4, ROWS, W), BF16),
                sds((HID, W), BF16),
                sds((8, W), F32),
            ],
            sc, mixed, call_c, *gu, *dn,
            grid=(4,),
            in_specs=[smem, rowb(W), rowb(W)] + [whole(288, 2 * HID)] * 4 + [whole(SUB, W)] * 4,
            out_specs=[
                rowb(HID),
                rowb(2 * HID),
                pl.BlockSpec((2, ROWS, W), lambda t: (jnp.minimum(t, 1), 0, 0)),
                pl.BlockSpec((2, ROWS, W), lambda t: (jnp.maximum(t - 2, 0), 0, 0)),
                whole(HID, W),
                whole(8, W),
            ],
            scratch=[pltpu.VMEM((W, 2 * HID), BF16)], name="feed",
        )
    )

    got = pc(pe, 1)
    grad_gu = order.then(lax.dot_general(order(mixed), dgu, TN, preferred_element_type=F32).astype(BF16))
    terms = send_ctx(order.then(scatter_ctx(pm, order(got))))
    gu_blocks = order.then(pick(order(grad_gu).reshape(4, 288, 2 * HID), g))
    gu_far = pz(gu_blocks[3], 1)
    grad_dn = order.then(lax.dot_general(order(hidden), call_c, TN, preferred_element_type=F32).astype(BF16))
    gu_mid = order.then(add_low(gu_blocks[2], order(gu_far)))
    gu_terms = (gu_blocks[0], pz(after(gu_blocks[1], gu_mid), 1), pz(gu_mid, 2))
    dn_blocks = order.then(pick(order(grad_dn).reshape(4, SUB, W), g))
    dn_far = pz(dn_blocks[3], 1)
    dres, low = order.then(
        call(
            mid_body, [sds((ROWS, W), F32), sds((ROWS, W), BF16)], *order(terms), c_own, res_own, gains, name="mid"
        )
    )
    lows = gather_ctx(low)

    hid_out = order(hidden)
    om_p = jnp.dot(hid_out[: 4 * ROWS], down, preferred_element_type=F32).astype(BF16)
    oe_p = order.then(jnp.dot(hid_out[4 * ROWS :], down, preferred_element_type=F32).astype(BF16))
    out_got = pc(oe_p.reshape(4, ROWS, W), 1)
    dn_mid = order.then(add_low(dn_blocks[2], order(dn_far)))
    dn_terms = (dn_blocks[0], pz(after(dn_blocks[1], dn_mid), 1), pz(dn_mid, 2))
    out_terms = send_ctx(order.then(scatter_ctx(om_p.reshape(4, ROWS, W), after(order(out_got), lows[1]))))

    dqkv, *slab_blocks = order.then(
        call(
            back_body,
            [sds((ALL, SLAB), BF16)] + [sds((EDGE, BACK), BF16)] * 4,
            sc, *order(lows), wo_own, qk, v, probs, cosine, sine, acted_t, att_t, w_slab, gains, dots_two,
            scratch=[
                pltpu.VMEM((ALL, 256), BF16),
                pltpu.VMEM((4, 8, 288), F32),
                pltpu.VMEM((4, EDGE - 288, BACK), F32),
            ],
            name="back",
        )
    )
    slab_far = pz(slab_blocks[3], 1)
    hid_sum = order.then(
        call(split_body, [sds((8, CHUNK, 2 * HID), BF16)], *order(gu_terms), name="split_hidden")
    )[0]
    hid_sum = lax.all_to_all(hid_sum, "ctx", 0, 0, tiled=True)
    dqkv = order(dqkv)
    dae = order.then(lax.dot_general(dqkv[4 * ROWS :], w_slab, NT, preferred_element_type=F32).astype(BF16))
    in_got = pc(dae.reshape(4, ROWS, W), 1)
    dam = order.then(lax.dot_general(dqkv[: 4 * ROWS], order(w_slab), NT, preferred_element_type=F32).astype(BF16))
    slab_mid = order.then(add_low(slab_blocks[2], order(slab_far)))
    slab_terms = (slab_blocks[0], pz(after(slab_blocks[1], slab_mid), 1), pz(slab_mid, 2))
    in_terms = send_ctx(order.then(scatter_ctx(dam.reshape(4, ROWS, W), order(in_got))))

    grad_down = order.then(call(down_body, [sds((864, 128), F32)], *order(dn_terms), name="down"))[0]
    outputs = order.then((res_own + sum(t.astype(F32) for t in order(out_terms))).astype(BF16))
    grad_gate, grad_up = order.then(
        call(unpack_hidden_body, [sds((864, 128), F32), sds((864, 128), F32)], order(hid_sum), name="unpack_hidden")
    )
    slab = order.then(call(split_back_body, [sds((8, 40, BACK), BF16)], *order(slab_terms), name="split_back"))[0]
    slab = lax.all_to_all(slab, "ctx", 0, 0, tiled=True)
    input_grad = order.then(
        call(last_body, [sds((ROWS, W), BF16)], *order(in_terms), x_own, dres, gains, name="last")
    )[0]
    grad_q, grad_k, grad_v, grad_out, grad_gains = call(
        unpack_back_body,
        [sds((324, 128), F32), sds((108, 128), F32), sds((108, 128), F32), sds((324, 128), F32), sds((8, 128), F32)],
        order(slab), name="unpack_back",
    )
    grad_gains = grad_gains[0, :72]

    shape = (MICRO, 1, POS, W)
    return (
        outputs.reshape(shape),
        input_grad.reshape(shape),
        grad_q.reshape(-1),
        grad_k.reshape(-1),
        grad_v.reshape(-1),
        grad_out.reshape(-1),
        grad_gate.reshape(-1),
        grad_up.reshape(-1),
        grad_down.reshape(-1),
        grad_gains,
    )


def solution(mesh):
    in_specs = (
        P(None, "grp", "ctx", None),
        P(None, "grp", "ctx"),
        P(("grp", "ctx")),
        P(("grp", "ctx")),
        P(("grp", "ctx")),
        P(("grp", "ctx")),
        P(("grp", "ctx")),
        P(("grp", "ctx")),
        P(("grp", "ctx")),
        P(("grp", "ctx")),
        P(None, "grp", "ctx", None),
    )
    out_specs = (
        P(None, "grp", "ctx", None),
        P(None, "grp", "ctx", None),
        P(("grp", "ctx")),
        P(("grp", "ctx")),
        P(("grp", "ctx")),
        P(("grp", "ctx")),
        P(("grp", "ctx")),
        P(("grp", "ctx")),
        P(("grp", "ctx")),
        P(("grp", "ctx")),
    )
    fits = (mesh.shape["ctx"], mesh.shape["grp"]) == (8, 4)
    return jax.shard_map(
        fast_local if fits else local,
        mesh=mesh,
        in_specs=in_specs,
        out_specs=out_specs,
        check_vma=False,
    )
```

```python
import jax
import jax.numpy as jnp
from jax import lax
from jax.experimental import pallas as pl
from jax.experimental.pallas import tpu as pltpu
from jax.sharding import PartitionSpec as P

MODEL_WIDTH = 1152
QUERY_HEADS = 18
KEY_HEADS = 6
HEAD_SIZE = 64
HIDDEN_UNITS = 3072
MICRO = 2


EPS = 1e-05
THETA = 10000.0
NEGATIVE_LARGE = -1e30


def rope_parts(positions):
    half = HEAD_SIZE // 2
    freq = THETA ** (-jnp.arange(half, dtype=jnp.float32) * 2.0 / HEAD_SIZE)
    angle = positions.astype(jnp.float32)[:, None] * freq[None, :]
    return (jnp.cos(angle)[:, None, :], jnp.sin(angle)[:, None, :])


def rotary_apply(value_rows, cosine_table, sine_table, sign):
    half = value_rows.shape[-1] // 2
    first = value_rows[..., :half]
    second = value_rows[..., half:]
    return jnp.concatenate(
        [
            first * cosine_table - sign * second * sine_table,
            second * cosine_table + sign * first * sine_table,
        ],
        -1,
    )


def shape_weights(full_precision):
    return (
        full_precision[0].reshape(MODEL_WIDTH, QUERY_HEADS * HEAD_SIZE),
        full_precision[1].reshape(MODEL_WIDTH, KEY_HEADS * HEAD_SIZE),
        full_precision[2].reshape(MODEL_WIDTH, KEY_HEADS * HEAD_SIZE),
        full_precision[3].reshape(QUERY_HEADS * HEAD_SIZE, MODEL_WIDTH),
        full_precision[4].reshape(MODEL_WIDTH, HIDDEN_UNITS),
        full_precision[5].reshape(MODEL_WIDTH, HIDDEN_UNITS),
        full_precision[6].reshape(HIDDEN_UNITS, MODEL_WIDTH),
        full_precision[7],
    )


def allowed(key_pos, key_seg, query_pos, query_seg):
    return (key_pos[None, :] <= query_pos[:, None]) & (key_seg[None, :] == query_seg[:, None])


def online_step(
    state, grouped_queries, key_block, value_block, pblock, sblock, query_pos, query_seg
):
    best, total, accum = state
    block_span = key_block.shape[0]
    key_head_rows = key_block.reshape(block_span, KEY_HEADS, HEAD_SIZE)
    value_head_rows = value_block.reshape(block_span, KEY_HEADS, HEAD_SIZE)
    scores = jnp.einsum(
        "tkgd,nkd->kgtn", grouped_queries, key_head_rows, preferred_element_type=jnp.float32
    ) * HEAD_SIZE ** (-0.5)
    mask = allowed(pblock, sblock, query_pos, query_seg)[None, None]
    scores = jnp.where(mask, scores, NEGATIVE_LARGE)
    new_best = jnp.maximum(best, jnp.max(scores, axis=-1))
    factor = jnp.exp(best - new_best)
    expo = jnp.where(mask, jnp.exp(scores - new_best[..., None]), 0.0)
    total = total * factor + jnp.sum(expo, axis=-1)
    accum = accum * factor[..., None] + jnp.einsum(
        "kgtn,nkd->kgtd",
        expo.astype(jnp.bfloat16),
        value_head_rows,
        preferred_element_type=jnp.float32,
    )
    return (new_best, total, accum)


def guarded_step(
    state, grouped_queries, key_block, value_block, pblock, sblock, query_pos, query_seg
):

    def guarded_work(current):
        return online_step(
            current, grouped_queries, key_block, value_block, pblock, sblock, query_pos, query_seg
        )

    def guarded_leave(current):
        return current

    return lax.cond(pblock[0] <= query_pos[-1], guarded_work, guarded_leave, state)


def online_blocks(
    carry, grouped_queries, key_rows, value_rows, key_pos, key_seg, query_pos, query_seg
):
    count = key_rows.shape[0]
    block_size = 512 if count > 512 and count % 512 == 0 else count
    if block_size == count:
        return guarded_step(
            carry, grouped_queries, key_rows, value_rows, key_pos, key_seg, query_pos, query_seg
        )

    def step(state, block_tile):
        return (
            guarded_step(
                state,
                grouped_queries,
                block_tile[0],
                block_tile[1],
                block_tile[2],
                block_tile[3],
                query_pos,
                query_seg,
            ),
            None,
        )

    block_tiles = (
        key_rows.reshape(-1, block_size, key_rows.shape[1]),
        value_rows.reshape(-1, block_size, value_rows.shape[1]),
        key_pos.reshape(-1, block_size),
        key_seg.reshape(-1, block_size),
    )
    carry, _ = lax.scan(step, carry, block_tiles)
    return carry


def forward_rows(xrow, seg_row, query_seg, positions, cosine_table, sine_table, weight_matrices):
    (
        query_weight,
        key_weight,
        value_weight,
        output_weight,
        gate_weight,
        up_weight,
        down_weight,
        gains,
    ) = weight_matrices
    token_rows = xrow.shape[0]
    query_groups = QUERY_HEADS // KEY_HEADS
    gain_one = gains[:MODEL_WIDTH].astype(jnp.float32)
    gain_two = gains[MODEL_WIDTH:].astype(jnp.float32)
    inv_one = lax.rsqrt(jnp.mean(xrow * xrow, axis=-1, keepdims=True) + EPS)
    normed_one = xrow * inv_one
    activated_hidden = (normed_one * gain_one).astype(jnp.bfloat16)
    query_unrotated = jnp.dot(
        activated_hidden, query_weight, preferred_element_type=jnp.float32
    ).reshape(token_rows, QUERY_HEADS, HEAD_SIZE)
    key_unrotated = jnp.dot(
        activated_hidden, key_weight, preferred_element_type=jnp.float32
    ).reshape(token_rows, KEY_HEADS, HEAD_SIZE)
    value_raw = jnp.dot(activated_hidden, value_weight, preferred_element_type=jnp.float32)
    grouped_queries = (
        rotary_apply(query_unrotated, cosine_table, sine_table, 1.0)
        .astype(jnp.bfloat16)
        .reshape(token_rows, KEY_HEADS, query_groups, HEAD_SIZE)
    )
    key_rows = (
        rotary_apply(key_unrotated, cosine_table, sine_table, 1.0)
        .astype(jnp.bfloat16)
        .reshape(token_rows, KEY_HEADS * HEAD_SIZE)
    )
    value_rows = value_raw.astype(jnp.bfloat16)
    start_state = (
        jnp.full((KEY_HEADS, query_groups, token_rows), NEGATIVE_LARGE, jnp.float32),
        jnp.zeros((KEY_HEADS, query_groups, token_rows), jnp.float32),
        jnp.zeros((KEY_HEADS, query_groups, token_rows, HEAD_SIZE), jnp.float32),
    )
    piece = (
        lax.all_gather(key_rows, "ctx", axis=0, tiled=True),
        lax.all_gather(value_rows, "ctx", axis=0, tiled=True),
    )
    count = piece[0].shape[0]
    key_pos = jnp.arange(count, dtype=jnp.int32)
    best, total, accum = online_blocks(
        start_state, grouped_queries, piece[0], piece[1], key_pos, seg_row, positions, query_seg
    )
    attn = accum / total[..., None]
    lse = best + jnp.log(total)
    attn_low = (
        jnp.transpose(attn, (2, 0, 1, 3))
        .reshape(token_rows, QUERY_HEADS * HEAD_SIZE)
        .astype(jnp.bfloat16)
    )
    residual = xrow + jnp.dot(attn_low, output_weight, preferred_element_type=jnp.float32)
    inv_two = lax.rsqrt(jnp.mean(residual * residual, axis=-1, keepdims=True) + EPS)
    normed_two = residual * inv_two
    mixed = (normed_two * gain_two).astype(jnp.bfloat16)
    gate = jnp.dot(mixed, gate_weight, preferred_element_type=jnp.float32)
    upper = jnp.dot(mixed, up_weight, preferred_element_type=jnp.float32)
    hidden = (jax.nn.silu(gate) * upper).astype(jnp.bfloat16)
    result = residual + jnp.dot(hidden, down_weight, preferred_element_type=jnp.float32)
    kept = (
        inv_one,
        normed_one,
        activated_hidden,
        grouped_queries,
        key_rows,
        value_rows,
        attn,
        lse,
        attn_low,
        inv_two,
        normed_two,
        mixed,
        gate,
        upper,
        hidden,
    )
    return (result, kept)


def backward_rows(
    dout, seg_row, query_seg, positions, cosine_table, sine_table, weight_matrices, kept
):
    (
        query_weight,
        key_weight,
        value_weight,
        output_weight,
        gate_weight,
        up_weight,
        down_weight,
        gains,
    ) = weight_matrices
    (
        inv_one,
        normed_one,
        activated_hidden,
        grouped_queries,
        key_rows,
        value_rows,
        attn,
        lse,
        attn_low,
        inv_two,
        normed_two,
        mixed,
        gate,
        upper,
        hidden,
    ) = kept
    token_rows = dout.shape[0]
    query_groups = QUERY_HEADS // KEY_HEADS
    scale = HEAD_SIZE ** (-0.5)
    gain_one = gains[:MODEL_WIDTH].astype(jnp.float32)
    gain_two = gains[MODEL_WIDTH:].astype(jnp.float32)
    dout_low = dout.astype(jnp.bfloat16)
    grad_down = jnp.einsum("tf,td->fd", hidden, dout_low, preferred_element_type=jnp.float32)
    grad_hidden = jnp.einsum("td,fd->tf", dout_low, down_weight, preferred_element_type=jnp.float32)
    sigma = jax.nn.sigmoid(gate)
    grad_gate_act = (grad_hidden * upper * (sigma + gate * sigma * (1.0 - sigma))).astype(
        jnp.bfloat16
    )
    grad_up_act = (grad_hidden * (gate * sigma)).astype(jnp.bfloat16)
    grad_gate = jnp.einsum("te,tf->ef", mixed, grad_gate_act, preferred_element_type=jnp.float32)
    grad_up = jnp.einsum("te,tf->ef", mixed, grad_up_act, preferred_element_type=jnp.float32)
    grad_mixed = jnp.einsum(
        "tf,ef->te", grad_gate_act, gate_weight, preferred_element_type=jnp.float32
    ) + jnp.einsum("tf,ef->te", grad_up_act, up_weight, preferred_element_type=jnp.float32)
    grad_gain_two = jnp.sum(grad_mixed * normed_two, axis=0)
    scaled_two = grad_mixed * gain_two
    grad_res = dout + inv_two * (
        scaled_two - normed_two * jnp.mean(scaled_two * normed_two, axis=-1, keepdims=True)
    )
    grad_branch = grad_res.astype(jnp.bfloat16)
    grad_output = jnp.einsum("te,td->ed", attn_low, grad_branch, preferred_element_type=jnp.float32)
    attention_gradient = jnp.einsum(
        "td,ed->te", grad_branch, output_weight, preferred_element_type=jnp.float32
    )
    attention_gradient_reduced = attention_gradient.astype(jnp.bfloat16).reshape(
        token_rows, KEY_HEADS, query_groups, HEAD_SIZE
    )
    delta = jnp.einsum("tkgd,kgtd->kgt", attention_gradient_reduced.astype(jnp.float32), attn)
    key_rows_total, value_rows_total = (
        lax.all_gather(key_rows, "ctx", axis=0, tiled=True),
        lax.all_gather(value_rows, "ctx", axis=0, tiled=True),
    )
    token_length = key_rows_total.shape[0]
    block_size = min(512, token_length)

    def reverse_block_step(grad_query, block_tile):
        key_block, value_block, pblock, sblock = block_tile

        def reverse_work(current):
            key_head_rows = key_block.reshape(block_size, KEY_HEADS, HEAD_SIZE)
            value_head_rows = value_block.reshape(block_size, KEY_HEADS, HEAD_SIZE)
            scores = (
                jnp.einsum(
                    "tkgd,nkd->kgtn",
                    grouped_queries,
                    key_head_rows,
                    preferred_element_type=jnp.float32,
                )
                * scale
            )
            mask = allowed(pblock, sblock, positions, query_seg)[None, None]
            probs = jnp.where(mask, jnp.exp(scores - lse[..., None]), 0.0)
            grad_probs = jnp.einsum(
                "tkgd,nkd->kgtn",
                attention_gradient_reduced,
                value_head_rows,
                preferred_element_type=jnp.float32,
            )
            grad_scores = (probs * (grad_probs - delta[..., None])).astype(jnp.bfloat16)
            updated_state = current + jnp.einsum(
                "kgtn,nkd->tkgd", grad_scores, key_head_rows, preferred_element_type=jnp.float32
            )
            key_gradient_term = (
                jnp.einsum(
                    "kgtn,tkgd->nkd",
                    grad_scores,
                    grouped_queries,
                    preferred_element_type=jnp.float32,
                )
                * scale
            )
            value_gradient_term = jnp.einsum(
                "kgtn,tkgd->nkd",
                probs.astype(jnp.bfloat16),
                attention_gradient_reduced,
                preferred_element_type=jnp.float32,
            )
            return (
                updated_state,
                (
                    key_gradient_term.reshape(block_size, KEY_HEADS * HEAD_SIZE),
                    value_gradient_term.reshape(block_size, KEY_HEADS * HEAD_SIZE),
                ),
            )

        def reverse_leave(current):
            empty_state = jnp.zeros((block_size, KEY_HEADS * HEAD_SIZE), jnp.float32)
            return (current, (empty_state, empty_state))

        return lax.cond(pblock[0] <= positions[-1], reverse_work, reverse_leave, grad_query)

    places = jnp.arange(token_length, dtype=jnp.int32)
    block_tiles = (
        key_rows_total.reshape(-1, block_size, KEY_HEADS * HEAD_SIZE),
        value_rows_total.reshape(-1, block_size, KEY_HEADS * HEAD_SIZE),
        places.reshape(-1, block_size),
        seg_row.reshape(-1, block_size),
    )
    grad_query_rot, (key_gradient_terms, value_gradient_terms) = lax.scan(
        reverse_block_step,
        jnp.zeros((token_rows, KEY_HEADS, query_groups, HEAD_SIZE), jnp.float32),
        block_tiles,
    )
    key_gradient_rows, grad_values = (
        lax.psum_scatter(
            key_gradient_terms.reshape(token_length, KEY_HEADS * HEAD_SIZE),
            "ctx",
            scatter_dimension=0,
            tiled=True,
        ),
        lax.psum_scatter(
            value_gradient_terms.reshape(token_length, KEY_HEADS * HEAD_SIZE),
            "ctx",
            scatter_dimension=0,
            tiled=True,
        ),
    )
    grad_q_low = (
        rotary_apply(
            (grad_query_rot * scale).reshape(token_rows, QUERY_HEADS, HEAD_SIZE),
            cosine_table,
            sine_table,
            -1.0,
        )
        .astype(jnp.bfloat16)
        .reshape(token_rows, QUERY_HEADS * HEAD_SIZE)
    )
    grad_k_low = (
        rotary_apply(
            key_gradient_rows.reshape(token_rows, KEY_HEADS, HEAD_SIZE),
            cosine_table,
            sine_table,
            -1.0,
        )
        .astype(jnp.bfloat16)
        .reshape(token_rows, KEY_HEADS * HEAD_SIZE)
    )
    grad_v_low = grad_values.astype(jnp.bfloat16)
    grad_wq = jnp.einsum(
        "te,tf->ef", activated_hidden, grad_q_low, preferred_element_type=jnp.float32
    )
    grad_wk = jnp.einsum(
        "te,tf->ef", activated_hidden, grad_k_low, preferred_element_type=jnp.float32
    )
    grad_wv = jnp.einsum(
        "te,tf->ef", activated_hidden, grad_v_low, preferred_element_type=jnp.float32
    )
    grad_acted = jnp.einsum(
        "tf,ef->te", grad_q_low, query_weight, preferred_element_type=jnp.float32
    )
    grad_acted = grad_acted + jnp.einsum(
        "tf,ef->te", grad_k_low, key_weight, preferred_element_type=jnp.float32
    )
    grad_acted = grad_acted + jnp.einsum(
        "tf,ef->te", grad_v_low, value_weight, preferred_element_type=jnp.float32
    )
    grad_gain_one = jnp.sum(grad_acted * normed_one, axis=0)
    scaled_one = grad_acted * gain_one
    grad_input = grad_res + inv_one * (
        scaled_one - normed_one * jnp.mean(scaled_one * normed_one, axis=-1, keepdims=True)
    )
    terms = [
        grad_wq.reshape(-1),
        grad_wk.reshape(-1),
        grad_wv.reshape(-1),
        grad_output.reshape(-1),
        grad_gate.reshape(-1),
        grad_up.reshape(-1),
        grad_down.reshape(-1),
        jnp.concatenate([grad_gain_one, grad_gain_two]),
    ]
    return (grad_input.astype(jnp.bfloat16), terms)


def local(
    inputs,
    segments,
    query_weight,
    key_weight,
    value_weight,
    output_weight,
    gate_weight,
    up_weight,
    down_weight,
    norm_gain_pair,
    cotangent,
):
    shard_rows = inputs.shape[2]
    seg_full = lax.all_gather(segments, "ctx", axis=2, tiled=True)
    positions = lax.axis_index("ctx") * shard_rows + jnp.arange(shard_rows, dtype=jnp.int32)
    cosine_table, sine_table = rope_parts(positions)
    weight_matrices = shape_weights(
        (
            lax.all_gather(query_weight, ("grp", "ctx"), axis=0, tiled=True),
            lax.all_gather(key_weight, ("grp", "ctx"), axis=0, tiled=True),
            lax.all_gather(value_weight, ("grp", "ctx"), axis=0, tiled=True),
            lax.all_gather(output_weight, ("grp", "ctx"), axis=0, tiled=True),
            lax.all_gather(gate_weight, ("grp", "ctx"), axis=0, tiled=True),
            lax.all_gather(up_weight, ("grp", "ctx"), axis=0, tiled=True),
            lax.all_gather(down_weight, ("grp", "ctx"), axis=0, tiled=True),
            lax.all_gather(norm_gain_pair, ("grp", "ctx"), axis=0, tiled=True),
        )
    )
    results = []
    saved = []
    for micro_step in range(MICRO):
        xrow = inputs[micro_step, 0].astype(jnp.float32)
        result, kept = forward_rows(
            xrow,
            seg_full[micro_step, 0],
            segments[micro_step, 0],
            positions,
            cosine_table,
            sine_table,
            weight_matrices,
        )
        results.append(result.astype(jnp.bfloat16))
        saved.append(kept)
    mats_back = shape_weights(
        (
            lax.all_gather(query_weight, ("grp", "ctx"), axis=0, tiled=True),
            lax.all_gather(key_weight, ("grp", "ctx"), axis=0, tiled=True),
            lax.all_gather(value_weight, ("grp", "ctx"), axis=0, tiled=True),
            lax.all_gather(output_weight, ("grp", "ctx"), axis=0, tiled=True),
            lax.all_gather(gate_weight, ("grp", "ctx"), axis=0, tiled=True),
            lax.all_gather(up_weight, ("grp", "ctx"), axis=0, tiled=True),
            lax.all_gather(down_weight, ("grp", "ctx"), axis=0, tiled=True),
            lax.all_gather(norm_gain_pair, ("grp", "ctx"), axis=0, tiled=True),
        )
    )
    input_grads = []
    shares = None
    totals = None
    for micro_step in range(MICRO):
        dout = cotangent[micro_step, 0].astype(jnp.float32)
        grad_input, terms = backward_rows(
            dout,
            seg_full[micro_step, 0],
            segments[micro_step, 0],
            positions,
            cosine_table,
            sine_table,
            mats_back,
            saved[micro_step],
        )
        input_grads.append(grad_input)
        totals = terms if totals is None else [a + b for a, b in zip(totals, terms)]
    shares = list(
        (
            lax.psum_scatter(totals[0], ("grp", "ctx"), scatter_dimension=0, tiled=True),
            lax.psum_scatter(totals[1], ("grp", "ctx"), scatter_dimension=0, tiled=True),
            lax.psum_scatter(totals[2], ("grp", "ctx"), scatter_dimension=0, tiled=True),
            lax.psum_scatter(totals[3], ("grp", "ctx"), scatter_dimension=0, tiled=True),
            lax.psum_scatter(totals[4], ("grp", "ctx"), scatter_dimension=0, tiled=True),
            lax.psum_scatter(totals[5], ("grp", "ctx"), scatter_dimension=0, tiled=True),
            lax.psum_scatter(totals[6], ("grp", "ctx"), scatter_dimension=0, tiled=True),
            lax.psum_scatter(totals[7], ("grp", "ctx"), scatter_dimension=0, tiled=True),
        )
    )
    outputs = jnp.stack(results)[:, None]
    input_grad = jnp.stack(input_grads)[:, None]
    return (
        outputs,
        input_grad,
        shares[0],
        shares[1],
        shares[2],
        shares[3],
        shares[4],
        shares[5],
        shares[6],
        shares[7],
    )


W = MODEL_WIDTH
HG = QUERY_HEADS // KEY_HEADS * HEAD_SIZE
QK = HG + HEAD_SIZE
SLAB = 384
QKV = HG + 2 * HEAD_SIZE
OUT = W // 8
BACK = 512
FEED = 432
EDGE = 304
CHUNK = W // 32
HID = HIDDEN_UNITS // 8
SUB = HIDDEN_UNITS // 32
ROWS = 128
ALL = 8 * ROWS
POS = 64
LEN = 512
RELATIVE = (0, 2, 4, 6, 1, 3, 5, 7)
F32 = jnp.float32
BF16 = jnp.bfloat16
SCALE = HEAD_SIZE ** (-0.5)
NT = (((1,), (1,)), ((), ()))
TN = (((0,), (0,)), ((), ()))
MIB = 1024 * 1024


def pc(value, k):
    return lax.ppermute(value, "ctx", [(s, s ^ k) for s in range(8)])


def pz(value, k):
    return lax.ppermute(value, "grp", [(s, s ^ k) for s in range(4)])


def after(value, *others):
    return lax.optimization_barrier((value,) + others)[0]


def first_ctx(value):
    far = pc(value, 6)
    return [value, pc(value, 2), pc(value, 4), far]


def both_cores(mine):
    return mine + [pc(m, 1) for m in mine]


def gather_ctx(value):
    return both_cores(first_ctx(value))


def gather_grp(value):
    one = pz(value, 1)
    two = pz(value, 2)
    return (value, one, two, pz(two, 1))


def add_low(a, b):
    return (a.astype(F32) + b.astype(F32)).astype(BF16)


class Order:
    def __init__(self):
        self.last = None

    def __call__(self, values):
        return values if self.last is None else after(values, self.last)

    def then(self, result):
        self.last = jax.tree.leaves(result)[-1]
        return result

    def wait(self, values):
        return self.then(self(values))


def scatter_ctx(even, got):
    return [add_low(even[k], got[k]) for k in range(4)]


def send_ctx(sums):
    far = pc(sums[3], 6)
    return sums[0], pc(sums[1], 2), pc(sums[2], 4), far


def pick(blocks, g):
    return [lax.dynamic_index_in_dim(blocks, g ^ k, 0, keepdims=False) for k in range(4)]


def call(body, outs, *args, grid=None, in_specs=None, out_specs=None, scratch=(), name=None):
    kwargs = {}
    if grid is not None:
        kwargs = dict(grid=grid, in_specs=in_specs, out_specs=out_specs)
    else:
        kwargs = dict(
            in_specs=[
                pl.BlockSpec(memory_space=pltpu.SMEM)
                if a.dtype == jnp.int32 and a.ndim == 1
                else pl.BlockSpec(memory_space=pltpu.VMEM)
                for a in args
            ],
            out_specs=out_specs or [pl.BlockSpec(memory_space=pltpu.VMEM) for _ in outs],
        )
    return pl.pallas_call(
        body,
        out_shape=outs,
        scratch_shapes=scratch,
        compiler_params=pltpu.CompilerParams(vmem_limit_bytes=32 * MIB),
        cost_estimate=pl.CostEstimate(flops=0, bytes_accessed=1, transcendentals=0),
        name=name,
        **kwargs,
    )(*args)


def late(values):
    return [pltpu.with_memory_space_constraint(v, pltpu.HBM) for v in values]


def hbm(shape, dtype):
    return pltpu.HBM(shape, dtype)


def hbm(shape, dtype):
    return pltpu.HBM(shape, dtype)


def hbm(shape, dtype):
    return pltpu.HBM(shape, dtype)


def sds(shape, dtype):
    return jax.ShapeDtypeStruct(shape, dtype)


def rows_of(ref, count):
    wide = ref.shape[0] // count
    return jnp.concatenate([ref[pl.ds(n, count, stride=wide), :] for n in range(wide)], 1)


def store_rows(ref, rows):
    count = rows.shape[0]
    wide = ref.shape[0] // count
    for n in range(wide):
        ref[pl.ds(n, count, stride=wide), :] = rows[:, n * 128 : (n + 1) * 128]


def pack_body(q_r, k_r, v_r, gate_r, up_r, gain, out, sq, sk, sv, sg, su):
    for src, dst in ((q_r, sq), (k_r, sk), (v_r, sv), (gate_r, sg), (up_r, su)):
        dst[...] = src[...].astype(F32)
    q, k, v, gate, up = (rows_of(s, CHUNK) for s in (sq, sk, sv, sg, su))
    tail = jnp.concatenate([gain[:, n * SLAB : (n + 1) * SLAB] for n in range(3)], 0).astype(F32)
    tail = jnp.concatenate([tail, jnp.zeros((1, SLAB), F32)], 0)
    for h in range(8):
        if h < KEY_HEADS:
            rows = jnp.concatenate(
                [
                    q[:, h * HG : (h + 1) * HG],
                    k[:, h * HEAD_SIZE : (h + 1) * HEAD_SIZE],
                    v[:, h * HEAD_SIZE : (h + 1) * HEAD_SIZE],
                    jnp.zeros((CHUNK, SLAB - QKV), F32),
                ],
                1,
            )
        else:
            rows = jnp.zeros((CHUNK, SLAB), F32)
        out[h, :, :SLAB] = jnp.concatenate([rows, tail], 0).astype(BF16)
        parts = [
            full[:, z * 768 + h * SUB : z * 768 + (h + 1) * SUB] for full in (gate, up) for z in range(4)
        ]
        rows = jnp.concatenate([jnp.concatenate(parts, 1), jnp.zeros((4, 2 * HID), F32)], 0)
        out[h, :, SLAB:] = rows.astype(BF16)


def unpack_body(src, slab, feed):
    for h in range(8):
        slab[h] = src[h, :, :SLAB]
    feed[...] = jnp.concatenate([src[h, :CHUNK, SLAB:].astype(F32) for h in range(8)], 0).astype(BF16)


def join_body(*refs):
    for n, block in enumerate(refs[:8]):
        refs[8][n * ROWS : (n + 1) * ROWS, :] = block[...]


def join(blocks):
    return call(join_body, [sds((ALL, W), BF16)], *blocks, name="join")[0]


def output_weight_body(sc, b0, b1, b2, b3, b4, b5, b6, b7, out, rows):
    i, g = sc[0], sc[1]
    for j, b in zip(RELATIVE, (b0, b1, b2, b3, b4, b5, b6, b7)):
        for k in range(4):
            rows[i ^ j, g ^ k] = b[k].astype(F32)
    for z in range(4):
        for q in range(2):
            parts = [rows_of(rows.at[c, z], CHUNK) for c in range(4 * q, 4 * q + 4)]
            start = z * 288 + q * 144
            out[start : start + 144, :] = jnp.concatenate(parts, 0).astype(BF16)


def rotate(x, cosine, sine, sign):
    lane = lax.broadcasted_iota(jnp.int32, (1, 128), 1) % HEAD_SIZE
    first = lane < HEAD_SIZE // 2
    halves = []
    for n in range(x.shape[1] // 128):
        part = x[:, n * 128 : (n + 1) * 128]
        swapped = jnp.where(first, pltpu.roll(part, 96, 1), pltpu.roll(part, 32, 1))
        halves.append(part * cosine + sign * (swapped * sine))
    return jnp.concatenate(halves, 1)


def attend_body(
    sc, x0, x1, x2, x3, x4, x5, x6, x7, w0, w1, w2, w3, cosine, sine, pcol, prow,
    att, gains, w_o, qk_h, v_h, acted_h, probs_h, x_h, qk_o, v_o, acted, probs, x_o, segs, held, sems,
):
    xs = (x0, x1, x2, x3, x4, x5, x6, x7)
    g = sc[1]
    copies = []

    def send(src, dst):
        copy = pltpu.make_async_copy(src, dst, sems.at[len(copies)])
        copy.start()
        copies.append(copy)

    sums = [jnp.zeros((3, SLAB), F32), jnp.zeros((3, SLAB), F32)]
    for k, w in enumerate((w0, w1, w2, w3)):
        z = g ^ k
        block = jnp.concatenate([w[h, :CHUNK, :].astype(F32) for h in range(8)], 0)
        w_o[pl.ds(pl.multiple_of(z * 288, 32), 288), :] = block.astype(BF16)
        rows = sum(w[h, CHUNK : CHUNK + 3, :].astype(F32) for h in range(8))
        sums[0] = sums[0] + jnp.where(z < 2, rows, 0.0)
        sums[1] = sums[1] + jnp.where(z < 2, 0.0, rows)
    gain = [jnp.concatenate([s[0:1], s[1:2], s[2:3]], 1) for s in sums]
    gains[...] = jnp.concatenate([gain[0], gain[1], jnp.zeros((6, W), F32)], 0)
    for b in range(8):
        x_o[b * ROWS : (b + 1) * ROWS, :] = xs[b][:, :W]
        segs[b] = xs[b][:, W:]

    @pl.loop(0, 8)
    def _(b):
        at = pl.ds(pl.multiple_of(b * ROWS, ROWS), ROWS)
        x = x_o[at, :].astype(F32)
        inv = lax.rsqrt(jnp.mean(x * x, axis=-1, keepdims=True) + EPS)
        acted[at, :] = (x * inv * gain[0]).astype(BF16)

    send(x_o, x_h)
    send(acted, acted_h)

    @pl.loop(0, MICRO)
    def _(m):
        part = pl.ds(pl.multiple_of(m * POS, POS), POS)
        rows = jnp.concatenate(
            [acted[pl.ds(pl.multiple_of(b * ROWS + m * POS, POS), POS), :] for b in range(8)], 0
        )
        seg = jnp.concatenate([segs[b, part, :].astype(F32) for b in range(8)], 0)
        y = jnp.dot(rows, w_o[...], preferred_element_type=F32)
        qk = rotate(y[:, :QK], cosine[...], sine[...], 1.0).astype(BF16)
        v = y[:, QK:].astype(BF16)
        qk_o[m] = qk
        v_o[m] = v
        seg_row = jnp.transpose(seg)[0:1, :]
        mask = (prow[0:1, :] <= pcol[:, 0:1]) & (seg_row == seg[:, 0:1])
        bias = jnp.where(mask, 0.0, NEGATIVE_LARGE)
        keys = qk[:, HG:]
        for h in range(3):
            s = lax.dot_general(
                qk[:, h * HEAD_SIZE : (h + 1) * HEAD_SIZE], keys, NT, preferred_element_type=F32
            )
            s = s * SCALE + bias
            e = jnp.exp(s - jnp.max(s, axis=-1, keepdims=True))
            p = (e * (1.0 / jnp.sum(e, axis=-1, keepdims=True))).astype(BF16)
            probs[m, h] = p
            held[m, :, h * HEAD_SIZE : (h + 1) * HEAD_SIZE] = jnp.dot(
                p, v[:, :HEAD_SIZE], preferred_element_type=F32
            ).astype(BF16)

    for m in range(MICRO):
        att[:, m * HG : (m + 1) * HG] = held[m]
    send(probs, probs_h)
    send(qk_o, qk_h)
    send(v_o, v_h)
    for copy in copies:
        copy.wait()


def project_body(sc, x, a0, a1, a2, a3, a4, a5, a6, a7, wo, gains, att_o, mixed_o, res_o, heads):
    i = sc[0]
    t = pl.program_id(0)
    for j, a in zip(RELATIVE, (a0, a1, a2, a3, a4, a5, a6, a7)):
        h = i ^ j
        for half in range(2):
            b = 2 * t + half
            q = (2 * (b & 3) + (b >> 2)) ^ j
            start = pl.multiple_of(((q & 1) * 4 + (q >> 1)) * POS, POS)
            rows = a[pl.ds(start, POS), :]
            for m in range(MICRO):
                heads[h, half * ROWS + m * POS : half * ROWS + (m + 1) * POS, :] = rows[:, m * HG : (m + 1) * HG]
    for h in range(KEY_HEADS):
        att_o[:, h * HG : (h + 1) * HG] = heads[h]
    residual = x[...].astype(F32) + jnp.dot(att_o[...], wo[...], preferred_element_type=F32)

    @pl.when(t == 0)
    def _():
        res_o[...] = residual[:ROWS]

    inv = lax.rsqrt(jnp.mean(residual * residual, axis=-1, keepdims=True) + EPS)
    mixed_o[...] = (residual * inv * gains[1:2, :]).astype(BF16)


def feed_body(
    sc, mixed_r, c, g0, g1, g2, g3, d0, d1, d2, d3, hidden_o, dgu_o, pm, pe, dn, sums, gu
):
    g = sc[1]
    t = pl.program_id(0)

    @pl.when(t == 0)
    def _():
        for k, (a, d) in enumerate(((g0, d0), (g1, d1), (g2, d2), (g3, d3))):
            z = g ^ k
            gu[pl.ds(pl.multiple_of(z * 288, 32), 288), :] = a[...]
            dn[pl.ds(pl.multiple_of(z * SUB, 32), SUB), :] = d[...]
        sums[...] = jnp.zeros((8, W), F32)

    mixed = mixed_r[...]
    y = jnp.dot(mixed, gu[...], preferred_element_type=F32)
    gate = y[:, :HID]
    up = y[:, HID:]
    sig = 1.0 / (1.0 + jnp.exp(-gate))
    silu = gate * sig
    hidden_o[...] = (silu * up).astype(BF16)
    dh = lax.dot_general(c[...], dn[...], NT, preferred_element_type=F32)
    dgate = (dh * up * (sig + silu * (1.0 - sig))).astype(BF16)
    dup = (dh * silu).astype(BF16)
    dgu = jnp.concatenate([dgate, dup], 1)
    dgu_o[...] = dgu
    dm = lax.dot_general(dgu, gu[...], NT, preferred_element_type=F32)
    sums[0:1, :] = sums[0:1, :] + jnp.sum(dm * mixed.astype(F32), axis=0, keepdims=True)
    dm = dm.astype(BF16).reshape(2, ROWS, W)

    @pl.when(t < 2)
    def _():
        pm[...] = dm

    @pl.when(t >= 2)
    def _():
        pe[...] = dm


def mid_body(a, b, d, f, c, res, gains, dres, low):
    dm = a[...].astype(F32) + b[...].astype(F32) + d[...].astype(F32) + f[...].astype(F32)
    r = res[...]
    inv = lax.rsqrt(jnp.mean(r * r, axis=-1, keepdims=True) + EPS)
    n = r * inv
    e = dm * gains[1:2, :]
    out = c[...].astype(F32) + inv * (e - n * jnp.mean(e * n, axis=-1, keepdims=True))
    dres[...] = out
    low[...] = out.astype(BF16)


def last_body(a, b, d, f, x, dres, gains, out):
    da = a[...].astype(F32) + b[...].astype(F32) + d[...].astype(F32) + f[...].astype(F32)
    r = x[...].astype(F32)
    inv = lax.rsqrt(jnp.mean(r * r, axis=-1, keepdims=True) + EPS)
    n = r * inv
    e = da * gains[0:1, :]
    out[...] = (dres[...] + inv * (e - n * jnp.mean(e * n, axis=-1, keepdims=True))).astype(BF16)


def back_body(
    sc, l0, l1, l2, l3, l4, l5, l6, l7, wo, qk_r, v_r, probs, cosine, sine, acted_t, att_t, w_slab, gains, sums,
    out, b0, b1, b2, b3, columns, dots, edge,
):
    lows = (l0, l1, l2, l3, l4, l5, l6, l7)
    i, g = sc[0], sc[1]
    place = lax.broadcasted_iota(jnp.int32, (256, W), 1) - lax.broadcasted_iota(jnp.int32, (256, W), 0)
    chosen = jnp.where(place == i * OUT, 1.0, 0.0).astype(BF16)
    @pl.loop(0, MICRO)
    def _(m):
        part = pl.ds(pl.multiple_of(m * POS, POS), POS)
        rows = jnp.concatenate([lows[b][part, :] for b in range(8)], 0)
        datt = lax.dot_general(rows, wo[...], NT, preferred_element_type=F32).astype(BF16)
        chosen_rows = lax.dot_general(rows, chosen, NT, preferred_element_type=F32).astype(BF16)
        qk = qk_r[m]
        keys = qk[:, HG:]
        v = v_r[m][:, :HEAD_SIZE]
        dq = []
        dk = jnp.zeros((HEAD_SIZE, LEN), F32)
        dv = jnp.zeros((HEAD_SIZE, LEN), F32)
        for h in range(3):
            da = datt[:, h * HEAD_SIZE : (h + 1) * HEAD_SIZE]
            q = qk[:, h * HEAD_SIZE : (h + 1) * HEAD_SIZE]
            low = probs[m, h]
            p = low.astype(F32)
            dp = lax.dot_general(da, v, NT, preferred_element_type=F32)
            delta = jnp.sum(p * dp, axis=-1, keepdims=True)
            ds = (p * (dp - delta)).astype(BF16)
            dq.append(jnp.dot(ds, keys, preferred_element_type=F32))
            dk = dk + lax.dot_general(q, ds, TN, preferred_element_type=F32)
            dv = dv + lax.dot_general(da, low, TN, preferred_element_type=F32)
        dqk = jnp.concatenate(dq + [jnp.transpose(dk)], 1) * SCALE
        dqk = rotate(dqk, cosine[...], sine[...], -1.0)
        dvt = jnp.transpose(jnp.concatenate([dv, jnp.zeros((HEAD_SIZE, LEN), F32)], 0))
        full = jnp.concatenate([dqk, dvt], 1).astype(BF16)
        for b in range(8):
            at = pl.ds(pl.multiple_of(b * ROWS + m * POS, POS), POS)
            out[at, :] = full[b * POS : (b + 1) * POS, :]
            columns[at, :] = chosen_rows[b * POS : (b + 1) * POS, :]

    blocks = (b0, b1, b2, b3)
    for k in range(4):
        z = g ^ k
        start = pl.multiple_of(z * 288, 32)
        y = jnp.dot(acted_t[pl.ds(start, 288), :], out[...], preferred_element_type=F32)
        yo = jnp.dot(att_t[pl.ds(start, 288), :], columns[...], preferred_element_type=F32)
        y2 = jnp.concatenate([y[:, :QKV], yo[:, : BACK - QKV]], 1)
        blocks[k][:288, :] = y2.astype(BF16)
        dot = jnp.sum(y * w_slab[pl.ds(start, 288), :].astype(F32), axis=-1, keepdims=True)
        dots[z] = jnp.transpose(jnp.broadcast_to(dot, (288, 128)))[:8, :]
    one = jnp.concatenate([dots[z][0:1, :] for z in range(4)], 1) / gains[0:1, :]
    two = sums[0:1, :] / gains[1:2, :]
    for z in range(4):
        full = one if z < 2 else two
        at = (z % 2) * 576
        rows = jnp.concatenate([full[:, at + 72 * c : at + 72 * (c + 1)] for c in range(8)], 0)
        rows = jnp.concatenate([rows, jnp.zeros((8, BACK - 72), F32)], 1)
        edge[z] = jnp.concatenate([rows, jnp.zeros((EDGE - 288 - 8, BACK), F32)], 0)
    for k in range(4):
        blocks[k][288:, :] = edge[g ^ k].astype(BF16)


def split_back_body(a, b, d, out):
    rows = a[...].astype(F32) + b[...].astype(F32) + d[...].astype(F32)
    for h in range(8):
        block = [rows[h * CHUNK : (h + 1) * CHUNK, :], rows[288 + h : 289 + h, :], jnp.zeros((3, BACK), F32)]
        out[h] = jnp.concatenate(block, 0).astype(BF16)


def grads_body(sc, grad_gu, grad_dn, b0, b1, b2, b3):
    g = sc[1]
    for k, block in enumerate((b0, b1, b2, b3)):
        z = g ^ k
        block[:288, :] = grad_gu[pl.ds(pl.multiple_of(z * 288, 32), 288), :]
        start = pl.multiple_of(z * SUB, 32)
        block[288 : 288 + SUB, :] = grad_dn[pl.ds(start, SUB), :768]
        block[288 + SUB :, :HID] = grad_dn[pl.ds(start, SUB // 2), 768:]
        block[288 + SUB :, HID:] = grad_dn[pl.ds(pl.multiple_of(start + SUB // 2, 16), SUB // 2), 768:]


def transpose_body(src, out):
    for n in range(ALL // 256):
        for m in range(W // 384):
            block = src[n * 256 : (n + 1) * 256, m * 384 : (m + 1) * 384]
            out[m * 384 : (m + 1) * 384, n * 256 : (n + 1) * 256] = jnp.transpose(block)


def transpose(value):
    return call(transpose_body, [sds((W, ALL), BF16)], value, name="transpose")[0]


def onward_body(rows, weight, even, odd):
    dims = NT if weight.shape[0] == W else (((1,), (0,)), ((), ()))
    for n in range(4):
        part = rows[n * 2 * ROWS : (n + 1) * 2 * ROWS, :]
        y = lax.dot_general(part, weight[...], dims, preferred_element_type=F32).astype(BF16)
        out = even if n < 2 else odd
        out[2 * (n % 2)] = y[:ROWS]
        out[2 * (n % 2) + 1] = y[ROWS:]


def onward(rows, weight, name):
    return call(onward_body, [sds((4, ROWS, W), BF16)] * 2, rows, weight, name=name)


def split_feed_body(a, b, d, out, down):
    rows = a[...].astype(F32) + b[...].astype(F32) + d[...].astype(F32)
    for h in range(8):
        out[h] = rows[h * CHUNK : (h + 1) * CHUNK, :].astype(BF16)
    right = jnp.concatenate([rows[288 + SUB :, :HID], rows[288 + SUB :, HID:]], 0)
    store_rows(down, jnp.concatenate([rows[288 : 288 + SUB, :], right], 1))


def split_back_body(a, b, d, out):
    rows = a[...].astype(F32) + b[...].astype(F32) + d[...].astype(F32)
    for h in range(8):
        block = [rows[h * CHUNK : (h + 1) * CHUNK, :], rows[288 + h : 289 + h, :], jnp.zeros((3, BACK), F32)]
        out[h] = jnp.concatenate(block, 0).astype(BF16)


def unpack_back_body(src, q, k, v, o, gains):
    parts = [src[h].astype(F32) for h in range(8)]
    rows = [p[:CHUNK, :] for p in parts]
    store_rows(q, jnp.concatenate([p[:, :HG] for p in rows[:KEY_HEADS]], 1))
    store_rows(k, jnp.concatenate([p[:, HG:QK] for p in rows[:KEY_HEADS]], 1))
    store_rows(v, jnp.concatenate([p[:, QK:QKV] for p in rows[:KEY_HEADS]], 1))
    store_rows(o, jnp.concatenate([p[:, QKV : QKV + OUT] for p in rows], 1))
    gains[...] = jnp.broadcast_to(sum(p[CHUNK : CHUNK + 1, :128] for p in parts), (8, 128))


def unpack_hidden_body(src, gate, up):
    for n, out in enumerate((gate, up)):
        parts = [
            src[h, :, n * HID + z * SUB : n * HID + (z + 1) * SUB].astype(F32)
            for z in range(4)
            for h in range(8)
        ]
        store_rows(out, jnp.concatenate(parts, 1))


def fast_local(inputs, segments, wq, wk, wv, wo, wg, wu, wd, gain_pair, cotangent):
    i = lax.axis_index("ctx").astype(jnp.int32)
    g = lax.axis_index("grp").astype(jnp.int32)
    r = g * 8 + i
    sc = jnp.stack([i, g])
    x_own = inputs.reshape(ROWS, W)
    c_own = cotangent.reshape(ROWS, W)
    order = Order()

    q2, k2, v2, gate2, up2 = (w.reshape(-1, 128) for w in (wq, wk, wv, wg, wu))
    placed = lax.dynamic_update_slice(jnp.zeros((1, W), BF16), gain_pair[None, :], (0, (r % 16) * 72))
    packed = order.then(
        call(
            pack_body,
            [sds((8, 40, SLAB + 2 * HID), BF16)],
            *late([q2, k2, v2, gate2, up2]), placed,
            scratch=[pltpu.VMEM(a.shape, F32) for a in (q2, k2, v2, gate2, up2)], name="pack",
        )
    )[0]
    packed = lax.all_to_all(packed, "ctx", 0, 0, tiled=True)

    x_late, seg_late, wo, wd, i_late, c_late = order((x_own, segments, wo, wd, i, c_own))
    o_own = wo.reshape(-1, 128)
    o_one, o_two = pz(o_own, 1), pz(o_own, 2)
    seg = jnp.broadcast_to(seg_late.reshape(ROWS, 1).astype(BF16), (ROWS, 128))
    x_sent = order.then(jnp.concatenate([x_late, seg], 1))
    d_own = order.then(order(wd).reshape(SUB, W))
    packed, o_one, o_two = order.wait((packed, o_one, o_two))

    slab, feed = order.then(
        call(unpack_body, [sds((8, 40, SLAB), BF16), sds((288, 2 * HID), BF16)], packed, name="unpack")
    )
    s_one, s_two = pz(slab, 1), pz(slab, 2)
    xs = first_ctx(order(x_sent))

    i_late = order(i_late)
    rel = jnp.array(RELATIVE, jnp.int32)
    positions = ((i_late ^ rel)[:, None] * POS + jnp.arange(POS, dtype=jnp.int32)[None, :]).reshape(LEN)
    half = HEAD_SIZE // 2
    freq = THETA ** (-jnp.arange(half, dtype=F32) * 2.0 / HEAD_SIZE)
    angle = positions.astype(F32)[:, None] * freq[None, :]
    cosine = jnp.tile(jnp.cos(angle), (1, 4))
    sine = jnp.sin(angle)
    sine = jnp.concatenate([-sine, sine, -sine, sine], 1)
    pcol = jnp.broadcast_to(positions.astype(F32)[:, None], (LEN, 128))
    prow = jnp.broadcast_to(positions.astype(F32)[None, :], (8, LEN))
    cosine, sine, pcol, prow = order.then((cosine, sine, pcol, prow))

    s_one = order.wait(s_one)
    o_three = pz(order(o_two), 1)
    s_two = order.wait(s_two)
    s_three = pz(s_two, 1)
    o_three = order.wait(o_three)
    g_one = pz(order(feed), 1)
    s_three = order.wait(s_three)
    g_two = pz(order(feed), 2)
    xs = order.wait(both_cores(order.wait(xs)))
    o_sent = order.then(jnp.stack([o_own, o_one, o_two, o_three]))
    os = first_ctx(o_sent)
    xs, slabs = order((xs, (slab, s_one, s_two, s_three)))

    anywhere = pl.BlockSpec(memory_space=pl.ANY)
    vmem = pl.BlockSpec(memory_space=pltpu.VMEM)
    held = [
        sds((MICRO, LEN, QK), BF16),
        sds((MICRO, LEN, 128), BF16),
        sds((ALL, W), BF16),
        sds((MICRO, 3, LEN, LEN), BF16),
        sds((ALL, W), BF16),
    ]
    att, gains, w_slab, qk, v, acted, probs, call_x = order.then(
        call(
            attend_body,
            [sds((LEN, 2 * HG), BF16), sds((8, W), F32), sds((W, SLAB), BF16)]
            + [hbm(o.shape, o.dtype) for o in held],
            sc, *late(xs), *late(slabs), cosine, sine, pcol, prow,
            out_specs=[vmem] * 3 + [anywhere] * 5,
            scratch=[pltpu.VMEM(o.shape, o.dtype) for o in held]
            + [pltpu.VMEM((8, ROWS, 128), BF16), pltpu.VMEM((MICRO, LEN, HG), BF16), pltpu.SemaphoreType.DMA((5,))],
            name="attend",
        )
    )
    att, g_one, g_two = order.wait((att, g_one, g_two))
    heads = first_ctx(att)
    os = order.wait(both_cores(order.wait(os)))
    w_out = order.then(
        call(
            output_weight_body, [sds((W, W), BF16)], sc, *late(os),
            scratch=[pltpu.VMEM((8, 4, wo.size // 128, 128), F32)], name="output_weight",
        )
    )[0]
    g_three = pz(order(g_two), 1)
    d_one, d_two = pz(order(d_own), 1), pz(order(d_own), 2)
    acted_t = order.then(transpose(order(acted)))
    d_one, d_two = order.wait((d_one, d_two))
    d_three = pz(d_two, 1)
    heads[1], heads[2] = order.wait((heads[1], heads[2]))
    heads = order.wait(both_cores(order.wait(heads)))
    cs = first_ctx(order(c_late))
    g_three, d_three = order.wait((g_three, d_three))

    whole = lambda *shape: pl.BlockSpec(shape, lambda t: (0,) * len(shape))
    rowb = lambda n: pl.BlockSpec((256, n), lambda t: (t, 0))
    smem = pl.BlockSpec(memory_space=pltpu.SMEM)
    att_full, mixed, res_own = order.then(
        call(
            project_body,
            [hbm((ALL, W), BF16), sds((ALL, W), BF16), hbm((ROWS, W), F32)],
            sc, call_x, *late(heads), w_out, gains,
            grid=(4,),
            in_specs=[smem, rowb(W)] + [whole(LEN, 2 * HG)] * 8 + [whole(W, W), whole(8, W)],
            out_specs=[rowb(W), rowb(W), whole(ROWS, W)],
            scratch=[pltpu.VMEM((8, 256, HG), BF16)], name="project",
        )
    )
    wo_own = order.then(lax.dynamic_slice(order(w_out), (jnp.minimum(i, KEY_HEADS - 1) * HG, 0), (HG, W)))
    call_c = order.then(join(late(order(both_cores(order.wait(cs))))))
    feeds = order((feed, g_one, g_two, g_three, d_own, d_one, d_two, d_three))
    hidden, dgu, pm, pe, down, dots_two = order.then(
        call(
            feed_body,
            [
                sds((ALL, HID), BF16),
                sds((ALL, 2 * HID), BF16),
                sds((4, ROWS, W), BF16),
                sds((4, ROWS, W), BF16),
                sds((HID, W), BF16),
                sds((8, W), F32),
            ],
            sc, mixed, call_c, *late(feeds),
            grid=(4,),
            in_specs=[smem, rowb(W), rowb(W)] + [whole(288, 2 * HID)] * 4 + [whole(SUB, W)] * 4,
            out_specs=[
                rowb(HID),
                rowb(2 * HID),
                pl.BlockSpec((2, ROWS, W), lambda t: (jnp.minimum(t, 1), 0, 0)),
                pl.BlockSpec((2, ROWS, W), lambda t: (jnp.maximum(t - 2, 0), 0, 0)),
                whole(HID, W),
                whole(8, W),
            ],
            scratch=[pltpu.VMEM((W, 2 * HID), BF16)], name="feed",
        )
    )

    got = pc(pe, 1)
    grad_gu = order.then(lax.dot_general(order(mixed), dgu, TN, preferred_element_type=F32).astype(BF16))
    terms = send_ctx(order.then(scatter_ctx(pm, order(got))))
    grad_dn = order.then(lax.dot_general(order(hidden), call_c, TN, preferred_element_type=F32).astype(BF16))
    feed_blocks = order.then(
        call(grads_body, [hbm((FEED, 2 * HID), BF16)] * 4, sc, grad_gu, grad_dn, name="grads")
    )
    feed_far = pz(feed_blocks[3], 1)
    att_t = order.then(transpose(order(att_full)))
    dres, low = order.then(
        call(
            mid_body, [hbm((ROWS, W), F32), hbm((ROWS, W), BF16)],
            *late([*order(terms), c_own, res_own]), gains, name="mid",
        )
    )
    lows = first_ctx(low)
    feed_mid = order.then(add_low(feed_blocks[2], order(feed_far)))
    feed_terms = (feed_blocks[0], pz(after(feed_blocks[1], feed_mid), 1), pz(feed_mid, 2))

    om_p, oe_p = order.then(onward(order(hidden), down, "outward"))
    out_got = pc(oe_p, 1)
    out_terms = send_ctx(order.then(scatter_ctx(om_p, order(out_got))))
    lows = both_cores(order(lows))

    dqkv, *slab_blocks = order.then(
        call(
            back_body,
            [sds((ALL, SLAB), BF16)] + [sds((EDGE, BACK), BF16)] * 4,
            sc, *late(order(lows)), wo_own, qk, v, probs, cosine, sine, acted_t, att_t, w_slab, gains, dots_two,
            scratch=[
                pltpu.VMEM((ALL, 256), BF16),
                pltpu.VMEM((4, 8, 288), F32),
                pltpu.VMEM((4, EDGE - 288, BACK), F32),
            ],
            name="back",
        )
    )
    slab_far = pz(slab_blocks[3], 1)
    hid_sum, grad_down = order.then(
        call(
            split_feed_body, [sds((8, CHUNK, 2 * HID), BF16), sds((864, 128), F32)],
            *late(order(feed_terms)), name="split_feed",
        )
    )
    hid_sum = lax.all_to_all(hid_sum, "ctx", 0, 0, tiled=True)
    dam, dae = order.then(onward(order(dqkv), w_slab, "inward"))
    in_got = pc(dae, 1)
    slab_mid = order.then(add_low(slab_blocks[2], order(slab_far)))
    slab_terms = (slab_blocks[0], pz(after(slab_blocks[1], slab_mid), 1), pz(slab_mid, 2))
    in_terms = send_ctx(order.then(scatter_ctx(dam, order(in_got))))

    outputs = order.then((res_own + sum(t.astype(F32) for t in order(out_terms))).astype(BF16))
    grad_gate, grad_up = order.then(
        call(unpack_hidden_body, [sds((864, 128), F32), sds((864, 128), F32)], order(hid_sum), name="unpack_hidden")
    )
    slab = order.then(call(split_back_body, [sds((8, 40, BACK), BF16)], *late(order(slab_terms)), name="split_back"))[0]
    slab = lax.all_to_all(slab, "ctx", 0, 0, tiled=True)
    input_grad = order.then(
        call(last_body, [sds((ROWS, W), BF16)], *late([*order(in_terms), x_own, dres]), gains, name="last")
    )[0]
    grad_q, grad_k, grad_v, grad_out, grad_gains = call(
        unpack_back_body,
        [sds((324, 128), F32), sds((108, 128), F32), sds((108, 128), F32), sds((324, 128), F32), sds((8, 128), F32)],
        order(slab), name="unpack_back",
    )
    grad_gains = grad_gains[0, :72]

    shape = (MICRO, 1, POS, W)
    return (
        outputs.reshape(shape),
        input_grad.reshape(shape),
        grad_q.reshape(-1),
        grad_k.reshape(-1),
        grad_v.reshape(-1),
        grad_out.reshape(-1),
        grad_gate.reshape(-1),
        grad_up.reshape(-1),
        grad_down.reshape(-1),
        grad_gains,
    )


def solution(mesh):
    in_specs = (
        P(None, "grp", "ctx", None),
        P(None, "grp", "ctx"),
        P(("grp", "ctx")),
        P(("grp", "ctx")),
        P(("grp", "ctx")),
        P(("grp", "ctx")),
        P(("grp", "ctx")),
        P(("grp", "ctx")),
        P(("grp", "ctx")),
        P(("grp", "ctx")),
        P(None, "grp", "ctx", None),
    )
    out_specs = (
        P(None, "grp", "ctx", None),
        P(None, "grp", "ctx", None),
        P(("grp", "ctx")),
        P(("grp", "ctx")),
        P(("grp", "ctx")),
        P(("grp", "ctx")),
        P(("grp", "ctx")),
        P(("grp", "ctx")),
        P(("grp", "ctx")),
        P(("grp", "ctx")),
    )
    fits = (mesh.shape["ctx"], mesh.shape["grp"]) == (8, 4)
    return jax.shard_map(
        fast_local if fits else local,
        mesh=mesh,
        in_specs=in_specs,
        out_specs=out_specs,
        check_vma=False,
    )
```

```python
import jax
import jax.numpy as jnp
from jax import lax
from jax.experimental import pallas as pl
from jax.experimental.pallas import tpu as pltpu
from jax.sharding import PartitionSpec as P

MODEL_WIDTH = 1152
QUERY_HEADS = 18
KEY_HEADS = 6
HEAD_SIZE = 64
HIDDEN_UNITS = 3072
MICRO = 2


EPS = 1e-05
THETA = 10000.0
NEGATIVE_LARGE = -1e30


def rope_parts(positions):
    half = HEAD_SIZE // 2
    freq = THETA ** (-jnp.arange(half, dtype=jnp.float32) * 2.0 / HEAD_SIZE)
    angle = positions.astype(jnp.float32)[:, None] * freq[None, :]
    return (jnp.cos(angle)[:, None, :], jnp.sin(angle)[:, None, :])


def rotary_apply(value_rows, cosine_table, sine_table, sign):
    half = value_rows.shape[-1] // 2
    first = value_rows[..., :half]
    second = value_rows[..., half:]
    return jnp.concatenate(
        [
            first * cosine_table - sign * second * sine_table,
            second * cosine_table + sign * first * sine_table,
        ],
        -1,
    )


def shape_weights(full_precision):
    return (
        full_precision[0].reshape(MODEL_WIDTH, QUERY_HEADS * HEAD_SIZE),
        full_precision[1].reshape(MODEL_WIDTH, KEY_HEADS * HEAD_SIZE),
        full_precision[2].reshape(MODEL_WIDTH, KEY_HEADS * HEAD_SIZE),
        full_precision[3].reshape(QUERY_HEADS * HEAD_SIZE, MODEL_WIDTH),
        full_precision[4].reshape(MODEL_WIDTH, HIDDEN_UNITS),
        full_precision[5].reshape(MODEL_WIDTH, HIDDEN_UNITS),
        full_precision[6].reshape(HIDDEN_UNITS, MODEL_WIDTH),
        full_precision[7],
    )


def allowed(key_pos, key_seg, query_pos, query_seg):
    return (key_pos[None, :] <= query_pos[:, None]) & (key_seg[None, :] == query_seg[:, None])


def online_step(
    state, grouped_queries, key_block, value_block, pblock, sblock, query_pos, query_seg
):
    best, total, accum = state
    block_span = key_block.shape[0]
    key_head_rows = key_block.reshape(block_span, KEY_HEADS, HEAD_SIZE)
    value_head_rows = value_block.reshape(block_span, KEY_HEADS, HEAD_SIZE)
    scores = jnp.einsum(
        "tkgd,nkd->kgtn", grouped_queries, key_head_rows, preferred_element_type=jnp.float32
    ) * HEAD_SIZE ** (-0.5)
    mask = allowed(pblock, sblock, query_pos, query_seg)[None, None]
    scores = jnp.where(mask, scores, NEGATIVE_LARGE)
    new_best = jnp.maximum(best, jnp.max(scores, axis=-1))
    factor = jnp.exp(best - new_best)
    expo = jnp.where(mask, jnp.exp(scores - new_best[..., None]), 0.0)
    total = total * factor + jnp.sum(expo, axis=-1)
    accum = accum * factor[..., None] + jnp.einsum(
        "kgtn,nkd->kgtd",
        expo.astype(jnp.bfloat16),
        value_head_rows,
        preferred_element_type=jnp.float32,
    )
    return (new_best, total, accum)


def guarded_step(
    state, grouped_queries, key_block, value_block, pblock, sblock, query_pos, query_seg
):

    def guarded_work(current):
        return online_step(
            current, grouped_queries, key_block, value_block, pblock, sblock, query_pos, query_seg
        )

    def guarded_leave(current):
        return current

    return lax.cond(pblock[0] <= query_pos[-1], guarded_work, guarded_leave, state)


def online_blocks(
    carry, grouped_queries, key_rows, value_rows, key_pos, key_seg, query_pos, query_seg
):
    count = key_rows.shape[0]
    block_size = 512 if count > 512 and count % 512 == 0 else count
    if block_size == count:
        return guarded_step(
            carry, grouped_queries, key_rows, value_rows, key_pos, key_seg, query_pos, query_seg
        )

    def step(state, block_tile):
        return (
            guarded_step(
                state,
                grouped_queries,
                block_tile[0],
                block_tile[1],
                block_tile[2],
                block_tile[3],
                query_pos,
                query_seg,
            ),
            None,
        )

    block_tiles = (
        key_rows.reshape(-1, block_size, key_rows.shape[1]),
        value_rows.reshape(-1, block_size, value_rows.shape[1]),
        key_pos.reshape(-1, block_size),
        key_seg.reshape(-1, block_size),
    )
    carry, _ = lax.scan(step, carry, block_tiles)
    return carry


def forward_rows(xrow, seg_row, query_seg, positions, cosine_table, sine_table, weight_matrices):
    (
        query_weight,
        key_weight,
        value_weight,
        output_weight,
        gate_weight,
        up_weight,
        down_weight,
        gains,
    ) = weight_matrices
    token_rows = xrow.shape[0]
    query_groups = QUERY_HEADS // KEY_HEADS
    gain_one = gains[:MODEL_WIDTH].astype(jnp.float32)
    gain_two = gains[MODEL_WIDTH:].astype(jnp.float32)
    inv_one = lax.rsqrt(jnp.mean(xrow * xrow, axis=-1, keepdims=True) + EPS)
    normed_one = xrow * inv_one
    activated_hidden = (normed_one * gain_one).astype(jnp.bfloat16)
    query_unrotated = jnp.dot(
        activated_hidden, query_weight, preferred_element_type=jnp.float32
    ).reshape(token_rows, QUERY_HEADS, HEAD_SIZE)
    key_unrotated = jnp.dot(
        activated_hidden, key_weight, preferred_element_type=jnp.float32
    ).reshape(token_rows, KEY_HEADS, HEAD_SIZE)
    value_raw = jnp.dot(activated_hidden, value_weight, preferred_element_type=jnp.float32)
    grouped_queries = (
        rotary_apply(query_unrotated, cosine_table, sine_table, 1.0)
        .astype(jnp.bfloat16)
        .reshape(token_rows, KEY_HEADS, query_groups, HEAD_SIZE)
    )
    key_rows = (
        rotary_apply(key_unrotated, cosine_table, sine_table, 1.0)
        .astype(jnp.bfloat16)
        .reshape(token_rows, KEY_HEADS * HEAD_SIZE)
    )
    value_rows = value_raw.astype(jnp.bfloat16)
    start_state = (
        jnp.full((KEY_HEADS, query_groups, token_rows), NEGATIVE_LARGE, jnp.float32),
        jnp.zeros((KEY_HEADS, query_groups, token_rows), jnp.float32),
        jnp.zeros((KEY_HEADS, query_groups, token_rows, HEAD_SIZE), jnp.float32),
    )
    piece = (
        lax.all_gather(key_rows, "ctx", axis=0, tiled=True),
        lax.all_gather(value_rows, "ctx", axis=0, tiled=True),
    )
    count = piece[0].shape[0]
    key_pos = jnp.arange(count, dtype=jnp.int32)
    best, total, accum = online_blocks(
        start_state, grouped_queries, piece[0], piece[1], key_pos, seg_row, positions, query_seg
    )
    attn = accum / total[..., None]
    lse = best + jnp.log(total)
    attn_low = (
        jnp.transpose(attn, (2, 0, 1, 3))
        .reshape(token_rows, QUERY_HEADS * HEAD_SIZE)
        .astype(jnp.bfloat16)
    )
    residual = xrow + jnp.dot(attn_low, output_weight, preferred_element_type=jnp.float32)
    inv_two = lax.rsqrt(jnp.mean(residual * residual, axis=-1, keepdims=True) + EPS)
    normed_two = residual * inv_two
    mixed = (normed_two * gain_two).astype(jnp.bfloat16)
    gate = jnp.dot(mixed, gate_weight, preferred_element_type=jnp.float32)
    upper = jnp.dot(mixed, up_weight, preferred_element_type=jnp.float32)
    hidden = (jax.nn.silu(gate) * upper).astype(jnp.bfloat16)
    result = residual + jnp.dot(hidden, down_weight, preferred_element_type=jnp.float32)
    kept = (
        inv_one,
        normed_one,
        activated_hidden,
        grouped_queries,
        key_rows,
        value_rows,
        attn,
        lse,
        attn_low,
        inv_two,
        normed_two,
        mixed,
        gate,
        upper,
        hidden,
    )
    return (result, kept)


def backward_rows(
    dout, seg_row, query_seg, positions, cosine_table, sine_table, weight_matrices, kept
):
    (
        query_weight,
        key_weight,
        value_weight,
        output_weight,
        gate_weight,
        up_weight,
        down_weight,
        gains,
    ) = weight_matrices
    (
        inv_one,
        normed_one,
        activated_hidden,
        grouped_queries,
        key_rows,
        value_rows,
        attn,
        lse,
        attn_low,
        inv_two,
        normed_two,
        mixed,
        gate,
        upper,
        hidden,
    ) = kept
    token_rows = dout.shape[0]
    query_groups = QUERY_HEADS // KEY_HEADS
    scale = HEAD_SIZE ** (-0.5)
    gain_one = gains[:MODEL_WIDTH].astype(jnp.float32)
    gain_two = gains[MODEL_WIDTH:].astype(jnp.float32)
    dout_low = dout.astype(jnp.bfloat16)
    grad_down = jnp.einsum("tf,td->fd", hidden, dout_low, preferred_element_type=jnp.float32)
    grad_hidden = jnp.einsum("td,fd->tf", dout_low, down_weight, preferred_element_type=jnp.float32)
    sigma = jax.nn.sigmoid(gate)
    grad_gate_act = (grad_hidden * upper * (sigma + gate * sigma * (1.0 - sigma))).astype(
        jnp.bfloat16
    )
    grad_up_act = (grad_hidden * (gate * sigma)).astype(jnp.bfloat16)
    grad_gate = jnp.einsum("te,tf->ef", mixed, grad_gate_act, preferred_element_type=jnp.float32)
    grad_up = jnp.einsum("te,tf->ef", mixed, grad_up_act, preferred_element_type=jnp.float32)
    grad_mixed = jnp.einsum(
        "tf,ef->te", grad_gate_act, gate_weight, preferred_element_type=jnp.float32
    ) + jnp.einsum("tf,ef->te", grad_up_act, up_weight, preferred_element_type=jnp.float32)
    grad_gain_two = jnp.sum(grad_mixed * normed_two, axis=0)
    scaled_two = grad_mixed * gain_two
    grad_res = dout + inv_two * (
        scaled_two - normed_two * jnp.mean(scaled_two * normed_two, axis=-1, keepdims=True)
    )
    grad_branch = grad_res.astype(jnp.bfloat16)
    grad_output = jnp.einsum("te,td->ed", attn_low, grad_branch, preferred_element_type=jnp.float32)
    attention_gradient = jnp.einsum(
        "td,ed->te", grad_branch, output_weight, preferred_element_type=jnp.float32
    )
    attention_gradient_reduced = attention_gradient.astype(jnp.bfloat16).reshape(
        token_rows, KEY_HEADS, query_groups, HEAD_SIZE
    )
    delta = jnp.einsum("tkgd,kgtd->kgt", attention_gradient_reduced.astype(jnp.float32), attn)
    key_rows_total, value_rows_total = (
        lax.all_gather(key_rows, "ctx", axis=0, tiled=True),
        lax.all_gather(value_rows, "ctx", axis=0, tiled=True),
    )
    token_length = key_rows_total.shape[0]
    block_size = min(512, token_length)

    def reverse_block_step(grad_query, block_tile):
        key_block, value_block, pblock, sblock = block_tile

        def reverse_work(current):
            key_head_rows = key_block.reshape(block_size, KEY_HEADS, HEAD_SIZE)
            value_head_rows = value_block.reshape(block_size, KEY_HEADS, HEAD_SIZE)
            scores = (
                jnp.einsum(
                    "tkgd,nkd->kgtn",
                    grouped_queries,
                    key_head_rows,
                    preferred_element_type=jnp.float32,
                )
                * scale
            )
            mask = allowed(pblock, sblock, positions, query_seg)[None, None]
            probs = jnp.where(mask, jnp.exp(scores - lse[..., None]), 0.0)
            grad_probs = jnp.einsum(
                "tkgd,nkd->kgtn",
                attention_gradient_reduced,
                value_head_rows,
                preferred_element_type=jnp.float32,
            )
            grad_scores = (probs * (grad_probs - delta[..., None])).astype(jnp.bfloat16)
            updated_state = current + jnp.einsum(
                "kgtn,nkd->tkgd", grad_scores, key_head_rows, preferred_element_type=jnp.float32
            )
            key_gradient_term = (
                jnp.einsum(
                    "kgtn,tkgd->nkd",
                    grad_scores,
                    grouped_queries,
                    preferred_element_type=jnp.float32,
                )
                * scale
            )
            value_gradient_term = jnp.einsum(
                "kgtn,tkgd->nkd",
                probs.astype(jnp.bfloat16),
                attention_gradient_reduced,
                preferred_element_type=jnp.float32,
            )
            return (
                updated_state,
                (
                    key_gradient_term.reshape(block_size, KEY_HEADS * HEAD_SIZE),
                    value_gradient_term.reshape(block_size, KEY_HEADS * HEAD_SIZE),
                ),
            )

        def reverse_leave(current):
            empty_state = jnp.zeros((block_size, KEY_HEADS * HEAD_SIZE), jnp.float32)
            return (current, (empty_state, empty_state))

        return lax.cond(pblock[0] <= positions[-1], reverse_work, reverse_leave, grad_query)

    places = jnp.arange(token_length, dtype=jnp.int32)
    block_tiles = (
        key_rows_total.reshape(-1, block_size, KEY_HEADS * HEAD_SIZE),
        value_rows_total.reshape(-1, block_size, KEY_HEADS * HEAD_SIZE),
        places.reshape(-1, block_size),
        seg_row.reshape(-1, block_size),
    )
    grad_query_rot, (key_gradient_terms, value_gradient_terms) = lax.scan(
        reverse_block_step,
        jnp.zeros((token_rows, KEY_HEADS, query_groups, HEAD_SIZE), jnp.float32),
        block_tiles,
    )
    key_gradient_rows, grad_values = (
        lax.psum_scatter(
            key_gradient_terms.reshape(token_length, KEY_HEADS * HEAD_SIZE),
            "ctx",
            scatter_dimension=0,
            tiled=True,
        ),
        lax.psum_scatter(
            value_gradient_terms.reshape(token_length, KEY_HEADS * HEAD_SIZE),
            "ctx",
            scatter_dimension=0,
            tiled=True,
        ),
    )
    grad_q_low = (
        rotary_apply(
            (grad_query_rot * scale).reshape(token_rows, QUERY_HEADS, HEAD_SIZE),
            cosine_table,
            sine_table,
            -1.0,
        )
        .astype(jnp.bfloat16)
        .reshape(token_rows, QUERY_HEADS * HEAD_SIZE)
    )
    grad_k_low = (
        rotary_apply(
            key_gradient_rows.reshape(token_rows, KEY_HEADS, HEAD_SIZE),
            cosine_table,
            sine_table,
            -1.0,
        )
        .astype(jnp.bfloat16)
        .reshape(token_rows, KEY_HEADS * HEAD_SIZE)
    )
    grad_v_low = grad_values.astype(jnp.bfloat16)
    grad_wq = jnp.einsum(
        "te,tf->ef", activated_hidden, grad_q_low, preferred_element_type=jnp.float32
    )
    grad_wk = jnp.einsum(
        "te,tf->ef", activated_hidden, grad_k_low, preferred_element_type=jnp.float32
    )
    grad_wv = jnp.einsum(
        "te,tf->ef", activated_hidden, grad_v_low, preferred_element_type=jnp.float32
    )
    grad_acted = jnp.einsum(
        "tf,ef->te", grad_q_low, query_weight, preferred_element_type=jnp.float32
    )
    grad_acted = grad_acted + jnp.einsum(
        "tf,ef->te", grad_k_low, key_weight, preferred_element_type=jnp.float32
    )
    grad_acted = grad_acted + jnp.einsum(
        "tf,ef->te", grad_v_low, value_weight, preferred_element_type=jnp.float32
    )
    grad_gain_one = jnp.sum(grad_acted * normed_one, axis=0)
    scaled_one = grad_acted * gain_one
    grad_input = grad_res + inv_one * (
        scaled_one - normed_one * jnp.mean(scaled_one * normed_one, axis=-1, keepdims=True)
    )
    terms = [
        grad_wq.reshape(-1),
        grad_wk.reshape(-1),
        grad_wv.reshape(-1),
        grad_output.reshape(-1),
        grad_gate.reshape(-1),
        grad_up.reshape(-1),
        grad_down.reshape(-1),
        jnp.concatenate([grad_gain_one, grad_gain_two]),
    ]
    return (grad_input.astype(jnp.bfloat16), terms)


def local(
    inputs,
    segments,
    query_weight,
    key_weight,
    value_weight,
    output_weight,
    gate_weight,
    up_weight,
    down_weight,
    norm_gain_pair,
    cotangent,
):
    shard_rows = inputs.shape[2]
    seg_full = lax.all_gather(segments, "ctx", axis=2, tiled=True)
    positions = lax.axis_index("ctx") * shard_rows + jnp.arange(shard_rows, dtype=jnp.int32)
    cosine_table, sine_table = rope_parts(positions)
    weight_matrices = shape_weights(
        (
            lax.all_gather(query_weight, ("grp", "ctx"), axis=0, tiled=True),
            lax.all_gather(key_weight, ("grp", "ctx"), axis=0, tiled=True),
            lax.all_gather(value_weight, ("grp", "ctx"), axis=0, tiled=True),
            lax.all_gather(output_weight, ("grp", "ctx"), axis=0, tiled=True),
            lax.all_gather(gate_weight, ("grp", "ctx"), axis=0, tiled=True),
            lax.all_gather(up_weight, ("grp", "ctx"), axis=0, tiled=True),
            lax.all_gather(down_weight, ("grp", "ctx"), axis=0, tiled=True),
            lax.all_gather(norm_gain_pair, ("grp", "ctx"), axis=0, tiled=True),
        )
    )
    results = []
    saved = []
    for micro_step in range(MICRO):
        xrow = inputs[micro_step, 0].astype(jnp.float32)
        result, kept = forward_rows(
            xrow,
            seg_full[micro_step, 0],
            segments[micro_step, 0],
            positions,
            cosine_table,
            sine_table,
            weight_matrices,
        )
        results.append(result.astype(jnp.bfloat16))
        saved.append(kept)
    mats_back = shape_weights(
        (
            lax.all_gather(query_weight, ("grp", "ctx"), axis=0, tiled=True),
            lax.all_gather(key_weight, ("grp", "ctx"), axis=0, tiled=True),
            lax.all_gather(value_weight, ("grp", "ctx"), axis=0, tiled=True),
            lax.all_gather(output_weight, ("grp", "ctx"), axis=0, tiled=True),
            lax.all_gather(gate_weight, ("grp", "ctx"), axis=0, tiled=True),
            lax.all_gather(up_weight, ("grp", "ctx"), axis=0, tiled=True),
            lax.all_gather(down_weight, ("grp", "ctx"), axis=0, tiled=True),
            lax.all_gather(norm_gain_pair, ("grp", "ctx"), axis=0, tiled=True),
        )
    )
    input_grads = []
    shares = None
    totals = None
    for micro_step in range(MICRO):
        dout = cotangent[micro_step, 0].astype(jnp.float32)
        grad_input, terms = backward_rows(
            dout,
            seg_full[micro_step, 0],
            segments[micro_step, 0],
            positions,
            cosine_table,
            sine_table,
            mats_back,
            saved[micro_step],
        )
        input_grads.append(grad_input)
        totals = terms if totals is None else [a + b for a, b in zip(totals, terms)]
    shares = list(
        (
            lax.psum_scatter(totals[0], ("grp", "ctx"), scatter_dimension=0, tiled=True),
            lax.psum_scatter(totals[1], ("grp", "ctx"), scatter_dimension=0, tiled=True),
            lax.psum_scatter(totals[2], ("grp", "ctx"), scatter_dimension=0, tiled=True),
            lax.psum_scatter(totals[3], ("grp", "ctx"), scatter_dimension=0, tiled=True),
            lax.psum_scatter(totals[4], ("grp", "ctx"), scatter_dimension=0, tiled=True),
            lax.psum_scatter(totals[5], ("grp", "ctx"), scatter_dimension=0, tiled=True),
            lax.psum_scatter(totals[6], ("grp", "ctx"), scatter_dimension=0, tiled=True),
            lax.psum_scatter(totals[7], ("grp", "ctx"), scatter_dimension=0, tiled=True),
        )
    )
    outputs = jnp.stack(results)[:, None]
    input_grad = jnp.stack(input_grads)[:, None]
    return (
        outputs,
        input_grad,
        shares[0],
        shares[1],
        shares[2],
        shares[3],
        shares[4],
        shares[5],
        shares[6],
        shares[7],
    )


W = MODEL_WIDTH
HG = QUERY_HEADS // KEY_HEADS * HEAD_SIZE
QK = HG + HEAD_SIZE
SLAB = 384
QKV = HG + 2 * HEAD_SIZE
OUT = W // 8
BACK = 512
FEED = 432
EDGE = 304
CHUNK = W // 32
HID = HIDDEN_UNITS // 8
SUB = HIDDEN_UNITS // 32
ROWS = 128
ALL = 8 * ROWS
POS = 64
LEN = 512
RELATIVE = (0, 2, 4, 6, 1, 3, 5, 7)
STEP = 512
STEPS = ALL // STEP
F32 = jnp.float32
BF16 = jnp.bfloat16
SCALE = HEAD_SIZE ** (-0.5)
NT = (((1,), (1,)), ((), ()))
TN = (((0,), (0,)), ((), ()))
MIB = 1024 * 1024
LARGE = ("attend", "project", "feed", "back")


def pc(value, k):
    return lax.ppermute(value, "ctx", [(s, s ^ k) for s in range(8)])


def pz(value, k):
    return lax.ppermute(value, "grp", [(s, s ^ k) for s in range(4)])


def after(value, *others):
    return lax.optimization_barrier((value,) + others)[0]


def first_ctx(value):
    far = pc(value, 6)
    return [value, pc(value, 2), pc(value, 4), far]


def both_cores(mine):
    return mine + [pc(m, 1) for m in mine]


def gather_ctx(value):
    return both_cores(first_ctx(value))


def gather_grp(value):
    one = pz(value, 1)
    two = pz(value, 2)
    return (value, one, two, pz(two, 1))


def add_low(a, b):
    return (a.astype(F32) + b.astype(F32)).astype(BF16)


class Order:
    def __init__(self):
        self.last = None

    def __call__(self, values):
        return values if self.last is None else after(values, self.last)

    def then(self, result):
        self.last = jax.tree.leaves(result)[-1]
        return result

    def wait(self, values):
        return self.then(self(values))


def scatter_ctx(even, got):
    return [add_low(even[k], got[k]) for k in range(4)]


def send_ctx(sums):
    far = pc(sums[3], 6)
    return sums[0], pc(sums[1], 2), pc(sums[2], 4), far


def pick(blocks, g):
    return [lax.dynamic_index_in_dim(blocks, g ^ k, 0, keepdims=False) for k in range(4)]


def call(body, outs, *args, grid=None, in_specs=None, out_specs=None, scratch=(), name=None):
    kwargs = {}
    if grid is not None:
        kwargs = dict(grid=grid, in_specs=in_specs, out_specs=out_specs)
    else:
        kwargs = dict(
            in_specs=[
                pl.BlockSpec(memory_space=pltpu.SMEM)
                if a.dtype == jnp.int32 and a.ndim == 1
                else pl.BlockSpec(memory_space=pltpu.VMEM)
                for a in args
            ],
            out_specs=out_specs or [pl.BlockSpec(memory_space=pltpu.VMEM) for _ in outs],
        )
    return pl.pallas_call(
        body,
        out_shape=outs,
        scratch_shapes=scratch,
        compiler_params=pltpu.CompilerParams(vmem_limit_bytes=(32 if name in LARGE else 16) * MIB),
        cost_estimate=pl.CostEstimate(flops=0, bytes_accessed=1, transcendentals=0),
        name=name,
        **kwargs,
    )(*args)


def late(values):
    return [pltpu.with_memory_space_constraint(v, pltpu.HBM) for v in values]


def hbm(shape, dtype):
    return pltpu.HBM(shape, dtype)


def hbm(shape, dtype):
    return pltpu.HBM(shape, dtype)


def hbm(shape, dtype):
    return pltpu.HBM(shape, dtype)


def sds(shape, dtype):
    return jax.ShapeDtypeStruct(shape, dtype)


def rows_of(ref, count):
    wide = ref.shape[0] // count
    return jnp.concatenate([ref[pl.ds(n, count, stride=wide), :] for n in range(wide)], 1)


def store_rows(ref, rows):
    count = rows.shape[0]
    wide = ref.shape[0] // count
    for n in range(wide):
        ref[pl.ds(n, count, stride=wide), :] = rows[:, n * 128 : (n + 1) * 128]


def pack_body(q_r, k_r, v_r, gate_r, up_r, gain, out, sq, sk, sv, sg, su):
    for src, dst in ((q_r, sq), (k_r, sk), (v_r, sv), (gate_r, sg), (up_r, su)):
        dst[...] = src[...].astype(F32)
    q, k, v, gate, up = (rows_of(s, CHUNK) for s in (sq, sk, sv, sg, su))
    tail = jnp.concatenate([gain[:, n * SLAB : (n + 1) * SLAB] for n in range(3)], 0).astype(F32)
    tail = jnp.concatenate([tail, jnp.zeros((1, SLAB), F32)], 0)
    for h in range(8):
        if h < KEY_HEADS:
            rows = jnp.concatenate(
                [
                    q[:, h * HG : (h + 1) * HG],
                    k[:, h * HEAD_SIZE : (h + 1) * HEAD_SIZE],
                    v[:, h * HEAD_SIZE : (h + 1) * HEAD_SIZE],
                    jnp.zeros((CHUNK, SLAB - QKV), F32),
                ],
                1,
            )
        else:
            rows = jnp.zeros((CHUNK, SLAB), F32)
        out[h, :, :SLAB] = jnp.concatenate([rows, tail], 0).astype(BF16)
        parts = [
            full[:, z * 768 + h * SUB : z * 768 + (h + 1) * SUB] for full in (gate, up) for z in range(4)
        ]
        rows = jnp.concatenate([jnp.concatenate(parts, 1), jnp.zeros((4, 2 * HID), F32)], 0)
        out[h, :, SLAB:] = rows.astype(BF16)


def unpack_body(src, slab, feed):
    for h in range(8):
        slab[h] = src[h, :, :SLAB]
    feed[...] = jnp.concatenate([src[h, :CHUNK, SLAB:].astype(F32) for h in range(8)], 0).astype(BF16)


def join_body(*refs):
    for n, block in enumerate(refs[:8]):
        refs[8][n * ROWS : (n + 1) * ROWS, :] = block[...]


def join(blocks):
    return call(join_body, [sds((ALL, W), BF16)], *blocks, name="join")[0]


def output_weight_body(sc, b0, b1, b2, b3, b4, b5, b6, b7, out, rows):
    i, g = sc[0], sc[1]
    for j, b in zip(RELATIVE, (b0, b1, b2, b3, b4, b5, b6, b7)):
        for k in range(4):
            rows[i ^ j, g ^ k] = b[k].astype(F32)
    for z in range(4):
        for q in range(2):
            parts = [rows_of(rows.at[c, z], CHUNK) for c in range(4 * q, 4 * q + 4)]
            start = z * 288 + q * 144
            out[start : start + 144, :] = jnp.concatenate(parts, 0).astype(BF16)


def rotate(x, cosine, sine, sign):
    lane = lax.broadcasted_iota(jnp.int32, (1, 128), 1) % HEAD_SIZE
    first = lane < HEAD_SIZE // 2
    halves = []
    for n in range(x.shape[1] // 128):
        part = x[:, n * 128 : (n + 1) * 128]
        swapped = jnp.where(first, pltpu.roll(part, 96, 1), pltpu.roll(part, 32, 1))
        halves.append(part * cosine + sign * (swapped * sine))
    return jnp.concatenate(halves, 1)


def attend_body(
    sc, x0, x1, x2, x3, x4, x5, x6, x7, w0, w1, w2, w3, cosine, sine, pcol, prow,
    att, gains, w_o, qk_h, v_h, acted_h, probs_h, x_h, qk_o, v_o, acted, probs, x_o, segs, held, sems,
):
    xs = (x0, x1, x2, x3, x4, x5, x6, x7)
    g = sc[1]
    copies = []

    def send(src, dst):
        copy = pltpu.make_async_copy(src, dst, sems.at[len(copies)])
        copy.start()
        copies.append(copy)

    sums = [jnp.zeros((3, SLAB), F32), jnp.zeros((3, SLAB), F32)]
    for k, w in enumerate((w0, w1, w2, w3)):
        z = g ^ k
        block = jnp.concatenate([w[h, :CHUNK, :].astype(F32) for h in range(8)], 0)
        w_o[pl.ds(pl.multiple_of(z * 288, 32), 288), :] = block.astype(BF16)
        rows = sum(w[h, CHUNK : CHUNK + 3, :].astype(F32) for h in range(8))
        sums[0] = sums[0] + jnp.where(z < 2, rows, 0.0)
        sums[1] = sums[1] + jnp.where(z < 2, 0.0, rows)
    gain = [jnp.concatenate([s[0:1], s[1:2], s[2:3]], 1) for s in sums]
    gains[...] = jnp.concatenate([gain[0], gain[1], jnp.zeros((6, W), F32)], 0)
    for b in range(8):
        x_o[b * ROWS : (b + 1) * ROWS, :] = xs[b][:, :W]
        segs[b] = xs[b][:, W:]

    @pl.loop(0, 8)
    def _(b):
        at = pl.ds(pl.multiple_of(b * ROWS, ROWS), ROWS)
        x = x_o[at, :].astype(F32)
        inv = lax.rsqrt(jnp.mean(x * x, axis=-1, keepdims=True) + EPS)
        acted[at, :] = (x * inv * gain[0]).astype(BF16)

    send(x_o, x_h)
    send(acted, acted_h)

    @pl.loop(0, MICRO)
    def _(m):
        part = pl.ds(pl.multiple_of(m * POS, POS), POS)
        rows = jnp.concatenate(
            [acted[pl.ds(pl.multiple_of(b * ROWS + m * POS, POS), POS), :] for b in range(8)], 0
        )
        seg = jnp.concatenate([segs[b, part, :].astype(F32) for b in range(8)], 0)
        y = jnp.dot(rows, w_o[...], preferred_element_type=F32)
        qk = rotate(y[:, :QK], cosine[...], sine[...], 1.0).astype(BF16)
        v = y[:, QK:].astype(BF16)
        qk_o[m] = qk
        v_o[m] = v
        seg_row = jnp.transpose(seg)[0:1, :]
        mask = (prow[0:1, :] <= pcol[:, 0:1]) & (seg_row == seg[:, 0:1])
        bias = jnp.where(mask, 0.0, NEGATIVE_LARGE)
        keys = qk[:, HG:]
        for h in range(3):
            s = lax.dot_general(
                qk[:, h * HEAD_SIZE : (h + 1) * HEAD_SIZE], keys, NT, preferred_element_type=F32
            )
            s = s * SCALE + bias
            e = jnp.exp(s - jnp.max(s, axis=-1, keepdims=True))
            p = (e * (1.0 / jnp.sum(e, axis=-1, keepdims=True))).astype(BF16)
            probs[m, h] = p
            held[m, :, h * HEAD_SIZE : (h + 1) * HEAD_SIZE] = jnp.dot(
                p, v[:, :HEAD_SIZE], preferred_element_type=F32
            ).astype(BF16)

    for m in range(MICRO):
        att[:, m * HG : (m + 1) * HG] = held[m]
    send(probs, probs_h)
    send(qk_o, qk_h)
    send(v_o, v_h)
    for copy in copies:
        copy.wait()


def project_body(sc, x, a0, a1, a2, a3, a4, a5, a6, a7, wo, gains, att_o, mixed_o, res_o, heads):
    i = sc[0]
    t = pl.program_id(0)
    for j, a in zip(RELATIVE, (a0, a1, a2, a3, a4, a5, a6, a7)):
        h = i ^ j
        for half in range(STEP // ROWS):
            b = STEP // ROWS * t + half
            q = (2 * (b & 3) + (b >> 2)) ^ j
            start = pl.multiple_of(((q & 1) * 4 + (q >> 1)) * POS, POS)
            rows = a[pl.ds(start, POS), :]
            for m in range(MICRO):
                heads[h, half * ROWS + m * POS : half * ROWS + (m + 1) * POS, :] = rows[:, m * HG : (m + 1) * HG]
    for h in range(KEY_HEADS):
        att_o[:, h * HG : (h + 1) * HG] = heads[h]
    residual = x[...].astype(F32) + jnp.dot(att_o[...], wo[...], preferred_element_type=F32)

    @pl.when(t == 0)
    def _():
        res_o[...] = residual[:ROWS]

    inv = lax.rsqrt(jnp.mean(residual * residual, axis=-1, keepdims=True) + EPS)
    mixed_o[...] = (residual * inv * gains[1:2, :]).astype(BF16)


def feed_body(
    sc, mixed_r, c, g0, g1, g2, g3, d0, d1, d2, d3, hidden_o, dgu_o, pm, pe, dn, sums, gu
):
    g = sc[1]
    t = pl.program_id(0)

    @pl.when(t == 0)
    def _():
        for k, (a, d) in enumerate(((g0, d0), (g1, d1), (g2, d2), (g3, d3))):
            z = g ^ k
            gu[pl.ds(pl.multiple_of(z * 288, 32), 288), :] = a[...]
            dn[pl.ds(pl.multiple_of(z * SUB, 32), SUB), :] = d[...]
        sums[...] = jnp.zeros((8, W), F32)

    mixed = mixed_r[...]
    y = jnp.dot(mixed, gu[...], preferred_element_type=F32)
    gate = y[:, :HID]
    up = y[:, HID:]
    sig = 1.0 / (1.0 + jnp.exp(-gate))
    silu = gate * sig
    hidden_o[...] = (silu * up).astype(BF16)
    dh = lax.dot_general(c[...], dn[...], NT, preferred_element_type=F32)
    dgate = (dh * up * (sig + silu * (1.0 - sig))).astype(BF16)
    dup = (dh * silu).astype(BF16)
    dgu = jnp.concatenate([dgate, dup], 1)
    dgu_o[...] = dgu
    dm = lax.dot_general(dgu, gu[...], NT, preferred_element_type=F32)
    sums[0:1, :] = sums[0:1, :] + jnp.sum(dm * mixed.astype(F32), axis=0, keepdims=True)
    dm = dm.astype(BF16).reshape(4, ROWS, W)

    @pl.when(t == 0)
    def _():
        pm[...] = dm

    @pl.when(t == 1)
    def _():
        pe[...] = dm


def whole(*shape):
    return pl.BlockSpec(shape, lambda t: (0,) * len(shape))


def rows_at(rows, columns):
    return pl.BlockSpec((rows, columns), lambda t: (t, 0))


def run_project(sc, x, heads, w_out, gains):
    return call(
        project_body,
        [hbm((ALL, W), BF16), sds((ALL, W), BF16), hbm((ROWS, W), F32)],
        sc, x, *heads, w_out, gains,
        grid=(STEPS,),
        in_specs=[pl.BlockSpec(memory_space=pltpu.SMEM), rows_at(STEP, W)]
        + [whole(LEN, 2 * HG)] * 8
        + [whole(W, W), whole(8, W)],
        out_specs=[rows_at(STEP, W), rows_at(STEP, W), whole(ROWS, W)],
        scratch=[pltpu.VMEM((8, STEP, HG), BF16)], name="project",
    )


def run_feed(sc, mixed, c, feeds):
    return call(
        feed_body,
        [
            sds((ALL, HID), BF16),
            sds((ALL, 2 * HID), BF16),
            sds((4, ROWS, W), BF16),
            sds((4, ROWS, W), BF16),
            sds((HID, W), BF16),
            sds((8, W), F32),
        ],
        sc, mixed, c, *feeds,
        grid=(STEPS,),
        in_specs=[pl.BlockSpec(memory_space=pltpu.SMEM), rows_at(STEP, W), rows_at(STEP, W)]
        + [whole(288, 2 * HID)] * 4
        + [whole(SUB, W)] * 4,
        out_specs=[
            rows_at(STEP, HID),
            rows_at(STEP, 2 * HID),
            whole(4, ROWS, W),
            whole(4, ROWS, W),
            whole(HID, W),
            whole(8, W),
        ],
        scratch=[pltpu.VMEM((W, 2 * HID), BF16)], name="feed",
    )


def mid_body(a, b, d, f, c, res, gains, dres, low):
    dm = a[...].astype(F32) + b[...].astype(F32) + d[...].astype(F32) + f[...].astype(F32)
    r = res[...]
    inv = lax.rsqrt(jnp.mean(r * r, axis=-1, keepdims=True) + EPS)
    n = r * inv
    e = dm * gains[1:2, :]
    out = c[...].astype(F32) + inv * (e - n * jnp.mean(e * n, axis=-1, keepdims=True))
    dres[...] = out
    low[...] = out.astype(BF16)


def last_body(a, b, d, f, x, dres, gains, out):
    da = a[...].astype(F32) + b[...].astype(F32) + d[...].astype(F32) + f[...].astype(F32)
    r = x[...].astype(F32)
    inv = lax.rsqrt(jnp.mean(r * r, axis=-1, keepdims=True) + EPS)
    n = r * inv
    e = da * gains[0:1, :]
    out[...] = (dres[...] + inv * (e - n * jnp.mean(e * n, axis=-1, keepdims=True))).astype(BF16)


def back_body(
    sc, l0, l1, l2, l3, l4, l5, l6, l7, wo, qk_r, v_r, probs, cosine, sine, acted_t, att_t, w_slab, gains, sums,
    out, b0, b1, b2, b3, columns, dots, edge,
):
    lows = (l0, l1, l2, l3, l4, l5, l6, l7)
    i, g = sc[0], sc[1]
    place = lax.broadcasted_iota(jnp.int32, (256, W), 1) - lax.broadcasted_iota(jnp.int32, (256, W), 0)
    chosen = jnp.where(place == i * OUT, 1.0, 0.0).astype(BF16)
    @pl.loop(0, MICRO)
    def _(m):
        part = pl.ds(pl.multiple_of(m * POS, POS), POS)
        rows = jnp.concatenate([lows[b][part, :] for b in range(8)], 0)
        datt = lax.dot_general(rows, wo[...], NT, preferred_element_type=F32).astype(BF16)
        chosen_rows = lax.dot_general(rows, chosen, NT, preferred_element_type=F32).astype(BF16)
        qk = qk_r[m]
        keys = qk[:, HG:]
        v = v_r[m][:, :HEAD_SIZE]
        dq = []
        dk = jnp.zeros((HEAD_SIZE, LEN), F32)
        dv = jnp.zeros((HEAD_SIZE, LEN), F32)
        for h in range(3):
            da = datt[:, h * HEAD_SIZE : (h + 1) * HEAD_SIZE]
            q = qk[:, h * HEAD_SIZE : (h + 1) * HEAD_SIZE]
            low = probs[m, h]
            p = low.astype(F32)
            dp = lax.dot_general(da, v, NT, preferred_element_type=F32)
            delta = jnp.sum(p * dp, axis=-1, keepdims=True)
            ds = (p * (dp - delta)).astype(BF16)
            dq.append(jnp.dot(ds, keys, preferred_element_type=F32))
            dk = dk + lax.dot_general(q, ds, TN, preferred_element_type=F32)
            dv = dv + lax.dot_general(da, low, TN, preferred_element_type=F32)
        dqk = jnp.concatenate(dq + [jnp.transpose(dk)], 1) * SCALE
        dqk = rotate(dqk, cosine[...], sine[...], -1.0)
        dvt = jnp.transpose(jnp.concatenate([dv, jnp.zeros((HEAD_SIZE, LEN), F32)], 0))
        full = jnp.concatenate([dqk, dvt], 1).astype(BF16)
        for b in range(8):
            at = pl.ds(pl.multiple_of(b * ROWS + m * POS, POS), POS)
            out[at, :] = full[b * POS : (b + 1) * POS, :]
            columns[at, :] = chosen_rows[b * POS : (b + 1) * POS, :]

    blocks = (b0, b1, b2, b3)
    for k in range(4):
        z = g ^ k
        start = pl.multiple_of(z * 288, 32)
        y = jnp.dot(acted_t[pl.ds(start, 288), :], out[...], preferred_element_type=F32)
        yo = jnp.dot(att_t[pl.ds(start, 288), :], columns[...], preferred_element_type=F32)
        y2 = jnp.concatenate([y[:, :QKV], yo[:, : BACK - QKV]], 1)
        blocks[k][:288, :] = y2.astype(BF16)
        dot = jnp.sum(y * w_slab[pl.ds(start, 288), :].astype(F32), axis=-1, keepdims=True)
        dots[z] = jnp.transpose(jnp.broadcast_to(dot, (288, 128)))[:8, :]
    one = jnp.concatenate([dots[z][0:1, :] for z in range(4)], 1) / gains[0:1, :]
    two = sums[0:1, :] / gains[1:2, :]
    for z in range(4):
        full = one if z < 2 else two
        at = (z % 2) * 576
        rows = jnp.concatenate([full[:, at + 72 * c : at + 72 * (c + 1)] for c in range(8)], 0)
        rows = jnp.concatenate([rows, jnp.zeros((8, BACK - 72), F32)], 1)
        edge[z] = jnp.concatenate([rows, jnp.zeros((EDGE - 288 - 8, BACK), F32)], 0)
    for k in range(4):
        blocks[k][288:, :] = edge[g ^ k].astype(BF16)


def split_back_body(a, b, d, out):
    rows = a[...].astype(F32) + b[...].astype(F32) + d[...].astype(F32)
    for h in range(8):
        block = [rows[h * CHUNK : (h + 1) * CHUNK, :], rows[288 + h : 289 + h, :], jnp.zeros((3, BACK), F32)]
        out[h] = jnp.concatenate(block, 0).astype(BF16)


def grads_body(sc, grad_gu, grad_dn, b0, b1, b2, b3):
    g = sc[1]
    for k, block in enumerate((b0, b1, b2, b3)):
        z = g ^ k
        block[:288, :] = grad_gu[pl.ds(pl.multiple_of(z * 288, 32), 288), :]
        start = pl.multiple_of(z * SUB, 32)
        block[288 : 288 + SUB, :] = grad_dn[pl.ds(start, SUB), :768]
        block[288 + SUB :, :HID] = grad_dn[pl.ds(start, SUB // 2), 768:]
        block[288 + SUB :, HID:] = grad_dn[pl.ds(pl.multiple_of(start + SUB // 2, 16), SUB // 2), 768:]


def transpose_body(src, out):
    for n in range(ALL // 256):
        for m in range(W // 384):
            block = src[n * 256 : (n + 1) * 256, m * 384 : (m + 1) * 384]
            out[m * 384 : (m + 1) * 384, n * 256 : (n + 1) * 256] = jnp.transpose(block)


def transpose(value):
    return call(transpose_body, [sds((W, ALL), BF16)], value, name="transpose")[0]


def onward_body(rows, weight, even, odd):
    dims = NT if weight.shape[0] == W else (((1,), (0,)), ((), ()))
    for n in range(4):
        part = rows[n * 2 * ROWS : (n + 1) * 2 * ROWS, :]
        y = lax.dot_general(part, weight[...], dims, preferred_element_type=F32).astype(BF16)
        out = even if n < 2 else odd
        out[2 * (n % 2)] = y[:ROWS]
        out[2 * (n % 2) + 1] = y[ROWS:]


def onward(rows, weight, name):
    return call(onward_body, [sds((4, ROWS, W), BF16)] * 2, rows, weight, name=name)


def split_feed_body(a, b, d, out, down):
    rows = a[...].astype(F32) + b[...].astype(F32) + d[...].astype(F32)
    for h in range(8):
        out[h] = rows[h * CHUNK : (h + 1) * CHUNK, :].astype(BF16)
    right = jnp.concatenate([rows[288 + SUB :, :HID], rows[288 + SUB :, HID:]], 0)
    store_rows(down, jnp.concatenate([rows[288 : 288 + SUB, :], right], 1))


def split_back_body(a, b, d, out):
    rows = a[...].astype(F32) + b[...].astype(F32) + d[...].astype(F32)
    for h in range(8):
        block = [rows[h * CHUNK : (h + 1) * CHUNK, :], rows[288 + h : 289 + h, :], jnp.zeros((3, BACK), F32)]
        out[h] = jnp.concatenate(block, 0).astype(BF16)


def unpack_back_body(src, q, k, v, o, gains):
    parts = [src[h].astype(F32) for h in range(8)]
    rows = [p[:CHUNK, :] for p in parts]
    store_rows(q, jnp.concatenate([p[:, :HG] for p in rows[:KEY_HEADS]], 1))
    store_rows(k, jnp.concatenate([p[:, HG:QK] for p in rows[:KEY_HEADS]], 1))
    store_rows(v, jnp.concatenate([p[:, QK:QKV] for p in rows[:KEY_HEADS]], 1))
    store_rows(o, jnp.concatenate([p[:, QKV : QKV + OUT] for p in rows], 1))
    gains[...] = jnp.broadcast_to(sum(p[CHUNK : CHUNK + 1, :128] for p in parts), (8, 128))


def unpack_hidden_body(src, gate, up):
    for n, out in enumerate((gate, up)):
        parts = [
            src[h, :, n * HID + z * SUB : n * HID + (z + 1) * SUB].astype(F32)
            for z in range(4)
            for h in range(8)
        ]
        store_rows(out, jnp.concatenate(parts, 1))


def fast_local(inputs, segments, wq, wk, wv, wo, wg, wu, wd, gain_pair, cotangent):
    i = lax.axis_index("ctx").astype(jnp.int32)
    g = lax.axis_index("grp").astype(jnp.int32)
    r = g * 8 + i
    sc = jnp.stack([i, g])
    x_own = inputs.reshape(ROWS, W)
    c_own = cotangent.reshape(ROWS, W)
    order = Order()

    q2, k2, v2, gate2, up2 = (w.reshape(-1, 128) for w in (wq, wk, wv, wg, wu))
    placed = lax.dynamic_update_slice(jnp.zeros((1, W), BF16), gain_pair[None, :], (0, (r % 16) * 72))
    packed = order.then(
        call(
            pack_body,
            [sds((8, 40, SLAB + 2 * HID), BF16)],
            *late([q2, k2, v2, gate2, up2]), placed,
            scratch=[pltpu.VMEM(a.shape, F32) for a in (q2, k2, v2, gate2, up2)], name="pack",
        )
    )[0]
    packed = lax.all_to_all(packed, "ctx", 0, 0, tiled=True)

    x_late, seg_late, wo, wd, i_late, c_late = order((x_own, segments, wo, wd, i, c_own))
    o_own = wo.reshape(-1, 128)
    o_one, o_two = pz(o_own, 1), pz(o_own, 2)
    c_near = pc(c_late, 2), pc(c_late, 4)
    seg = jnp.broadcast_to(seg_late.reshape(ROWS, 1).astype(BF16), (ROWS, 128))
    x_sent = order.then(jnp.concatenate([x_late, seg], 1))
    d_own = order.then(order(wd).reshape(SUB, W))
    packed, o_one, o_two = order.wait((packed, o_one, o_two))

    slab, feed = order.then(
        call(unpack_body, [sds((8, 40, SLAB), BF16), sds((288, 2 * HID), BF16)], packed, name="unpack")
    )
    s_one, s_two = pz(slab, 1), pz(slab, 2)
    xs = first_ctx(order(x_sent))

    i_late = order(i_late)
    rel = jnp.array(RELATIVE, jnp.int32)
    positions = ((i_late ^ rel)[:, None] * POS + jnp.arange(POS, dtype=jnp.int32)[None, :]).reshape(LEN)
    half = HEAD_SIZE // 2
    freq = THETA ** (-jnp.arange(half, dtype=F32) * 2.0 / HEAD_SIZE)
    angle = positions.astype(F32)[:, None] * freq[None, :]
    cosine = jnp.tile(jnp.cos(angle), (1, 4))
    sine = jnp.sin(angle)
    sine = jnp.concatenate([-sine, sine, -sine, sine], 1)
    pcol = jnp.broadcast_to(positions.astype(F32)[:, None], (LEN, 128))
    prow = jnp.broadcast_to(positions.astype(F32)[None, :], (8, LEN))
    cosine, sine, pcol, prow = order.then((cosine, sine, pcol, prow))

    c_near = order.wait(c_near)
    s_one = order.wait(s_one)
    o_three = pz(order(o_two), 1)
    s_two = order.wait(s_two)
    s_three = pz(s_two, 1)
    o_three = order.wait(o_three)
    o_sent = order.then(jnp.stack([o_own, o_one, o_two, o_three]))
    g_one, g_two = pz(order(feed), 1), pz(order(feed), 2)
    s_three = order.wait(s_three)
    os = first_ctx(order(o_sent))
    xs = order.wait(both_cores(order.wait(xs)))
    xs, slabs = order((xs, (slab, s_one, s_two, s_three)))

    anywhere = pl.BlockSpec(memory_space=pl.ANY)
    vmem = pl.BlockSpec(memory_space=pltpu.VMEM)
    held = [
        sds((MICRO, LEN, QK), BF16),
        sds((MICRO, LEN, 128), BF16),
        sds((ALL, W), BF16),
        sds((MICRO, 3, LEN, LEN), BF16),
        sds((ALL, W), BF16),
    ]
    att, gains, w_slab, qk, v, acted, probs, call_x = order.then(
        call(
            attend_body,
            [sds((LEN, 2 * HG), BF16), sds((8, W), F32), sds((W, SLAB), BF16)]
            + [hbm(o.shape, o.dtype) for o in held],
            sc, *late(xs), *late(slabs), cosine, sine, pcol, prow,
            out_specs=[vmem] * 3 + [anywhere] * 5,
            scratch=[pltpu.VMEM(o.shape, o.dtype) for o in held]
            + [pltpu.VMEM((8, ROWS, 128), BF16), pltpu.VMEM((MICRO, LEN, HG), BF16), pltpu.SemaphoreType.DMA((5,))],
            name="attend",
        )
    )
    att, g_one, g_two = order.wait((att, g_one, g_two))
    heads = first_ctx(att)
    os = order.wait(both_cores(order.wait(os)))
    w_out = order.then(
        call(
            output_weight_body, [sds((W, W), BF16)], sc, *late(os),
            scratch=[pltpu.VMEM((8, 4, wo.size // 128, 128), F32)], name="output_weight",
        )
    )[0]
    g_three = pz(order(g_two), 1)
    d_one, d_two = pz(order(d_own), 1), pz(order(d_own), 2)
    acted_t = order.then(transpose(order(acted)))
    d_one, d_two = order.wait((d_one, d_two))
    d_three = pz(d_two, 1)
    heads[1], heads[2] = order.wait((heads[1], heads[2]))
    heads = order.wait(both_cores(order.wait(heads)))
    cs = [c_late, *c_near, pc(order(c_late), 6)]
    g_three, d_three = order.wait((g_three, d_three))

    att_full, mixed, res_own = order.then(run_project(sc, call_x, late(heads), w_out, gains))
    wo_own = order.then(lax.dynamic_slice(order(w_out), (jnp.minimum(i, KEY_HEADS - 1) * HG, 0), (HG, W)))
    call_c = order.then(join(late(order(both_cores(order.wait(cs))))))
    feeds = order((feed, g_one, g_two, g_three, d_own, d_one, d_two, d_three))
    hidden, dgu, pm, pe, down, dots_two = order.then(run_feed(sc, mixed, call_c, late(feeds)))

    got = pc(pe, 1)
    grad_gu = order.then(lax.dot_general(order(mixed), dgu, TN, preferred_element_type=F32).astype(BF16))
    terms = send_ctx(order.then(scatter_ctx(pm, order(got))))
    grad_dn = order.then(lax.dot_general(order(hidden), call_c, TN, preferred_element_type=F32).astype(BF16))
    feed_blocks = order.then(
        call(grads_body, [hbm((FEED, 2 * HID), BF16)] * 4, sc, grad_gu, grad_dn, name="grads")
    )
    feed_far = pz(feed_blocks[3], 1)
    att_t = order.then(transpose(order(att_full)))
    dres, low = order.then(
        call(
            mid_body, [hbm((ROWS, W), F32), hbm((ROWS, W), BF16)],
            *late([*order(terms), c_own, res_own]), gains, name="mid",
        )
    )
    lows = first_ctx(low)
    feed_mid = order.then(add_low(feed_blocks[2], order(feed_far)))
    feed_terms = (feed_blocks[0], pz(after(feed_blocks[1], feed_mid), 1), pz(feed_mid, 2))

    om_p, oe_p = order.then(onward(order(hidden), down, "outward"))
    out_got = pc(oe_p, 1)
    out_terms = send_ctx(order.then(scatter_ctx(om_p, order(out_got))))
    lows = both_cores(order(lows))

    dqkv, *slab_blocks = order.then(
        call(
            back_body,
            [sds((ALL, SLAB), BF16)] + [sds((EDGE, BACK), BF16)] * 4,
            sc, *late(order(lows)), wo_own, qk, v, probs, cosine, sine, acted_t, att_t, w_slab, gains, dots_two,
            scratch=[
                pltpu.VMEM((ALL, 256), BF16),
                pltpu.VMEM((4, 8, 288), F32),
                pltpu.VMEM((4, EDGE - 288, BACK), F32),
            ],
            name="back",
        )
    )
    slab_far = pz(slab_blocks[3], 1)
    hid_sum, grad_down = order.then(
        call(
            split_feed_body, [sds((8, CHUNK, 2 * HID), BF16), sds((864, 128), F32)],
            *late(order(feed_terms)), name="split_feed",
        )
    )
    hid_sum = lax.all_to_all(hid_sum, "ctx", 0, 0, tiled=True)
    dam, dae = order.then(onward(order(dqkv), w_slab, "inward"))
    in_got = pc(dae, 1)
    slab_mid = order.then(add_low(slab_blocks[2], order(slab_far)))
    slab_terms = (slab_blocks[0], pz(after(slab_blocks[1], slab_mid), 1), pz(slab_mid, 2))
    in_terms = send_ctx(order.then(scatter_ctx(dam, order(in_got))))

    outputs = order.then((res_own + sum(t.astype(F32) for t in order(out_terms))).astype(BF16))
    grad_gate, grad_up = order.then(
        call(unpack_hidden_body, [sds((864, 128), F32), sds((864, 128), F32)], order(hid_sum), name="unpack_hidden")
    )
    slab = order.then(call(split_back_body, [sds((8, 40, BACK), BF16)], *late(order(slab_terms)), name="split_back"))[0]
    slab = lax.all_to_all(slab, "ctx", 0, 0, tiled=True)
    input_grad = order.then(
        call(last_body, [sds((ROWS, W), BF16)], *late([*order(in_terms), x_own, dres]), gains, name="last")
    )[0]
    grad_q, grad_k, grad_v, grad_out, grad_gains = call(
        unpack_back_body,
        [sds((324, 128), F32), sds((108, 128), F32), sds((108, 128), F32), sds((324, 128), F32), sds((8, 128), F32)],
        order(slab), name="unpack_back",
    )
    grad_gains = grad_gains[0, :72]

    shape = (MICRO, 1, POS, W)
    return (
        outputs.reshape(shape),
        input_grad.reshape(shape),
        grad_q.reshape(-1),
        grad_k.reshape(-1),
        grad_v.reshape(-1),
        grad_out.reshape(-1),
        grad_gate.reshape(-1),
        grad_up.reshape(-1),
        grad_down.reshape(-1),
        grad_gains,
    )


def solution(mesh):
    in_specs = (
        P(None, "grp", "ctx", None),
        P(None, "grp", "ctx"),
        P(("grp", "ctx")),
        P(("grp", "ctx")),
        P(("grp", "ctx")),
        P(("grp", "ctx")),
        P(("grp", "ctx")),
        P(("grp", "ctx")),
        P(("grp", "ctx")),
        P(("grp", "ctx")),
        P(None, "grp", "ctx", None),
    )
    out_specs = (
        P(None, "grp", "ctx", None),
        P(None, "grp", "ctx", None),
        P(("grp", "ctx")),
        P(("grp", "ctx")),
        P(("grp", "ctx")),
        P(("grp", "ctx")),
        P(("grp", "ctx")),
        P(("grp", "ctx")),
        P(("grp", "ctx")),
        P(("grp", "ctx")),
    )
    fits = (mesh.shape["ctx"], mesh.shape["grp"]) == (8, 4)
    return jax.shard_map(
        fast_local if fits else local,
        mesh=mesh,
        in_specs=in_specs,
        out_specs=out_specs,
        check_vma=False,
    )
```

```python
import jax
import jax.numpy as jnp
from jax import lax
from jax.experimental import pallas as pl
from jax.experimental.pallas import tpu as pltpu
from jax.sharding import PartitionSpec as P

MODEL_WIDTH = 1152
QUERY_HEADS = 18
KEY_HEADS = 6
HEAD_SIZE = 64
HIDDEN_UNITS = 3072
MICRO = 2


EPS = 1e-05
THETA = 10000.0
NEGATIVE_LARGE = -1e30


def rope_parts(positions):
    half = HEAD_SIZE // 2
    freq = THETA ** (-jnp.arange(half, dtype=jnp.float32) * 2.0 / HEAD_SIZE)
    angle = positions.astype(jnp.float32)[:, None] * freq[None, :]
    return (jnp.cos(angle)[:, None, :], jnp.sin(angle)[:, None, :])


def rotary_apply(value_rows, cosine_table, sine_table, sign):
    half = value_rows.shape[-1] // 2
    first = value_rows[..., :half]
    second = value_rows[..., half:]
    return jnp.concatenate(
        [
            first * cosine_table - sign * second * sine_table,
            second * cosine_table + sign * first * sine_table,
        ],
        -1,
    )


def shape_weights(full_precision):
    return (
        full_precision[0].reshape(MODEL_WIDTH, QUERY_HEADS * HEAD_SIZE),
        full_precision[1].reshape(MODEL_WIDTH, KEY_HEADS * HEAD_SIZE),
        full_precision[2].reshape(MODEL_WIDTH, KEY_HEADS * HEAD_SIZE),
        full_precision[3].reshape(QUERY_HEADS * HEAD_SIZE, MODEL_WIDTH),
        full_precision[4].reshape(MODEL_WIDTH, HIDDEN_UNITS),
        full_precision[5].reshape(MODEL_WIDTH, HIDDEN_UNITS),
        full_precision[6].reshape(HIDDEN_UNITS, MODEL_WIDTH),
        full_precision[7],
    )


def allowed(key_pos, key_seg, query_pos, query_seg):
    return (key_pos[None, :] <= query_pos[:, None]) & (key_seg[None, :] == query_seg[:, None])


def online_step(
    state, grouped_queries, key_block, value_block, pblock, sblock, query_pos, query_seg
):
    best, total, accum = state
    block_span = key_block.shape[0]
    key_head_rows = key_block.reshape(block_span, KEY_HEADS, HEAD_SIZE)
    value_head_rows = value_block.reshape(block_span, KEY_HEADS, HEAD_SIZE)
    scores = jnp.einsum(
        "tkgd,nkd->kgtn", grouped_queries, key_head_rows, preferred_element_type=jnp.float32
    ) * HEAD_SIZE ** (-0.5)
    mask = allowed(pblock, sblock, query_pos, query_seg)[None, None]
    scores = jnp.where(mask, scores, NEGATIVE_LARGE)
    new_best = jnp.maximum(best, jnp.max(scores, axis=-1))
    factor = jnp.exp(best - new_best)
    expo = jnp.where(mask, jnp.exp(scores - new_best[..., None]), 0.0)
    total = total * factor + jnp.sum(expo, axis=-1)
    accum = accum * factor[..., None] + jnp.einsum(
        "kgtn,nkd->kgtd",
        expo.astype(jnp.bfloat16),
        value_head_rows,
        preferred_element_type=jnp.float32,
    )
    return (new_best, total, accum)


def guarded_step(
    state, grouped_queries, key_block, value_block, pblock, sblock, query_pos, query_seg
):

    def guarded_work(current):
        return online_step(
            current, grouped_queries, key_block, value_block, pblock, sblock, query_pos, query_seg
        )

    def guarded_leave(current):
        return current

    return lax.cond(pblock[0] <= query_pos[-1], guarded_work, guarded_leave, state)


def online_blocks(
    carry, grouped_queries, key_rows, value_rows, key_pos, key_seg, query_pos, query_seg
):
    count = key_rows.shape[0]
    block_size = 512 if count > 512 and count % 512 == 0 else count
    if block_size == count:
        return guarded_step(
            carry, grouped_queries, key_rows, value_rows, key_pos, key_seg, query_pos, query_seg
        )

    def step(state, block_tile):
        return (
            guarded_step(
                state,
                grouped_queries,
                block_tile[0],
                block_tile[1],
                block_tile[2],
                block_tile[3],
                query_pos,
                query_seg,
            ),
            None,
        )

    block_tiles = (
        key_rows.reshape(-1, block_size, key_rows.shape[1]),
        value_rows.reshape(-1, block_size, value_rows.shape[1]),
        key_pos.reshape(-1, block_size),
        key_seg.reshape(-1, block_size),
    )
    carry, _ = lax.scan(step, carry, block_tiles)
    return carry


def forward_rows(xrow, seg_row, query_seg, positions, cosine_table, sine_table, weight_matrices):
    (
        query_weight,
        key_weight,
        value_weight,
        output_weight,
        gate_weight,
        up_weight,
        down_weight,
        gains,
    ) = weight_matrices
    token_rows = xrow.shape[0]
    query_groups = QUERY_HEADS // KEY_HEADS
    gain_one = gains[:MODEL_WIDTH].astype(jnp.float32)
    gain_two = gains[MODEL_WIDTH:].astype(jnp.float32)
    inv_one = lax.rsqrt(jnp.mean(xrow * xrow, axis=-1, keepdims=True) + EPS)
    normed_one = xrow * inv_one
    activated_hidden = (normed_one * gain_one).astype(jnp.bfloat16)
    query_unrotated = jnp.dot(
        activated_hidden, query_weight, preferred_element_type=jnp.float32
    ).reshape(token_rows, QUERY_HEADS, HEAD_SIZE)
    key_unrotated = jnp.dot(
        activated_hidden, key_weight, preferred_element_type=jnp.float32
    ).reshape(token_rows, KEY_HEADS, HEAD_SIZE)
    value_raw = jnp.dot(activated_hidden, value_weight, preferred_element_type=jnp.float32)
    grouped_queries = (
        rotary_apply(query_unrotated, cosine_table, sine_table, 1.0)
        .astype(jnp.bfloat16)
        .reshape(token_rows, KEY_HEADS, query_groups, HEAD_SIZE)
    )
    key_rows = (
        rotary_apply(key_unrotated, cosine_table, sine_table, 1.0)
        .astype(jnp.bfloat16)
        .reshape(token_rows, KEY_HEADS * HEAD_SIZE)
    )
    value_rows = value_raw.astype(jnp.bfloat16)
    start_state = (
        jnp.full((KEY_HEADS, query_groups, token_rows), NEGATIVE_LARGE, jnp.float32),
        jnp.zeros((KEY_HEADS, query_groups, token_rows), jnp.float32),
        jnp.zeros((KEY_HEADS, query_groups, token_rows, HEAD_SIZE), jnp.float32),
    )
    piece = (
        lax.all_gather(key_rows, "ctx", axis=0, tiled=True),
        lax.all_gather(value_rows, "ctx", axis=0, tiled=True),
    )
    count = piece[0].shape[0]
    key_pos = jnp.arange(count, dtype=jnp.int32)
    best, total, accum = online_blocks(
        start_state, grouped_queries, piece[0], piece[1], key_pos, seg_row, positions, query_seg
    )
    attn = accum / total[..., None]
    lse = best + jnp.log(total)
    attn_low = (
        jnp.transpose(attn, (2, 0, 1, 3))
        .reshape(token_rows, QUERY_HEADS * HEAD_SIZE)
        .astype(jnp.bfloat16)
    )
    residual = xrow + jnp.dot(attn_low, output_weight, preferred_element_type=jnp.float32)
    inv_two = lax.rsqrt(jnp.mean(residual * residual, axis=-1, keepdims=True) + EPS)
    normed_two = residual * inv_two
    mixed = (normed_two * gain_two).astype(jnp.bfloat16)
    gate = jnp.dot(mixed, gate_weight, preferred_element_type=jnp.float32)
    upper = jnp.dot(mixed, up_weight, preferred_element_type=jnp.float32)
    hidden = (jax.nn.silu(gate) * upper).astype(jnp.bfloat16)
    result = residual + jnp.dot(hidden, down_weight, preferred_element_type=jnp.float32)
    kept = (
        inv_one,
        normed_one,
        activated_hidden,
        grouped_queries,
        key_rows,
        value_rows,
        attn,
        lse,
        attn_low,
        inv_two,
        normed_two,
        mixed,
        gate,
        upper,
        hidden,
    )
    return (result, kept)


def backward_rows(
    dout, seg_row, query_seg, positions, cosine_table, sine_table, weight_matrices, kept
):
    (
        query_weight,
        key_weight,
        value_weight,
        output_weight,
        gate_weight,
        up_weight,
        down_weight,
        gains,
    ) = weight_matrices
    (
        inv_one,
        normed_one,
        activated_hidden,
        grouped_queries,
        key_rows,
        value_rows,
        attn,
        lse,
        attn_low,
        inv_two,
        normed_two,
        mixed,
        gate,
        upper,
        hidden,
    ) = kept
    token_rows = dout.shape[0]
    query_groups = QUERY_HEADS // KEY_HEADS
    scale = HEAD_SIZE ** (-0.5)
    gain_one = gains[:MODEL_WIDTH].astype(jnp.float32)
    gain_two = gains[MODEL_WIDTH:].astype(jnp.float32)
    dout_low = dout.astype(jnp.bfloat16)
    grad_down = jnp.einsum("tf,td->fd", hidden, dout_low, preferred_element_type=jnp.float32)
    grad_hidden = jnp.einsum("td,fd->tf", dout_low, down_weight, preferred_element_type=jnp.float32)
    sigma = jax.nn.sigmoid(gate)
    grad_gate_act = (grad_hidden * upper * (sigma + gate * sigma * (1.0 - sigma))).astype(
        jnp.bfloat16
    )
    grad_up_act = (grad_hidden * (gate * sigma)).astype(jnp.bfloat16)
    grad_gate = jnp.einsum("te,tf->ef", mixed, grad_gate_act, preferred_element_type=jnp.float32)
    grad_up = jnp.einsum("te,tf->ef", mixed, grad_up_act, preferred_element_type=jnp.float32)
    grad_mixed = jnp.einsum(
        "tf,ef->te", grad_gate_act, gate_weight, preferred_element_type=jnp.float32
    ) + jnp.einsum("tf,ef->te", grad_up_act, up_weight, preferred_element_type=jnp.float32)
    grad_gain_two = jnp.sum(grad_mixed * normed_two, axis=0)
    scaled_two = grad_mixed * gain_two
    grad_res = dout + inv_two * (
        scaled_two - normed_two * jnp.mean(scaled_two * normed_two, axis=-1, keepdims=True)
    )
    grad_branch = grad_res.astype(jnp.bfloat16)
    grad_output = jnp.einsum("te,td->ed", attn_low, grad_branch, preferred_element_type=jnp.float32)
    attention_gradient = jnp.einsum(
        "td,ed->te", grad_branch, output_weight, preferred_element_type=jnp.float32
    )
    attention_gradient_reduced = attention_gradient.astype(jnp.bfloat16).reshape(
        token_rows, KEY_HEADS, query_groups, HEAD_SIZE
    )
    delta = jnp.einsum("tkgd,kgtd->kgt", attention_gradient_reduced.astype(jnp.float32), attn)
    key_rows_total, value_rows_total = (
        lax.all_gather(key_rows, "ctx", axis=0, tiled=True),
        lax.all_gather(value_rows, "ctx", axis=0, tiled=True),
    )
    token_length = key_rows_total.shape[0]
    block_size = min(512, token_length)

    def reverse_block_step(grad_query, block_tile):
        key_block, value_block, pblock, sblock = block_tile

        def reverse_work(current):
            key_head_rows = key_block.reshape(block_size, KEY_HEADS, HEAD_SIZE)
            value_head_rows = value_block.reshape(block_size, KEY_HEADS, HEAD_SIZE)
            scores = (
                jnp.einsum(
                    "tkgd,nkd->kgtn",
                    grouped_queries,
                    key_head_rows,
                    preferred_element_type=jnp.float32,
                )
                * scale
            )
            mask = allowed(pblock, sblock, positions, query_seg)[None, None]
            probs = jnp.where(mask, jnp.exp(scores - lse[..., None]), 0.0)
            grad_probs = jnp.einsum(
                "tkgd,nkd->kgtn",
                attention_gradient_reduced,
                value_head_rows,
                preferred_element_type=jnp.float32,
            )
            grad_scores = (probs * (grad_probs - delta[..., None])).astype(jnp.bfloat16)
            updated_state = current + jnp.einsum(
                "kgtn,nkd->tkgd", grad_scores, key_head_rows, preferred_element_type=jnp.float32
            )
            key_gradient_term = (
                jnp.einsum(
                    "kgtn,tkgd->nkd",
                    grad_scores,
                    grouped_queries,
                    preferred_element_type=jnp.float32,
                )
                * scale
            )
            value_gradient_term = jnp.einsum(
                "kgtn,tkgd->nkd",
                probs.astype(jnp.bfloat16),
                attention_gradient_reduced,
                preferred_element_type=jnp.float32,
            )
            return (
                updated_state,
                (
                    key_gradient_term.reshape(block_size, KEY_HEADS * HEAD_SIZE),
                    value_gradient_term.reshape(block_size, KEY_HEADS * HEAD_SIZE),
                ),
            )

        def reverse_leave(current):
            empty_state = jnp.zeros((block_size, KEY_HEADS * HEAD_SIZE), jnp.float32)
            return (current, (empty_state, empty_state))

        return lax.cond(pblock[0] <= positions[-1], reverse_work, reverse_leave, grad_query)

    places = jnp.arange(token_length, dtype=jnp.int32)
    block_tiles = (
        key_rows_total.reshape(-1, block_size, KEY_HEADS * HEAD_SIZE),
        value_rows_total.reshape(-1, block_size, KEY_HEADS * HEAD_SIZE),
        places.reshape(-1, block_size),
        seg_row.reshape(-1, block_size),
    )
    grad_query_rot, (key_gradient_terms, value_gradient_terms) = lax.scan(
        reverse_block_step,
        jnp.zeros((token_rows, KEY_HEADS, query_groups, HEAD_SIZE), jnp.float32),
        block_tiles,
    )
    key_gradient_rows, grad_values = (
        lax.psum_scatter(
            key_gradient_terms.reshape(token_length, KEY_HEADS * HEAD_SIZE),
            "ctx",
            scatter_dimension=0,
            tiled=True,
        ),
        lax.psum_scatter(
            value_gradient_terms.reshape(token_length, KEY_HEADS * HEAD_SIZE),
            "ctx",
            scatter_dimension=0,
            tiled=True,
        ),
    )
    grad_q_low = (
        rotary_apply(
            (grad_query_rot * scale).reshape(token_rows, QUERY_HEADS, HEAD_SIZE),
            cosine_table,
            sine_table,
            -1.0,
        )
        .astype(jnp.bfloat16)
        .reshape(token_rows, QUERY_HEADS * HEAD_SIZE)
    )
    grad_k_low = (
        rotary_apply(
            key_gradient_rows.reshape(token_rows, KEY_HEADS, HEAD_SIZE),
            cosine_table,
            sine_table,
            -1.0,
        )
        .astype(jnp.bfloat16)
        .reshape(token_rows, KEY_HEADS * HEAD_SIZE)
    )
    grad_v_low = grad_values.astype(jnp.bfloat16)
    grad_wq = jnp.einsum(
        "te,tf->ef", activated_hidden, grad_q_low, preferred_element_type=jnp.float32
    )
    grad_wk = jnp.einsum(
        "te,tf->ef", activated_hidden, grad_k_low, preferred_element_type=jnp.float32
    )
    grad_wv = jnp.einsum(
        "te,tf->ef", activated_hidden, grad_v_low, preferred_element_type=jnp.float32
    )
    grad_acted = jnp.einsum(
        "tf,ef->te", grad_q_low, query_weight, preferred_element_type=jnp.float32
    )
    grad_acted = grad_acted + jnp.einsum(
        "tf,ef->te", grad_k_low, key_weight, preferred_element_type=jnp.float32
    )
    grad_acted = grad_acted + jnp.einsum(
        "tf,ef->te", grad_v_low, value_weight, preferred_element_type=jnp.float32
    )
    grad_gain_one = jnp.sum(grad_acted * normed_one, axis=0)
    scaled_one = grad_acted * gain_one
    grad_input = grad_res + inv_one * (
        scaled_one - normed_one * jnp.mean(scaled_one * normed_one, axis=-1, keepdims=True)
    )
    terms = [
        grad_wq.reshape(-1),
        grad_wk.reshape(-1),
        grad_wv.reshape(-1),
        grad_output.reshape(-1),
        grad_gate.reshape(-1),
        grad_up.reshape(-1),
        grad_down.reshape(-1),
        jnp.concatenate([grad_gain_one, grad_gain_two]),
    ]
    return (grad_input.astype(jnp.bfloat16), terms)


def local(
    inputs,
    segments,
    query_weight,
    key_weight,
    value_weight,
    output_weight,
    gate_weight,
    up_weight,
    down_weight,
    norm_gain_pair,
    cotangent,
):
    shard_rows = inputs.shape[2]
    seg_full = lax.all_gather(segments, "ctx", axis=2, tiled=True)
    positions = lax.axis_index("ctx") * shard_rows + jnp.arange(shard_rows, dtype=jnp.int32)
    cosine_table, sine_table = rope_parts(positions)
    weight_matrices = shape_weights(
        (
            lax.all_gather(query_weight, ("grp", "ctx"), axis=0, tiled=True),
            lax.all_gather(key_weight, ("grp", "ctx"), axis=0, tiled=True),
            lax.all_gather(value_weight, ("grp", "ctx"), axis=0, tiled=True),
            lax.all_gather(output_weight, ("grp", "ctx"), axis=0, tiled=True),
            lax.all_gather(gate_weight, ("grp", "ctx"), axis=0, tiled=True),
            lax.all_gather(up_weight, ("grp", "ctx"), axis=0, tiled=True),
            lax.all_gather(down_weight, ("grp", "ctx"), axis=0, tiled=True),
            lax.all_gather(norm_gain_pair, ("grp", "ctx"), axis=0, tiled=True),
        )
    )
    results = []
    saved = []
    for micro_step in range(MICRO):
        xrow = inputs[micro_step, 0].astype(jnp.float32)
        result, kept = forward_rows(
            xrow,
            seg_full[micro_step, 0],
            segments[micro_step, 0],
            positions,
            cosine_table,
            sine_table,
            weight_matrices,
        )
        results.append(result.astype(jnp.bfloat16))
        saved.append(kept)
    mats_back = shape_weights(
        (
            lax.all_gather(query_weight, ("grp", "ctx"), axis=0, tiled=True),
            lax.all_gather(key_weight, ("grp", "ctx"), axis=0, tiled=True),
            lax.all_gather(value_weight, ("grp", "ctx"), axis=0, tiled=True),
            lax.all_gather(output_weight, ("grp", "ctx"), axis=0, tiled=True),
            lax.all_gather(gate_weight, ("grp", "ctx"), axis=0, tiled=True),
            lax.all_gather(up_weight, ("grp", "ctx"), axis=0, tiled=True),
            lax.all_gather(down_weight, ("grp", "ctx"), axis=0, tiled=True),
            lax.all_gather(norm_gain_pair, ("grp", "ctx"), axis=0, tiled=True),
        )
    )
    input_grads = []
    shares = None
    totals = None
    for micro_step in range(MICRO):
        dout = cotangent[micro_step, 0].astype(jnp.float32)
        grad_input, terms = backward_rows(
            dout,
            seg_full[micro_step, 0],
            segments[micro_step, 0],
            positions,
            cosine_table,
            sine_table,
            mats_back,
            saved[micro_step],
        )
        input_grads.append(grad_input)
        totals = terms if totals is None else [a + b for a, b in zip(totals, terms)]
    shares = list(
        (
            lax.psum_scatter(totals[0], ("grp", "ctx"), scatter_dimension=0, tiled=True),
            lax.psum_scatter(totals[1], ("grp", "ctx"), scatter_dimension=0, tiled=True),
            lax.psum_scatter(totals[2], ("grp", "ctx"), scatter_dimension=0, tiled=True),
            lax.psum_scatter(totals[3], ("grp", "ctx"), scatter_dimension=0, tiled=True),
            lax.psum_scatter(totals[4], ("grp", "ctx"), scatter_dimension=0, tiled=True),
            lax.psum_scatter(totals[5], ("grp", "ctx"), scatter_dimension=0, tiled=True),
            lax.psum_scatter(totals[6], ("grp", "ctx"), scatter_dimension=0, tiled=True),
            lax.psum_scatter(totals[7], ("grp", "ctx"), scatter_dimension=0, tiled=True),
        )
    )
    outputs = jnp.stack(results)[:, None]
    input_grad = jnp.stack(input_grads)[:, None]
    return (
        outputs,
        input_grad,
        shares[0],
        shares[1],
        shares[2],
        shares[3],
        shares[4],
        shares[5],
        shares[6],
        shares[7],
    )


W = MODEL_WIDTH
HG = QUERY_HEADS // KEY_HEADS * HEAD_SIZE
QK = HG + HEAD_SIZE
SLAB = 384
QKV = HG + 2 * HEAD_SIZE
OUT = W // 8
BACK = 512
FEED = 432
EDGE = 304
CHUNK = W // 32
HID = HIDDEN_UNITS // 8
SUB = HIDDEN_UNITS // 32
ROWS = 128
ALL = 8 * ROWS
POS = 64
LEN = 512
RELATIVE = (0, 2, 4, 6, 1, 3, 5, 7)
STEP = 512
STEPS = ALL // STEP
F32 = jnp.float32
BF16 = jnp.bfloat16
SCALE = HEAD_SIZE ** (-0.5)
NT = (((1,), (1,)), ((), ()))
TN = (((0,), (0,)), ((), ()))
MIB = 1024 * 1024
LARGE = ("attend", "project", "feed", "back")


def pc(value, k):
    return lax.ppermute(value, "ctx", [(s, s ^ k) for s in range(8)])


def pz(value, k):
    return lax.ppermute(value, "grp", [(s, s ^ k) for s in range(4)])


def after(value, *others):
    return lax.optimization_barrier((value,) + others)[0]


def first_ctx(value):
    far = pc(value, 6)
    return [value, pc(value, 2), pc(value, 4), far]


def both_cores(mine):
    return mine + [pc(m, 1) for m in mine]


def gather_ctx(value):
    return both_cores(first_ctx(value))


def gather_grp(value):
    one = pz(value, 1)
    two = pz(value, 2)
    return (value, one, two, pz(two, 1))


def add_low(a, b):
    return (a.astype(F32) + b.astype(F32)).astype(BF16)


class Order:
    def __init__(self):
        self.last = None

    def __call__(self, values):
        return values if self.last is None else after(values, self.last)

    def then(self, result):
        self.last = jax.tree.leaves(result)[-1]
        return result

    def wait(self, values):
        return self.then(self(values))


def scatter_ctx(even, got):
    return [add_low(even[k], got[k]) for k in range(4)]


def send_ctx(sums):
    far = pc(sums[3], 6)
    return sums[0], pc(sums[1], 2), pc(sums[2], 4), far


def pick(blocks, g):
    return [lax.dynamic_index_in_dim(blocks, g ^ k, 0, keepdims=False) for k in range(4)]


def call(body, outs, *args, grid=None, in_specs=None, out_specs=None, scratch=(), name=None):
    kwargs = {}
    if grid is not None:
        kwargs = dict(grid=grid, in_specs=in_specs, out_specs=out_specs)
    else:
        kwargs = dict(
            in_specs=[
                pl.BlockSpec(memory_space=pltpu.SMEM)
                if a.dtype == jnp.int32 and a.ndim == 1
                else pl.BlockSpec(memory_space=pltpu.VMEM)
                for a in args
            ],
            out_specs=out_specs or [pl.BlockSpec(memory_space=pltpu.VMEM) for _ in outs],
        )
    return pl.pallas_call(
        body,
        out_shape=outs,
        scratch_shapes=scratch,
        compiler_params=pltpu.CompilerParams(vmem_limit_bytes=(32 if name in LARGE else 16) * MIB),
        cost_estimate=pl.CostEstimate(flops=0, bytes_accessed=1, transcendentals=0),
        name=name,
        **kwargs,
    )(*args)


def late(values):
    return [pltpu.with_memory_space_constraint(v, pltpu.HBM) for v in values]


def hbm(shape, dtype):
    return pltpu.HBM(shape, dtype)


def hbm(shape, dtype):
    return pltpu.HBM(shape, dtype)


def hbm(shape, dtype):
    return pltpu.HBM(shape, dtype)


def sds(shape, dtype):
    return jax.ShapeDtypeStruct(shape, dtype)


def rows_of(ref, count):
    wide = ref.shape[0] // count
    return jnp.concatenate([ref[pl.ds(n, count, stride=wide), :] for n in range(wide)], 1)


def store_rows(ref, rows):
    count = rows.shape[0]
    wide = ref.shape[0] // count
    for n in range(wide):
        ref[pl.ds(n, count, stride=wide), :] = rows[:, n * 128 : (n + 1) * 128]


def pack_body(q_r, k_r, v_r, gate_r, up_r, gain, out, sq, sk, sv, sg, su):
    for src, dst in ((q_r, sq), (k_r, sk), (v_r, sv), (gate_r, sg), (up_r, su)):
        dst[...] = src[...].astype(F32)
    q, k, v, gate, up = (rows_of(s, CHUNK) for s in (sq, sk, sv, sg, su))
    tail = jnp.concatenate([gain[:, n * SLAB : (n + 1) * SLAB] for n in range(3)], 0).astype(F32)
    tail = jnp.concatenate([tail, jnp.zeros((1, SLAB), F32)], 0)
    for h in range(8):
        if h < KEY_HEADS:
            rows = jnp.concatenate(
                [
                    q[:, h * HG : (h + 1) * HG],
                    k[:, h * HEAD_SIZE : (h + 1) * HEAD_SIZE],
                    v[:, h * HEAD_SIZE : (h + 1) * HEAD_SIZE],
                    jnp.zeros((CHUNK, SLAB - QKV), F32),
                ],
                1,
            )
        else:
            rows = jnp.zeros((CHUNK, SLAB), F32)
        out[h, :, :SLAB] = jnp.concatenate([rows, tail], 0).astype(BF16)
        parts = [
            full[:, z * 768 + h * SUB : z * 768 + (h + 1) * SUB] for full in (gate, up) for z in range(4)
        ]
        rows = jnp.concatenate([jnp.concatenate(parts, 1), jnp.zeros((4, 2 * HID), F32)], 0)
        out[h, :, SLAB:] = rows.astype(BF16)


def unpack_body(src, slab, feed):
    for h in range(8):
        slab[h] = src[h, :, :SLAB]
    feed[...] = jnp.concatenate([src[h, :CHUNK, SLAB:].astype(F32) for h in range(8)], 0).astype(BF16)


def join_body(*refs):
    for n, block in enumerate(refs[:8]):
        refs[8][n * ROWS : (n + 1) * ROWS, :] = block[...]


def join(blocks):
    return call(join_body, [sds((ALL, W), BF16)], *blocks, name="join")[0]


def output_weight_body(sc, b0, b1, b2, b3, b4, b5, b6, b7, out, rows):
    i, g = sc[0], sc[1]
    for j, b in zip(RELATIVE, (b0, b1, b2, b3, b4, b5, b6, b7)):
        for k in range(4):
            rows[i ^ j, g ^ k] = b[k].astype(F32)
    for z in range(4):
        for q in range(2):
            parts = [rows_of(rows.at[c, z], CHUNK) for c in range(4 * q, 4 * q + 4)]
            start = z * 288 + q * 144
            out[start : start + 144, :] = jnp.concatenate(parts, 0).astype(BF16)


def rotate(x, cosine, sine, sign):
    lane = lax.broadcasted_iota(jnp.int32, (1, 128), 1) % HEAD_SIZE
    first = lane < HEAD_SIZE // 2
    halves = []
    for n in range(x.shape[1] // 128):
        part = x[:, n * 128 : (n + 1) * 128]
        swapped = jnp.where(first, pltpu.roll(part, 96, 1), pltpu.roll(part, 32, 1))
        halves.append(part * cosine + sign * (swapped * sine))
    return jnp.concatenate(halves, 1)


def attend_body(
    sc, x0, x1, x2, x3, x4, x5, x6, x7, w0, w1, w2, w3, cosine, sine, pcol, prow,
    att, gains, w_o, qk_h, v_h, acted_h, probs_h, x_h, qk_o, v_o, acted, probs, x_o, segs, held, sems,
):
    xs = (x0, x1, x2, x3, x4, x5, x6, x7)
    g = sc[1]
    copies = []

    def send(src, dst):
        copy = pltpu.make_async_copy(src, dst, sems.at[len(copies)])
        copy.start()
        copies.append(copy)

    sums = [jnp.zeros((3, SLAB), F32), jnp.zeros((3, SLAB), F32)]
    for k, w in enumerate((w0, w1, w2, w3)):
        z = g ^ k
        block = jnp.concatenate([w[h, :CHUNK, :].astype(F32) for h in range(8)], 0)
        w_o[pl.ds(pl.multiple_of(z * 288, 32), 288), :] = block.astype(BF16)
        rows = sum(w[h, CHUNK : CHUNK + 3, :].astype(F32) for h in range(8))
        sums[0] = sums[0] + jnp.where(z < 2, rows, 0.0)
        sums[1] = sums[1] + jnp.where(z < 2, 0.0, rows)
    gain = [jnp.concatenate([s[0:1], s[1:2], s[2:3]], 1) for s in sums]
    gains[...] = jnp.concatenate([gain[0], gain[1], jnp.zeros((6, W), F32)], 0)
    for b in range(8):
        x_o[b * ROWS : (b + 1) * ROWS, :] = xs[b][:, :W]
        segs[b] = xs[b][:, W:]

    @pl.loop(0, 8)
    def _(b):
        at = pl.ds(pl.multiple_of(b * ROWS, ROWS), ROWS)
        x = x_o[at, :].astype(F32)
        inv = lax.rsqrt(jnp.mean(x * x, axis=-1, keepdims=True) + EPS)
        acted[at, :] = (x * inv * gain[0]).astype(BF16)

    send(x_o, x_h)
    send(acted, acted_h)

    @pl.loop(0, MICRO)
    def _(m):
        part = pl.ds(pl.multiple_of(m * POS, POS), POS)
        rows = jnp.concatenate(
            [acted[pl.ds(pl.multiple_of(b * ROWS + m * POS, POS), POS), :] for b in range(8)], 0
        )
        seg = jnp.concatenate([segs[b, part, :].astype(F32) for b in range(8)], 0)
        y = jnp.dot(rows, w_o[...], preferred_element_type=F32)
        qk = rotate(y[:, :QK], cosine[...], sine[...], 1.0).astype(BF16)
        v = y[:, QK:].astype(BF16)
        qk_o[m] = qk
        v_o[m] = v
        seg_row = jnp.transpose(seg)[0:1, :]
        mask = (prow[0:1, :] <= pcol[:, 0:1]) & (seg_row == seg[:, 0:1])
        bias = jnp.where(mask, 0.0, NEGATIVE_LARGE)
        keys = qk[:, HG:]
        for h in range(3):
            s = lax.dot_general(
                qk[:, h * HEAD_SIZE : (h + 1) * HEAD_SIZE], keys, NT, preferred_element_type=F32
            )
            s = s * SCALE + bias
            e = jnp.exp(s - jnp.max(s, axis=-1, keepdims=True))
            p = (e * (1.0 / jnp.sum(e, axis=-1, keepdims=True))).astype(BF16)
            probs[m, h] = p
            held[m, :, h * HEAD_SIZE : (h + 1) * HEAD_SIZE] = jnp.dot(
                p, v[:, :HEAD_SIZE], preferred_element_type=F32
            ).astype(BF16)

    for m in range(MICRO):
        att[:, m * HG : (m + 1) * HG] = held[m]
    send(probs, probs_h)
    send(qk_o, qk_h)
    send(v_o, v_h)
    for copy in copies:
        copy.wait()


def project_body(sc, x, a0, a1, a2, a3, a4, a5, a6, a7, wo, gains, att_o, mixed_o, res_o, heads):
    i = sc[0]
    t = pl.program_id(0)
    for j, a in zip(RELATIVE, (a0, a1, a2, a3, a4, a5, a6, a7)):
        h = i ^ j
        for half in range(STEP // ROWS):
            b = STEP // ROWS * t + half
            q = (2 * (b & 3) + (b >> 2)) ^ j
            start = pl.multiple_of(((q & 1) * 4 + (q >> 1)) * POS, POS)
            rows = a[pl.ds(start, POS), :]
            for m in range(MICRO):
                heads[h, half * ROWS + m * POS : half * ROWS + (m + 1) * POS, :] = rows[:, m * HG : (m + 1) * HG]
    for h in range(KEY_HEADS):
        att_o[:, h * HG : (h + 1) * HG] = heads[h]
    residual = x[...].astype(F32) + jnp.dot(att_o[...], wo[...], preferred_element_type=F32)

    @pl.when(t == 0)
    def _():
        res_o[...] = residual[:ROWS]

    inv = lax.rsqrt(jnp.mean(residual * residual, axis=-1, keepdims=True) + EPS)
    mixed_o[...] = (residual * inv * gains[1:2, :]).astype(BF16)


def feed_body(
    sc, mixed_r, c, g0, g1, g2, g3, d0, d1, d2, d3, hidden_o, dgu_o, pm, pe, dn, sums, gu
):
    g = sc[1]
    t = pl.program_id(0)

    @pl.when(t == 0)
    def _():
        for k, (a, d) in enumerate(((g0, d0), (g1, d1), (g2, d2), (g3, d3))):
            z = g ^ k
            gu[pl.ds(pl.multiple_of(z * 288, 32), 288), :] = a[...]
            dn[pl.ds(pl.multiple_of(z * SUB, 32), SUB), :] = d[...]
        sums[...] = jnp.zeros((8, W), F32)

    mixed = mixed_r[...]
    y = jnp.dot(mixed, gu[...], preferred_element_type=F32)
    gate = y[:, :HID]
    up = y[:, HID:]
    sig = 1.0 / (1.0 + jnp.exp(-gate))
    silu = gate * sig
    hidden_o[...] = (silu * up).astype(BF16)
    dh = lax.dot_general(c[...], dn[...], NT, preferred_element_type=F32)
    dgate = (dh * up * (sig + silu * (1.0 - sig))).astype(BF16)
    dup = (dh * silu).astype(BF16)
    dgu = jnp.concatenate([dgate, dup], 1)
    dgu_o[...] = dgu
    dm = lax.dot_general(dgu, gu[...], NT, preferred_element_type=F32)
    sums[0:1, :] = sums[0:1, :] + jnp.sum(dm * mixed.astype(F32), axis=0, keepdims=True)
    dm = dm.astype(BF16).reshape(4, ROWS, W)

    @pl.when(t == 0)
    def _():
        pm[...] = dm

    @pl.when(t == 1)
    def _():
        pe[...] = dm


def whole(*shape):
    return pl.BlockSpec(shape, lambda t: (0,) * len(shape))


def rows_at(rows, columns):
    return pl.BlockSpec((rows, columns), lambda t: (t, 0))


def run_project(sc, x, heads, w_out, gains):
    return call(
        project_body,
        [hbm((ALL, W), BF16), sds((ALL, W), BF16), hbm((ROWS, W), F32)],
        sc, x, *heads, w_out, gains,
        grid=(STEPS,),
        in_specs=[pl.BlockSpec(memory_space=pltpu.SMEM), rows_at(STEP, W)]
        + [whole(LEN, 2 * HG)] * 8
        + [whole(W, W), whole(8, W)],
        out_specs=[rows_at(STEP, W), rows_at(STEP, W), whole(ROWS, W)],
        scratch=[pltpu.VMEM((8, STEP, HG), BF16)], name="project",
    )


def run_feed(sc, mixed, c, feeds):
    return call(
        feed_body,
        [
            sds((ALL, HID), BF16),
            sds((ALL, 2 * HID), BF16),
            sds((4, ROWS, W), BF16),
            sds((4, ROWS, W), BF16),
            sds((HID, W), BF16),
            sds((8, W), F32),
        ],
        sc, mixed, c, *feeds,
        grid=(STEPS,),
        in_specs=[pl.BlockSpec(memory_space=pltpu.SMEM), rows_at(STEP, W), rows_at(STEP, W)]
        + [whole(288, 2 * HID)] * 4
        + [whole(SUB, W)] * 4,
        out_specs=[
            rows_at(STEP, HID),
            rows_at(STEP, 2 * HID),
            whole(4, ROWS, W),
            whole(4, ROWS, W),
            whole(HID, W),
            whole(8, W),
        ],
        scratch=[pltpu.VMEM((W, 2 * HID), BF16)], name="feed",
    )


def mid_body(a, b, d, f, c, res, gains, dres, low):
    dm = a[...].astype(F32) + b[...].astype(F32) + d[...].astype(F32) + f[...].astype(F32)
    r = res[...]
    inv = lax.rsqrt(jnp.mean(r * r, axis=-1, keepdims=True) + EPS)
    n = r * inv
    e = dm * gains[1:2, :]
    out = c[...].astype(F32) + inv * (e - n * jnp.mean(e * n, axis=-1, keepdims=True))
    dres[...] = out
    low[...] = out.astype(BF16)


def last_body(a, b, d, f, x, dres, gains, out):
    da = a[...].astype(F32) + b[...].astype(F32) + d[...].astype(F32) + f[...].astype(F32)
    r = x[...].astype(F32)
    inv = lax.rsqrt(jnp.mean(r * r, axis=-1, keepdims=True) + EPS)
    n = r * inv
    e = da * gains[0:1, :]
    out[...] = (dres[...] + inv * (e - n * jnp.mean(e * n, axis=-1, keepdims=True))).astype(BF16)


def back_body(
    sc, l0, l1, l2, l3, l4, l5, l6, l7, wo, qk_r, v_r, probs, cosine, sine, acted_t, att_t, w_slab, gains, sums,
    out, b0, b1, b2, b3, columns, dots, edge,
):
    lows = (l0, l1, l2, l3, l4, l5, l6, l7)
    i, g = sc[0], sc[1]
    place = lax.broadcasted_iota(jnp.int32, (256, W), 1) - lax.broadcasted_iota(jnp.int32, (256, W), 0)
    chosen = jnp.where(place == i * OUT, 1.0, 0.0).astype(BF16)
    @pl.loop(0, MICRO)
    def _(m):
        part = pl.ds(pl.multiple_of(m * POS, POS), POS)
        rows = jnp.concatenate([lows[b][part, :] for b in range(8)], 0)
        datt = lax.dot_general(rows, wo[...], NT, preferred_element_type=F32).astype(BF16)
        chosen_rows = lax.dot_general(rows, chosen, NT, preferred_element_type=F32).astype(BF16)
        qk = qk_r[m]
        keys = qk[:, HG:]
        v = v_r[m][:, :HEAD_SIZE]
        dq = []
        dk = jnp.zeros((HEAD_SIZE, LEN), F32)
        dv = jnp.zeros((HEAD_SIZE, LEN), F32)
        for h in range(3):
            da = datt[:, h * HEAD_SIZE : (h + 1) * HEAD_SIZE]
            q = qk[:, h * HEAD_SIZE : (h + 1) * HEAD_SIZE]
            low = probs[m, h]
            p = low.astype(F32)
            dp = lax.dot_general(da, v, NT, preferred_element_type=F32)
            delta = jnp.sum(p * dp, axis=-1, keepdims=True)
            ds = (p * (dp - delta)).astype(BF16)
            dq.append(jnp.dot(ds, keys, preferred_element_type=F32))
            dk = dk + lax.dot_general(q, ds, TN, preferred_element_type=F32)
            dv = dv + lax.dot_general(da, low, TN, preferred_element_type=F32)
        dqk = jnp.concatenate(dq + [jnp.transpose(dk)], 1) * SCALE
        dqk = rotate(dqk, cosine[...], sine[...], -1.0)
        dvt = jnp.transpose(jnp.concatenate([dv, jnp.zeros((HEAD_SIZE, LEN), F32)], 0))
        full = jnp.concatenate([dqk, dvt], 1).astype(BF16)
        for b in range(8):
            at = pl.ds(pl.multiple_of(b * ROWS + m * POS, POS), POS)
            out[at, :] = full[b * POS : (b + 1) * POS, :]
            columns[at, :] = chosen_rows[b * POS : (b + 1) * POS, :]

    blocks = (b0, b1, b2, b3)
    for k in range(4):
        z = g ^ k
        start = pl.multiple_of(z * 288, 32)
        y = jnp.dot(acted_t[pl.ds(start, 288), :], out[...], preferred_element_type=F32)
        yo = jnp.dot(att_t[pl.ds(start, 288), :], columns[...], preferred_element_type=F32)
        y2 = jnp.concatenate([y[:, :QKV], yo[:, : BACK - QKV]], 1)
        blocks[k][:288, :] = y2.astype(BF16)
        dot = jnp.sum(y * w_slab[pl.ds(start, 288), :].astype(F32), axis=-1, keepdims=True)
        dots[z] = jnp.transpose(jnp.broadcast_to(dot, (288, 128)))[:8, :]
    one = jnp.concatenate([dots[z][0:1, :] for z in range(4)], 1) / gains[0:1, :]
    two = sums[0:1, :] / gains[1:2, :]
    for z in range(4):
        full = one if z < 2 else two
        at = (z % 2) * 576
        rows = jnp.concatenate([full[:, at + 72 * c : at + 72 * (c + 1)] for c in range(8)], 0)
        rows = jnp.concatenate([rows, jnp.zeros((8, BACK - 72), F32)], 1)
        edge[z] = jnp.concatenate([rows, jnp.zeros((EDGE - 288 - 8, BACK), F32)], 0)
    for k in range(4):
        blocks[k][288:, :] = edge[g ^ k].astype(BF16)


def split_back_body(a, b, d, out):
    rows = a[...].astype(F32) + b[...].astype(F32) + d[...].astype(F32)
    for h in range(8):
        block = [rows[h * CHUNK : (h + 1) * CHUNK, :], rows[288 + h : 289 + h, :], jnp.zeros((3, BACK), F32)]
        out[h] = jnp.concatenate(block, 0).astype(BF16)


def grads_body(sc, grad_gu, grad_dn, b0, b1, b2, b3):
    g = sc[1]
    for k, block in enumerate((b0, b1, b2, b3)):
        z = g ^ k
        block[:288, :] = grad_gu[pl.ds(pl.multiple_of(z * 288, 32), 288), :]
        start = pl.multiple_of(z * SUB, 32)
        block[288 : 288 + SUB, :] = grad_dn[pl.ds(start, SUB), :768]
        block[288 + SUB :, :HID] = grad_dn[pl.ds(start, SUB // 2), 768:]
        block[288 + SUB :, HID:] = grad_dn[pl.ds(pl.multiple_of(start + SUB // 2, 16), SUB // 2), 768:]


def transpose_body(src, out):
    for n in range(ALL // 256):
        for m in range(W // 384):
            block = src[n * 256 : (n + 1) * 256, m * 384 : (m + 1) * 384]
            out[m * 384 : (m + 1) * 384, n * 256 : (n + 1) * 256] = jnp.transpose(block)


def transpose(value):
    return call(transpose_body, [sds((W, ALL), BF16)], value, name="transpose")[0]


def onward_body(rows, weight, even, odd):
    dims = NT if weight.shape[0] == W else (((1,), (0,)), ((), ()))
    for n in range(4):
        part = rows[n * 2 * ROWS : (n + 1) * 2 * ROWS, :]
        y = lax.dot_general(part, weight[...], dims, preferred_element_type=F32).astype(BF16)
        out = even if n < 2 else odd
        out[2 * (n % 2)] = y[:ROWS]
        out[2 * (n % 2) + 1] = y[ROWS:]


def onward(rows, weight, name):
    return call(onward_body, [sds((4, ROWS, W), BF16)] * 2, rows, weight, name=name)


def split_feed_body(a, b, d, out, down):
    rows = a[...].astype(F32) + b[...].astype(F32) + d[...].astype(F32)
    for h in range(8):
        out[h] = rows[h * CHUNK : (h + 1) * CHUNK, :].astype(BF16)
    right = jnp.concatenate([rows[288 + SUB :, :HID], rows[288 + SUB :, HID:]], 0)
    store_rows(down, jnp.concatenate([rows[288 : 288 + SUB, :], right], 1))


def split_back_body(a, b, d, out):
    rows = a[...].astype(F32) + b[...].astype(F32) + d[...].astype(F32)
    for h in range(8):
        block = [rows[h * CHUNK : (h + 1) * CHUNK, :], rows[288 + h : 289 + h, :], jnp.zeros((3, BACK), F32)]
        out[h] = jnp.concatenate(block, 0).astype(BF16)


def unpack_back_body(src, q, k, v, o, gains):
    parts = [src[h].astype(F32) for h in range(8)]
    rows = [p[:CHUNK, :] for p in parts]
    store_rows(q, jnp.concatenate([p[:, :HG] for p in rows[:KEY_HEADS]], 1))
    store_rows(k, jnp.concatenate([p[:, HG:QK] for p in rows[:KEY_HEADS]], 1))
    store_rows(v, jnp.concatenate([p[:, QK:QKV] for p in rows[:KEY_HEADS]], 1))
    store_rows(o, jnp.concatenate([p[:, QKV : QKV + OUT] for p in rows], 1))
    gains[...] = jnp.broadcast_to(sum(p[CHUNK : CHUNK + 1, :128] for p in parts), (8, 128))


def unpack_hidden_body(src, gate, up):
    for n, out in enumerate((gate, up)):
        parts = [
            src[h, :, n * HID + z * SUB : n * HID + (z + 1) * SUB].astype(F32)
            for z in range(4)
            for h in range(8)
        ]
        store_rows(out, jnp.concatenate(parts, 1))


def fast_local(inputs, segments, wq, wk, wv, wo, wg, wu, wd, gain_pair, cotangent):
    i = lax.axis_index("ctx").astype(jnp.int32)
    g = lax.axis_index("grp").astype(jnp.int32)
    r = g * 8 + i
    sc = jnp.stack([i, g])
    x_own = inputs.reshape(ROWS, W)
    c_own = cotangent.reshape(ROWS, W)
    order = Order()

    q2, k2, v2, gate2, up2 = (w.reshape(-1, 128) for w in (wq, wk, wv, wg, wu))
    placed = lax.dynamic_update_slice(jnp.zeros((1, W), BF16), gain_pair[None, :], (0, (r % 16) * 72))
    packed = order.then(
        call(
            pack_body,
            [sds((8, 40, SLAB + 2 * HID), BF16)],
            *late([q2, k2, v2, gate2, up2]), placed,
            scratch=[pltpu.VMEM(a.shape, F32) for a in (q2, k2, v2, gate2, up2)], name="pack",
        )
    )[0]
    packed = lax.all_to_all(packed, "ctx", 0, 0, tiled=True)

    x_late, seg_late, wo, wd, i_late, c_late = order((x_own, segments, wo, wd, i, c_own))
    o_own = wo.reshape(-1, 128)
    o_one, o_two = pz(o_own, 1), pz(o_own, 2)
    c_near = pc(c_late, 2), pc(c_late, 4)
    seg = jnp.broadcast_to(seg_late.reshape(ROWS, 1).astype(BF16), (ROWS, 128))
    x_sent = order.then(jnp.concatenate([x_late, seg], 1))
    d_own = order.then(order(wd).reshape(SUB, W))
    packed, o_one, o_two = order.wait((packed, o_one, o_two))

    slab, feed = order.then(
        call(unpack_body, [sds((8, 40, SLAB), BF16), sds((288, 2 * HID), BF16)], packed, name="unpack")
    )
    s_one, s_two = pz(slab, 1), pz(slab, 2)
    xs = first_ctx(order(x_sent))

    i_late = order(i_late)
    rel = jnp.array(RELATIVE, jnp.int32)
    positions = ((i_late ^ rel)[:, None] * POS + jnp.arange(POS, dtype=jnp.int32)[None, :]).reshape(LEN)
    half = HEAD_SIZE // 2
    freq = THETA ** (-jnp.arange(half, dtype=F32) * 2.0 / HEAD_SIZE)
    angle = positions.astype(F32)[:, None] * freq[None, :]
    cosine = jnp.tile(jnp.cos(angle), (1, 4))
    sine = jnp.sin(angle)
    sine = jnp.concatenate([-sine, sine, -sine, sine], 1)
    pcol = jnp.broadcast_to(positions.astype(F32)[:, None], (LEN, 128))
    prow = jnp.broadcast_to(positions.astype(F32)[None, :], (8, LEN))
    cosine, sine, pcol, prow = order.then((cosine, sine, pcol, prow))

    c_near = order.wait(c_near)
    s_one = order.wait(s_one)
    o_three = pz(order(o_two), 1)
    s_two = order.wait(s_two)
    s_three = pz(s_two, 1)
    o_three = order.wait(o_three)
    o_sent = order.then(jnp.stack([o_own, o_one, o_two, o_three]))
    d_one, d_two = pz(order(d_own), 1), pz(order(d_own), 2)
    s_three = order.wait(s_three)
    os = first_ctx(order(o_sent))
    xs = order.wait(both_cores(order.wait(xs)))
    xs, slabs = order((xs, (slab, s_one, s_two, s_three)))

    anywhere = pl.BlockSpec(memory_space=pl.ANY)
    vmem = pl.BlockSpec(memory_space=pltpu.VMEM)
    held = [
        sds((MICRO, LEN, QK), BF16),
        sds((MICRO, LEN, 128), BF16),
        sds((ALL, W), BF16),
        sds((MICRO, 3, LEN, LEN), BF16),
        sds((ALL, W), BF16),
    ]
    att, gains, w_slab, qk, v, acted, probs, call_x = order.then(
        call(
            attend_body,
            [sds((LEN, 2 * HG), BF16), sds((8, W), F32), sds((W, SLAB), BF16)]
            + [hbm(o.shape, o.dtype) for o in held],
            sc, *late(xs), *late(slabs), cosine, sine, pcol, prow,
            out_specs=[vmem] * 3 + [anywhere] * 5,
            scratch=[pltpu.VMEM(o.shape, o.dtype) for o in held]
            + [pltpu.VMEM((8, ROWS, 128), BF16), pltpu.VMEM((MICRO, LEN, HG), BF16), pltpu.SemaphoreType.DMA((5,))],
            name="attend",
        )
    )
    att, d_one, d_two = order.wait((att, d_one, d_two))
    heads = first_ctx(att)
    os = order.wait(os)
    g_one, g_two = pz(order(feed), 1), pz(order(feed), 2)
    os = order.wait(both_cores(os))
    w_out = order.then(
        call(
            output_weight_body, [sds((W, W), BF16)], sc, *late(os),
            scratch=[pltpu.VMEM((8, 4, wo.size // 128, 128), F32)], name="output_weight",
        )
    )[0]
    d_three = order.wait(pz(d_two, 1))
    acted_t = order.then(transpose(order(acted)))
    heads[1], heads[2] = order.wait((heads[1], heads[2]))
    heads = order.wait(both_cores(order.wait(heads)))
    g_two = order.wait(g_two)
    g_three = pz(g_two, 1)
    cs = [c_late, *c_near, pc(order(c_late), 6)]
    g_three, d_three = order.wait((g_three, d_three))

    att_full, mixed, res_own = order.then(run_project(sc, *late([call_x]), late(heads), w_out, gains))
    wo_own = order.then(lax.dynamic_slice(order(w_out), (jnp.minimum(i, KEY_HEADS - 1) * HG, 0), (HG, W)))
    call_c = order.then(join(late(order(both_cores(order.wait(cs))))))
    feeds = order((feed, g_one, g_two, g_three, d_own, d_one, d_two, d_three))
    hidden, dgu, pm, pe, down, dots_two = order.then(run_feed(sc, mixed, call_c, late(feeds)))

    got = pc(pe, 1)
    grad_gu = order.then(lax.dot_general(order(mixed), dgu, TN, preferred_element_type=F32).astype(BF16))
    terms = send_ctx(order.then(scatter_ctx(pm, order(got))))
    grad_dn = order.then(lax.dot_general(order(hidden), call_c, TN, preferred_element_type=F32).astype(BF16))
    feed_blocks = order.then(
        call(grads_body, [hbm((FEED, 2 * HID), BF16)] * 4, sc, grad_gu, grad_dn, name="grads")
    )
    feed_far = pz(feed_blocks[3], 1)
    att_t = order.then(transpose(order(att_full)))
    feed_mid = order.then(add_low(feed_blocks[2], order(feed_far)))
    feed_terms = (feed_blocks[0], pz(after(feed_blocks[1], feed_mid), 1), pz(feed_mid, 2))
    dres, low = order.then(
        call(
            mid_body, [hbm((ROWS, W), F32), hbm((ROWS, W), BF16)],
            *order(terms), *late([c_own, res_own]), gains, name="mid",
        )
    )
    lows = first_ctx(low)

    om_p, oe_p = order.then(onward(order(hidden), down, "outward"))
    out_got = pc(oe_p, 1)
    out_terms = send_ctx(order.then(scatter_ctx(om_p, order(out_got))))
    lows = both_cores(order(lows))

    dqkv, *slab_blocks = order.then(
        call(
            back_body,
            [sds((ALL, SLAB), BF16)] + [sds((EDGE, BACK), BF16)] * 4,
            sc, *late(order(lows)), wo_own, qk, v, probs, cosine, sine, acted_t, att_t, w_slab, gains, dots_two,
            scratch=[
                pltpu.VMEM((ALL, 256), BF16),
                pltpu.VMEM((4, 8, 288), F32),
                pltpu.VMEM((4, EDGE - 288, BACK), F32),
            ],
            name="back",
        )
    )
    slab_far = pz(slab_blocks[3], 1)
    hid_sum, grad_down = order.then(
        call(
            split_feed_body, [sds((8, CHUNK, 2 * HID), BF16), sds((864, 128), F32)],
            *order(feed_terms), name="split_feed",
        )
    )
    hid_sum = lax.all_to_all(hid_sum, "ctx", 0, 0, tiled=True)
    dam, dae = order.then(onward(order(dqkv), w_slab, "inward"))
    in_got = pc(dae, 1)
    slab_mid = order.then(add_low(slab_blocks[2], order(slab_far)))
    slab_terms = (slab_blocks[0], pz(after(slab_blocks[1], slab_mid), 1), pz(slab_mid, 2))
    in_terms = send_ctx(order.then(scatter_ctx(dam, order(in_got))))

    outputs = order.then((res_own + sum(t.astype(F32) for t in order(out_terms))).astype(BF16))
    grad_gate, grad_up = order.then(
        call(unpack_hidden_body, [sds((864, 128), F32), sds((864, 128), F32)], order(hid_sum), name="unpack_hidden")
    )
    slab = order.then(call(split_back_body, [sds((8, 40, BACK), BF16)], *order(slab_terms), name="split_back"))[0]
    slab = lax.all_to_all(slab, "ctx", 0, 0, tiled=True)
    input_grad = order.then(
        call(last_body, [sds((ROWS, W), BF16)], *late([*order(in_terms), x_own, dres]), gains, name="last")
    )[0]
    grad_q, grad_k, grad_v, grad_out, grad_gains = call(
        unpack_back_body,
        [sds((324, 128), F32), sds((108, 128), F32), sds((108, 128), F32), sds((324, 128), F32), sds((8, 128), F32)],
        order(slab), name="unpack_back",
    )
    grad_gains = grad_gains[0, :72]

    shape = (MICRO, 1, POS, W)
    return (
        outputs.reshape(shape),
        input_grad.reshape(shape),
        grad_q.reshape(-1),
        grad_k.reshape(-1),
        grad_v.reshape(-1),
        grad_out.reshape(-1),
        grad_gate.reshape(-1),
        grad_up.reshape(-1),
        grad_down.reshape(-1),
        grad_gains,
    )


def solution(mesh):
    in_specs = (
        P(None, "grp", "ctx", None),
        P(None, "grp", "ctx"),
        P(("grp", "ctx")),
        P(("grp", "ctx")),
        P(("grp", "ctx")),
        P(("grp", "ctx")),
        P(("grp", "ctx")),
        P(("grp", "ctx")),
        P(("grp", "ctx")),
        P(("grp", "ctx")),
        P(None, "grp", "ctx", None),
    )
    out_specs = (
        P(None, "grp", "ctx", None),
        P(None, "grp", "ctx", None),
        P(("grp", "ctx")),
        P(("grp", "ctx")),
        P(("grp", "ctx")),
        P(("grp", "ctx")),
        P(("grp", "ctx")),
        P(("grp", "ctx")),
        P(("grp", "ctx")),
        P(("grp", "ctx")),
    )
    fits = (mesh.shape["ctx"], mesh.shape["grp"]) == (8, 4)
    return jax.shard_map(
        fast_local if fits else local,
        mesh=mesh,
        in_specs=in_specs,
        out_specs=out_specs,
        check_vma=False,
    )
```

```python
import jax
import jax.numpy as jnp
from jax import lax
from jax.experimental import pallas as pl
from jax.experimental.pallas import tpu as pltpu
from jax.sharding import PartitionSpec as P

MODEL_WIDTH = 1152
QUERY_HEADS = 18
KEY_HEADS = 6
HEAD_SIZE = 64
HIDDEN_UNITS = 3072
MICRO = 2


EPS = 1e-05
THETA = 10000.0
NEGATIVE_LARGE = -1e30


def rope_parts(positions):
    half = HEAD_SIZE // 2
    freq = THETA ** (-jnp.arange(half, dtype=jnp.float32) * 2.0 / HEAD_SIZE)
    angle = positions.astype(jnp.float32)[:, None] * freq[None, :]
    return (jnp.cos(angle)[:, None, :], jnp.sin(angle)[:, None, :])


def rotary_apply(value_rows, cosine_table, sine_table, sign):
    half = value_rows.shape[-1] // 2
    first = value_rows[..., :half]
    second = value_rows[..., half:]
    return jnp.concatenate(
        [
            first * cosine_table - sign * second * sine_table,
            second * cosine_table + sign * first * sine_table,
        ],
        -1,
    )


def shape_weights(full_precision):
    return (
        full_precision[0].reshape(MODEL_WIDTH, QUERY_HEADS * HEAD_SIZE),
        full_precision[1].reshape(MODEL_WIDTH, KEY_HEADS * HEAD_SIZE),
        full_precision[2].reshape(MODEL_WIDTH, KEY_HEADS * HEAD_SIZE),
        full_precision[3].reshape(QUERY_HEADS * HEAD_SIZE, MODEL_WIDTH),
        full_precision[4].reshape(MODEL_WIDTH, HIDDEN_UNITS),
        full_precision[5].reshape(MODEL_WIDTH, HIDDEN_UNITS),
        full_precision[6].reshape(HIDDEN_UNITS, MODEL_WIDTH),
        full_precision[7],
    )


def allowed(key_pos, key_seg, query_pos, query_seg):
    return (key_pos[None, :] <= query_pos[:, None]) & (key_seg[None, :] == query_seg[:, None])


def online_step(
    state, grouped_queries, key_block, value_block, pblock, sblock, query_pos, query_seg
):
    best, total, accum = state
    block_span = key_block.shape[0]
    key_head_rows = key_block.reshape(block_span, KEY_HEADS, HEAD_SIZE)
    value_head_rows = value_block.reshape(block_span, KEY_HEADS, HEAD_SIZE)
    scores = jnp.einsum(
        "tkgd,nkd->kgtn", grouped_queries, key_head_rows, preferred_element_type=jnp.float32
    ) * HEAD_SIZE ** (-0.5)
    mask = allowed(pblock, sblock, query_pos, query_seg)[None, None]
    scores = jnp.where(mask, scores, NEGATIVE_LARGE)
    new_best = jnp.maximum(best, jnp.max(scores, axis=-1))
    factor = jnp.exp(best - new_best)
    expo = jnp.where(mask, jnp.exp(scores - new_best[..., None]), 0.0)
    total = total * factor + jnp.sum(expo, axis=-1)
    accum = accum * factor[..., None] + jnp.einsum(
        "kgtn,nkd->kgtd",
        expo.astype(jnp.bfloat16),
        value_head_rows,
        preferred_element_type=jnp.float32,
    )
    return (new_best, total, accum)


def guarded_step(
    state, grouped_queries, key_block, value_block, pblock, sblock, query_pos, query_seg
):

    def guarded_work(current):
        return online_step(
            current, grouped_queries, key_block, value_block, pblock, sblock, query_pos, query_seg
        )

    def guarded_leave(current):
        return current

    return lax.cond(pblock[0] <= query_pos[-1], guarded_work, guarded_leave, state)


def online_blocks(
    carry, grouped_queries, key_rows, value_rows, key_pos, key_seg, query_pos, query_seg
):
    count = key_rows.shape[0]
    block_size = 512 if count > 512 and count % 512 == 0 else count
    if block_size == count:
        return guarded_step(
            carry, grouped_queries, key_rows, value_rows, key_pos, key_seg, query_pos, query_seg
        )

    def step(state, block_tile):
        return (
            guarded_step(
                state,
                grouped_queries,
                block_tile[0],
                block_tile[1],
                block_tile[2],
                block_tile[3],
                query_pos,
                query_seg,
            ),
            None,
        )

    block_tiles = (
        key_rows.reshape(-1, block_size, key_rows.shape[1]),
        value_rows.reshape(-1, block_size, value_rows.shape[1]),
        key_pos.reshape(-1, block_size),
        key_seg.reshape(-1, block_size),
    )
    carry, _ = lax.scan(step, carry, block_tiles)
    return carry


def forward_rows(xrow, seg_row, query_seg, positions, cosine_table, sine_table, weight_matrices):
    (
        query_weight,
        key_weight,
        value_weight,
        output_weight,
        gate_weight,
        up_weight,
        down_weight,
        gains,
    ) = weight_matrices
    token_rows = xrow.shape[0]
    query_groups = QUERY_HEADS // KEY_HEADS
    gain_one = gains[:MODEL_WIDTH].astype(jnp.float32)
    gain_two = gains[MODEL_WIDTH:].astype(jnp.float32)
    inv_one = lax.rsqrt(jnp.mean(xrow * xrow, axis=-1, keepdims=True) + EPS)
    normed_one = xrow * inv_one
    activated_hidden = (normed_one * gain_one).astype(jnp.bfloat16)
    query_unrotated = jnp.dot(
        activated_hidden, query_weight, preferred_element_type=jnp.float32
    ).reshape(token_rows, QUERY_HEADS, HEAD_SIZE)
    key_unrotated = jnp.dot(
        activated_hidden, key_weight, preferred_element_type=jnp.float32
    ).reshape(token_rows, KEY_HEADS, HEAD_SIZE)
    value_raw = jnp.dot(activated_hidden, value_weight, preferred_element_type=jnp.float32)
    grouped_queries = (
        rotary_apply(query_unrotated, cosine_table, sine_table, 1.0)
        .astype(jnp.bfloat16)
        .reshape(token_rows, KEY_HEADS, query_groups, HEAD_SIZE)
    )
    key_rows = (
        rotary_apply(key_unrotated, cosine_table, sine_table, 1.0)
        .astype(jnp.bfloat16)
        .reshape(token_rows, KEY_HEADS * HEAD_SIZE)
    )
    value_rows = value_raw.astype(jnp.bfloat16)
    start_state = (
        jnp.full((KEY_HEADS, query_groups, token_rows), NEGATIVE_LARGE, jnp.float32),
        jnp.zeros((KEY_HEADS, query_groups, token_rows), jnp.float32),
        jnp.zeros((KEY_HEADS, query_groups, token_rows, HEAD_SIZE), jnp.float32),
    )
    piece = (
        lax.all_gather(key_rows, "ctx", axis=0, tiled=True),
        lax.all_gather(value_rows, "ctx", axis=0, tiled=True),
    )
    count = piece[0].shape[0]
    key_pos = jnp.arange(count, dtype=jnp.int32)
    best, total, accum = online_blocks(
        start_state, grouped_queries, piece[0], piece[1], key_pos, seg_row, positions, query_seg
    )
    attn = accum / total[..., None]
    lse = best + jnp.log(total)
    attn_low = (
        jnp.transpose(attn, (2, 0, 1, 3))
        .reshape(token_rows, QUERY_HEADS * HEAD_SIZE)
        .astype(jnp.bfloat16)
    )
    residual = xrow + jnp.dot(attn_low, output_weight, preferred_element_type=jnp.float32)
    inv_two = lax.rsqrt(jnp.mean(residual * residual, axis=-1, keepdims=True) + EPS)
    normed_two = residual * inv_two
    mixed = (normed_two * gain_two).astype(jnp.bfloat16)
    gate = jnp.dot(mixed, gate_weight, preferred_element_type=jnp.float32)
    upper = jnp.dot(mixed, up_weight, preferred_element_type=jnp.float32)
    hidden = (jax.nn.silu(gate) * upper).astype(jnp.bfloat16)
    result = residual + jnp.dot(hidden, down_weight, preferred_element_type=jnp.float32)
    kept = (
        inv_one,
        normed_one,
        activated_hidden,
        grouped_queries,
        key_rows,
        value_rows,
        attn,
        lse,
        attn_low,
        inv_two,
        normed_two,
        mixed,
        gate,
        upper,
        hidden,
    )
    return (result, kept)


def backward_rows(
    dout, seg_row, query_seg, positions, cosine_table, sine_table, weight_matrices, kept
):
    (
        query_weight,
        key_weight,
        value_weight,
        output_weight,
        gate_weight,
        up_weight,
        down_weight,
        gains,
    ) = weight_matrices
    (
        inv_one,
        normed_one,
        activated_hidden,
        grouped_queries,
        key_rows,
        value_rows,
        attn,
        lse,
        attn_low,
        inv_two,
        normed_two,
        mixed,
        gate,
        upper,
        hidden,
    ) = kept
    token_rows = dout.shape[0]
    query_groups = QUERY_HEADS // KEY_HEADS
    scale = HEAD_SIZE ** (-0.5)
    gain_one = gains[:MODEL_WIDTH].astype(jnp.float32)
    gain_two = gains[MODEL_WIDTH:].astype(jnp.float32)
    dout_low = dout.astype(jnp.bfloat16)
    grad_down = jnp.einsum("tf,td->fd", hidden, dout_low, preferred_element_type=jnp.float32)
    grad_hidden = jnp.einsum("td,fd->tf", dout_low, down_weight, preferred_element_type=jnp.float32)
    sigma = jax.nn.sigmoid(gate)
    grad_gate_act = (grad_hidden * upper * (sigma + gate * sigma * (1.0 - sigma))).astype(
        jnp.bfloat16
    )
    grad_up_act = (grad_hidden * (gate * sigma)).astype(jnp.bfloat16)
    grad_gate = jnp.einsum("te,tf->ef", mixed, grad_gate_act, preferred_element_type=jnp.float32)
    grad_up = jnp.einsum("te,tf->ef", mixed, grad_up_act, preferred_element_type=jnp.float32)
    grad_mixed = jnp.einsum(
        "tf,ef->te", grad_gate_act, gate_weight, preferred_element_type=jnp.float32
    ) + jnp.einsum("tf,ef->te", grad_up_act, up_weight, preferred_element_type=jnp.float32)
    grad_gain_two = jnp.sum(grad_mixed * normed_two, axis=0)
    scaled_two = grad_mixed * gain_two
    grad_res = dout + inv_two * (
        scaled_two - normed_two * jnp.mean(scaled_two * normed_two, axis=-1, keepdims=True)
    )
    grad_branch = grad_res.astype(jnp.bfloat16)
    grad_output = jnp.einsum("te,td->ed", attn_low, grad_branch, preferred_element_type=jnp.float32)
    attention_gradient = jnp.einsum(
        "td,ed->te", grad_branch, output_weight, preferred_element_type=jnp.float32
    )
    attention_gradient_reduced = attention_gradient.astype(jnp.bfloat16).reshape(
        token_rows, KEY_HEADS, query_groups, HEAD_SIZE
    )
    delta = jnp.einsum("tkgd,kgtd->kgt", attention_gradient_reduced.astype(jnp.float32), attn)
    key_rows_total, value_rows_total = (
        lax.all_gather(key_rows, "ctx", axis=0, tiled=True),
        lax.all_gather(value_rows, "ctx", axis=0, tiled=True),
    )
    token_length = key_rows_total.shape[0]
    block_size = min(512, token_length)

    def reverse_block_step(grad_query, block_tile):
        key_block, value_block, pblock, sblock = block_tile

        def reverse_work(current):
            key_head_rows = key_block.reshape(block_size, KEY_HEADS, HEAD_SIZE)
            value_head_rows = value_block.reshape(block_size, KEY_HEADS, HEAD_SIZE)
            scores = (
                jnp.einsum(
                    "tkgd,nkd->kgtn",
                    grouped_queries,
                    key_head_rows,
                    preferred_element_type=jnp.float32,
                )
                * scale
            )
            mask = allowed(pblock, sblock, positions, query_seg)[None, None]
            probs = jnp.where(mask, jnp.exp(scores - lse[..., None]), 0.0)
            grad_probs = jnp.einsum(
                "tkgd,nkd->kgtn",
                attention_gradient_reduced,
                value_head_rows,
                preferred_element_type=jnp.float32,
            )
            grad_scores = (probs * (grad_probs - delta[..., None])).astype(jnp.bfloat16)
            updated_state = current + jnp.einsum(
                "kgtn,nkd->tkgd", grad_scores, key_head_rows, preferred_element_type=jnp.float32
            )
            key_gradient_term = (
                jnp.einsum(
                    "kgtn,tkgd->nkd",
                    grad_scores,
                    grouped_queries,
                    preferred_element_type=jnp.float32,
                )
                * scale
            )
            value_gradient_term = jnp.einsum(
                "kgtn,tkgd->nkd",
                probs.astype(jnp.bfloat16),
                attention_gradient_reduced,
                preferred_element_type=jnp.float32,
            )
            return (
                updated_state,
                (
                    key_gradient_term.reshape(block_size, KEY_HEADS * HEAD_SIZE),
                    value_gradient_term.reshape(block_size, KEY_HEADS * HEAD_SIZE),
                ),
            )

        def reverse_leave(current):
            empty_state = jnp.zeros((block_size, KEY_HEADS * HEAD_SIZE), jnp.float32)
            return (current, (empty_state, empty_state))

        return lax.cond(pblock[0] <= positions[-1], reverse_work, reverse_leave, grad_query)

    places = jnp.arange(token_length, dtype=jnp.int32)
    block_tiles = (
        key_rows_total.reshape(-1, block_size, KEY_HEADS * HEAD_SIZE),
        value_rows_total.reshape(-1, block_size, KEY_HEADS * HEAD_SIZE),
        places.reshape(-1, block_size),
        seg_row.reshape(-1, block_size),
    )
    grad_query_rot, (key_gradient_terms, value_gradient_terms) = lax.scan(
        reverse_block_step,
        jnp.zeros((token_rows, KEY_HEADS, query_groups, HEAD_SIZE), jnp.float32),
        block_tiles,
    )
    key_gradient_rows, grad_values = (
        lax.psum_scatter(
            key_gradient_terms.reshape(token_length, KEY_HEADS * HEAD_SIZE),
            "ctx",
            scatter_dimension=0,
            tiled=True,
        ),
        lax.psum_scatter(
            value_gradient_terms.reshape(token_length, KEY_HEADS * HEAD_SIZE),
            "ctx",
            scatter_dimension=0,
            tiled=True,
        ),
    )
    grad_q_low = (
        rotary_apply(
            (grad_query_rot * scale).reshape(token_rows, QUERY_HEADS, HEAD_SIZE),
            cosine_table,
            sine_table,
            -1.0,
        )
        .astype(jnp.bfloat16)
        .reshape(token_rows, QUERY_HEADS * HEAD_SIZE)
    )
    grad_k_low = (
        rotary_apply(
            key_gradient_rows.reshape(token_rows, KEY_HEADS, HEAD_SIZE),
            cosine_table,
            sine_table,
            -1.0,
        )
        .astype(jnp.bfloat16)
        .reshape(token_rows, KEY_HEADS * HEAD_SIZE)
    )
    grad_v_low = grad_values.astype(jnp.bfloat16)
    grad_wq = jnp.einsum(
        "te,tf->ef", activated_hidden, grad_q_low, preferred_element_type=jnp.float32
    )
    grad_wk = jnp.einsum(
        "te,tf->ef", activated_hidden, grad_k_low, preferred_element_type=jnp.float32
    )
    grad_wv = jnp.einsum(
        "te,tf->ef", activated_hidden, grad_v_low, preferred_element_type=jnp.float32
    )
    grad_acted = jnp.einsum(
        "tf,ef->te", grad_q_low, query_weight, preferred_element_type=jnp.float32
    )
    grad_acted = grad_acted + jnp.einsum(
        "tf,ef->te", grad_k_low, key_weight, preferred_element_type=jnp.float32
    )
    grad_acted = grad_acted + jnp.einsum(
        "tf,ef->te", grad_v_low, value_weight, preferred_element_type=jnp.float32
    )
    grad_gain_one = jnp.sum(grad_acted * normed_one, axis=0)
    scaled_one = grad_acted * gain_one
    grad_input = grad_res + inv_one * (
        scaled_one - normed_one * jnp.mean(scaled_one * normed_one, axis=-1, keepdims=True)
    )
    terms = [
        grad_wq.reshape(-1),
        grad_wk.reshape(-1),
        grad_wv.reshape(-1),
        grad_output.reshape(-1),
        grad_gate.reshape(-1),
        grad_up.reshape(-1),
        grad_down.reshape(-1),
        jnp.concatenate([grad_gain_one, grad_gain_two]),
    ]
    return (grad_input.astype(jnp.bfloat16), terms)


def local(
    inputs,
    segments,
    query_weight,
    key_weight,
    value_weight,
    output_weight,
    gate_weight,
    up_weight,
    down_weight,
    norm_gain_pair,
    cotangent,
):
    shard_rows = inputs.shape[2]
    seg_full = lax.all_gather(segments, "ctx", axis=2, tiled=True)
    positions = lax.axis_index("ctx") * shard_rows + jnp.arange(shard_rows, dtype=jnp.int32)
    cosine_table, sine_table = rope_parts(positions)
    weight_matrices = shape_weights(
        (
            lax.all_gather(query_weight, ("grp", "ctx"), axis=0, tiled=True),
            lax.all_gather(key_weight, ("grp", "ctx"), axis=0, tiled=True),
            lax.all_gather(value_weight, ("grp", "ctx"), axis=0, tiled=True),
            lax.all_gather(output_weight, ("grp", "ctx"), axis=0, tiled=True),
            lax.all_gather(gate_weight, ("grp", "ctx"), axis=0, tiled=True),
            lax.all_gather(up_weight, ("grp", "ctx"), axis=0, tiled=True),
            lax.all_gather(down_weight, ("grp", "ctx"), axis=0, tiled=True),
            lax.all_gather(norm_gain_pair, ("grp", "ctx"), axis=0, tiled=True),
        )
    )
    results = []
    saved = []
    for micro_step in range(MICRO):
        xrow = inputs[micro_step, 0].astype(jnp.float32)
        result, kept = forward_rows(
            xrow,
            seg_full[micro_step, 0],
            segments[micro_step, 0],
            positions,
            cosine_table,
            sine_table,
            weight_matrices,
        )
        results.append(result.astype(jnp.bfloat16))
        saved.append(kept)
    mats_back = shape_weights(
        (
            lax.all_gather(query_weight, ("grp", "ctx"), axis=0, tiled=True),
            lax.all_gather(key_weight, ("grp", "ctx"), axis=0, tiled=True),
            lax.all_gather(value_weight, ("grp", "ctx"), axis=0, tiled=True),
            lax.all_gather(output_weight, ("grp", "ctx"), axis=0, tiled=True),
            lax.all_gather(gate_weight, ("grp", "ctx"), axis=0, tiled=True),
            lax.all_gather(up_weight, ("grp", "ctx"), axis=0, tiled=True),
            lax.all_gather(down_weight, ("grp", "ctx"), axis=0, tiled=True),
            lax.all_gather(norm_gain_pair, ("grp", "ctx"), axis=0, tiled=True),
        )
    )
    input_grads = []
    shares = None
    totals = None
    for micro_step in range(MICRO):
        dout = cotangent[micro_step, 0].astype(jnp.float32)
        grad_input, terms = backward_rows(
            dout,
            seg_full[micro_step, 0],
            segments[micro_step, 0],
            positions,
            cosine_table,
            sine_table,
            mats_back,
            saved[micro_step],
        )
        input_grads.append(grad_input)
        totals = terms if totals is None else [a + b for a, b in zip(totals, terms)]
    shares = list(
        (
            lax.psum_scatter(totals[0], ("grp", "ctx"), scatter_dimension=0, tiled=True),
            lax.psum_scatter(totals[1], ("grp", "ctx"), scatter_dimension=0, tiled=True),
            lax.psum_scatter(totals[2], ("grp", "ctx"), scatter_dimension=0, tiled=True),
            lax.psum_scatter(totals[3], ("grp", "ctx"), scatter_dimension=0, tiled=True),
            lax.psum_scatter(totals[4], ("grp", "ctx"), scatter_dimension=0, tiled=True),
            lax.psum_scatter(totals[5], ("grp", "ctx"), scatter_dimension=0, tiled=True),
            lax.psum_scatter(totals[6], ("grp", "ctx"), scatter_dimension=0, tiled=True),
            lax.psum_scatter(totals[7], ("grp", "ctx"), scatter_dimension=0, tiled=True),
        )
    )
    outputs = jnp.stack(results)[:, None]
    input_grad = jnp.stack(input_grads)[:, None]
    return (
        outputs,
        input_grad,
        shares[0],
        shares[1],
        shares[2],
        shares[3],
        shares[4],
        shares[5],
        shares[6],
        shares[7],
    )


W = MODEL_WIDTH
HG = QUERY_HEADS // KEY_HEADS * HEAD_SIZE
QK = HG + HEAD_SIZE
SLAB = 384
QKV = HG + 2 * HEAD_SIZE
OUT = W // 8
BACK = 512
FEED = 432
EDGE = 304
CHUNK = W // 32
HID = HIDDEN_UNITS // 8
SUB = HIDDEN_UNITS // 32
ROWS = 128
ALL = 8 * ROWS
POS = 64
LEN = 512
RELATIVE = (0, 2, 4, 6, 1, 3, 5, 7)
STEP = 512
STEPS = ALL // STEP
F32 = jnp.float32
BF16 = jnp.bfloat16
SCALE = HEAD_SIZE ** (-0.5)
NT = (((1,), (1,)), ((), ()))
TN = (((0,), (0,)), ((), ()))
MIB = 1024 * 1024
LARGE = ("attend", "project", "feed", "back")


def pc(value, k):
    return lax.ppermute(value, "ctx", [(s, s ^ k) for s in range(8)])


def pz(value, k):
    return lax.ppermute(value, "grp", [(s, s ^ k) for s in range(4)])


def after(value, *others):
    return lax.optimization_barrier((value,) + others)[0]


def first_ctx(value):
    far = pc(value, 6)
    return [value, pc(value, 2), pc(value, 4), far]


def both_cores(mine):
    return mine + [pc(m, 1) for m in mine]


def gather_ctx(value):
    return both_cores(first_ctx(value))


def gather_grp(value):
    one = pz(value, 1)
    two = pz(value, 2)
    return (value, one, two, pz(two, 1))


def add_low(a, b):
    return (a.astype(F32) + b.astype(F32)).astype(BF16)


class Order:
    def __init__(self):
        self.last = None

    def __call__(self, values):
        return values if self.last is None else after(values, self.last)

    def then(self, result):
        self.last = jax.tree.leaves(result)[-1]
        return result

    def wait(self, values):
        return self.then(self(values))


def scatter_ctx(even, got):
    return [add_low(even[k], got[k]) for k in range(4)]


def send_ctx(sums):
    far = pc(sums[3], 6)
    return sums[0], pc(sums[1], 2), pc(sums[2], 4), far


def pick(blocks, g):
    return [lax.dynamic_index_in_dim(blocks, g ^ k, 0, keepdims=False) for k in range(4)]


def call(body, outs, *args, grid=None, in_specs=None, out_specs=None, scratch=(), name=None):
    kwargs = {}
    if grid is not None:
        kwargs = dict(grid=grid, in_specs=in_specs, out_specs=out_specs)
    else:
        kwargs = dict(
            in_specs=[
                pl.BlockSpec(memory_space=pltpu.SMEM)
                if a.dtype == jnp.int32 and a.ndim == 1
                else pl.BlockSpec(memory_space=pltpu.VMEM)
                for a in args
            ],
            out_specs=out_specs or [pl.BlockSpec(memory_space=pltpu.VMEM) for _ in outs],
        )
    return pl.pallas_call(
        body,
        out_shape=outs,
        scratch_shapes=scratch,
        compiler_params=pltpu.CompilerParams(vmem_limit_bytes=(32 if name in LARGE else 16) * MIB),
        cost_estimate=pl.CostEstimate(flops=0, bytes_accessed=1, transcendentals=0),
        name=name,
        **kwargs,
    )(*args)


def late(values):
    return [pltpu.with_memory_space_constraint(v, pltpu.HBM) for v in values]


def hbm(shape, dtype):
    return pltpu.HBM(shape, dtype)


def hbm(shape, dtype):
    return pltpu.HBM(shape, dtype)


def hbm(shape, dtype):
    return pltpu.HBM(shape, dtype)


def sds(shape, dtype):
    return jax.ShapeDtypeStruct(shape, dtype)


def rows_of(ref, count):
    wide = ref.shape[0] // count
    return jnp.concatenate([ref[pl.ds(n, count, stride=wide), :] for n in range(wide)], 1)


def store_rows(ref, rows):
    count = rows.shape[0]
    wide = ref.shape[0] // count
    for n in range(wide):
        ref[pl.ds(n, count, stride=wide), :] = rows[:, n * 128 : (n + 1) * 128]


def pack_body(q_r, k_r, v_r, gate_r, up_r, gain, out, sq, sk, sv, sg, su):
    for src, dst in ((q_r, sq), (k_r, sk), (v_r, sv), (gate_r, sg), (up_r, su)):
        dst[...] = src[...].astype(F32)
    q, k, v, gate, up = (rows_of(s, CHUNK) for s in (sq, sk, sv, sg, su))
    tail = jnp.concatenate([gain[:, n * SLAB : (n + 1) * SLAB] for n in range(3)], 0).astype(F32)
    tail = jnp.concatenate([tail, jnp.zeros((1, SLAB), F32)], 0)
    for h in range(8):
        if h < KEY_HEADS:
            rows = jnp.concatenate(
                [
                    q[:, h * HG : (h + 1) * HG],
                    k[:, h * HEAD_SIZE : (h + 1) * HEAD_SIZE],
                    v[:, h * HEAD_SIZE : (h + 1) * HEAD_SIZE],
                    jnp.zeros((CHUNK, SLAB - QKV), F32),
                ],
                1,
            )
        else:
            rows = jnp.zeros((CHUNK, SLAB), F32)
        out[h, :, :SLAB] = jnp.concatenate([rows, tail], 0).astype(BF16)
        parts = [
            full[:, z * 768 + h * SUB : z * 768 + (h + 1) * SUB] for full in (gate, up) for z in range(4)
        ]
        rows = jnp.concatenate([jnp.concatenate(parts, 1), jnp.zeros((4, 2 * HID), F32)], 0)
        out[h, :, SLAB:] = rows.astype(BF16)


def unpack_body(src, slab, feed):
    for h in range(8):
        slab[h] = src[h, :, :SLAB]
    feed[...] = jnp.concatenate([src[h, :CHUNK, SLAB:].astype(F32) for h in range(8)], 0).astype(BF16)


def join_body(*refs):
    for n, block in enumerate(refs[:8]):
        refs[8][n * ROWS : (n + 1) * ROWS, :] = block[...]


def join(blocks):
    return call(join_body, [sds((ALL, W), BF16)], *blocks, name="join")[0]


def output_weight_body(sc, b0, b1, b2, b3, b4, b5, b6, b7, out, rows):
    i, g = sc[0], sc[1]
    for j, b in zip(RELATIVE, (b0, b1, b2, b3, b4, b5, b6, b7)):
        for k in range(4):
            rows[i ^ j, g ^ k] = b[k].astype(F32)
    for z in range(4):
        for q in range(2):
            parts = [rows_of(rows.at[c, z], CHUNK) for c in range(4 * q, 4 * q + 4)]
            start = z * 288 + q * 144
            out[start : start + 144, :] = jnp.concatenate(parts, 0).astype(BF16)


def rotate(x, cosine, sine, sign):
    lane = lax.broadcasted_iota(jnp.int32, (1, 128), 1) % HEAD_SIZE
    first = lane < HEAD_SIZE // 2
    halves = []
    for n in range(x.shape[1] // 128):
        part = x[:, n * 128 : (n + 1) * 128]
        swapped = jnp.where(first, pltpu.roll(part, 96, 1), pltpu.roll(part, 32, 1))
        halves.append(part * cosine + sign * (swapped * sine))
    return jnp.concatenate(halves, 1)


def attend_body(
    sc, x0, x1, x2, x3, x4, x5, x6, x7, w0, w1, w2, w3, cosine, sine, pcol, prow,
    att, gains, w_o, qk_h, v_h, acted_h, probs_h, x_h, qk_o, v_o, acted, probs, x_o, segs, held, sems,
):
    xs = (x0, x1, x2, x3, x4, x5, x6, x7)
    g = sc[1]
    copies = []

    def send(src, dst):
        copy = pltpu.make_async_copy(src, dst, sems.at[len(copies)])
        copy.start()
        copies.append(copy)

    sums = [jnp.zeros((3, SLAB), F32), jnp.zeros((3, SLAB), F32)]
    for k, w in enumerate((w0, w1, w2, w3)):
        z = g ^ k
        block = jnp.concatenate([w[h, :CHUNK, :].astype(F32) for h in range(8)], 0)
        w_o[pl.ds(pl.multiple_of(z * 288, 32), 288), :] = block.astype(BF16)
        rows = sum(w[h, CHUNK : CHUNK + 3, :].astype(F32) for h in range(8))
        sums[0] = sums[0] + jnp.where(z < 2, rows, 0.0)
        sums[1] = sums[1] + jnp.where(z < 2, 0.0, rows)
    gain = [jnp.concatenate([s[0:1], s[1:2], s[2:3]], 1) for s in sums]
    gains[...] = jnp.concatenate([gain[0], gain[1], jnp.zeros((6, W), F32)], 0)
    for b in range(8):
        x_o[b * ROWS : (b + 1) * ROWS, :] = xs[b][:, :W]
        segs[b] = xs[b][:, W:]

    @pl.loop(0, 8)
    def _(b):
        at = pl.ds(pl.multiple_of(b * ROWS, ROWS), ROWS)
        x = x_o[at, :].astype(F32)
        inv = lax.rsqrt(jnp.mean(x * x, axis=-1, keepdims=True) + EPS)
        acted[at, :] = (x * inv * gain[0]).astype(BF16)

    send(x_o, x_h)
    send(acted, acted_h)

    @pl.loop(0, MICRO)
    def _(m):
        part = pl.ds(pl.multiple_of(m * POS, POS), POS)
        rows = jnp.concatenate(
            [acted[pl.ds(pl.multiple_of(b * ROWS + m * POS, POS), POS), :] for b in range(8)], 0
        )
        seg = jnp.concatenate([segs[b, part, :].astype(F32) for b in range(8)], 0)
        y = jnp.dot(rows, w_o[...], preferred_element_type=F32)
        qk = rotate(y[:, :QK], cosine[...], sine[...], 1.0).astype(BF16)
        v = y[:, QK:].astype(BF16)
        qk_o[m] = qk
        v_o[m] = v
        seg_row = jnp.transpose(seg)[0:1, :]
        mask = (prow[0:1, :] <= pcol[:, 0:1]) & (seg_row == seg[:, 0:1])
        bias = jnp.where(mask, 0.0, NEGATIVE_LARGE)
        keys = qk[:, HG:]
        for h in range(3):
            s = lax.dot_general(
                qk[:, h * HEAD_SIZE : (h + 1) * HEAD_SIZE], keys, NT, preferred_element_type=F32
            )
            s = s * SCALE + bias
            e = jnp.exp(s - jnp.max(s, axis=-1, keepdims=True))
            p = (e * (1.0 / jnp.sum(e, axis=-1, keepdims=True))).astype(BF16)
            probs[m, h] = p
            held[m, :, h * HEAD_SIZE : (h + 1) * HEAD_SIZE] = jnp.dot(
                p, v[:, :HEAD_SIZE], preferred_element_type=F32
            ).astype(BF16)

    for m in range(MICRO):
        att[:, m * HG : (m + 1) * HG] = held[m]
    send(probs, probs_h)
    send(qk_o, qk_h)
    send(v_o, v_h)
    for copy in copies:
        copy.wait()


def project_body(sc, x, a0, a1, a2, a3, a4, a5, a6, a7, wo, gains, att_o, mixed_o, res_o, heads):
    i = sc[0]
    t = pl.program_id(0)
    for j, a in zip(RELATIVE, (a0, a1, a2, a3, a4, a5, a6, a7)):
        h = i ^ j
        for half in range(STEP // ROWS):
            b = STEP // ROWS * t + half
            q = (2 * (b & 3) + (b >> 2)) ^ j
            start = pl.multiple_of(((q & 1) * 4 + (q >> 1)) * POS, POS)
            rows = a[pl.ds(start, POS), :]
            for m in range(MICRO):
                heads[h, half * ROWS + m * POS : half * ROWS + (m + 1) * POS, :] = rows[:, m * HG : (m + 1) * HG]
    for h in range(KEY_HEADS):
        att_o[:, h * HG : (h + 1) * HG] = heads[h]
    residual = x[...].astype(F32) + jnp.dot(att_o[...], wo[...], preferred_element_type=F32)

    @pl.when(t == 0)
    def _():
        res_o[...] = residual[:ROWS]

    inv = lax.rsqrt(jnp.mean(residual * residual, axis=-1, keepdims=True) + EPS)
    mixed_o[...] = (residual * inv * gains[1:2, :]).astype(BF16)


def feed_body(
    sc, mixed_r, c, g0, g1, g2, g3, d0, d1, d2, d3, hidden_o, dgu_o, pm, pe, dn, sums, gu
):
    g = sc[1]
    t = pl.program_id(0)

    @pl.when(t == 0)
    def _():
        for k, (a, d) in enumerate(((g0, d0), (g1, d1), (g2, d2), (g3, d3))):
            z = g ^ k
            gu[pl.ds(pl.multiple_of(z * 288, 32), 288), :] = a[...]
            dn[pl.ds(pl.multiple_of(z * SUB, 32), SUB), :] = d[...]
        sums[...] = jnp.zeros((8, W), F32)

    mixed = mixed_r[...]
    y = jnp.dot(mixed, gu[...], preferred_element_type=F32)
    gate = y[:, :HID]
    up = y[:, HID:]
    sig = 1.0 / (1.0 + jnp.exp(-gate))
    silu = gate * sig
    hidden_o[...] = (silu * up).astype(BF16)
    dh = lax.dot_general(c[...], dn[...], NT, preferred_element_type=F32)
    dgate = (dh * up * (sig + silu * (1.0 - sig))).astype(BF16)
    dup = (dh * silu).astype(BF16)
    dgu = jnp.concatenate([dgate, dup], 1)
    dgu_o[...] = dgu
    dm = lax.dot_general(dgu, gu[...], NT, preferred_element_type=F32)
    sums[0:1, :] = sums[0:1, :] + jnp.sum(dm * mixed.astype(F32), axis=0, keepdims=True)
    dm = dm.astype(BF16).reshape(4, ROWS, W)

    @pl.when(t == 0)
    def _():
        pm[...] = dm

    @pl.when(t == 1)
    def _():
        pe[...] = dm


def whole(*shape):
    return pl.BlockSpec(shape, lambda t: (0,) * len(shape))


def rows_at(rows, columns):
    return pl.BlockSpec((rows, columns), lambda t: (t, 0))


def run_project(sc, x, heads, w_out, gains):
    return call(
        project_body,
        [hbm((ALL, W), BF16), sds((ALL, W), BF16), hbm((ROWS, W), F32)],
        sc, x, *heads, w_out, gains,
        grid=(STEPS,),
        in_specs=[pl.BlockSpec(memory_space=pltpu.SMEM), rows_at(STEP, W)]
        + [whole(LEN, 2 * HG)] * 8
        + [whole(W, W), whole(8, W)],
        out_specs=[rows_at(STEP, W), rows_at(STEP, W), whole(ROWS, W)],
        scratch=[pltpu.VMEM((8, STEP, HG), BF16)], name="project",
    )


def run_feed(sc, mixed, c, feeds):
    return call(
        feed_body,
        [
            sds((ALL, HID), BF16),
            sds((ALL, 2 * HID), BF16),
            sds((4, ROWS, W), BF16),
            sds((4, ROWS, W), BF16),
            sds((HID, W), BF16),
            sds((8, W), F32),
        ],
        sc, mixed, c, *feeds,
        grid=(STEPS,),
        in_specs=[pl.BlockSpec(memory_space=pltpu.SMEM), rows_at(STEP, W), rows_at(STEP, W)]
        + [whole(288, 2 * HID)] * 4
        + [whole(SUB, W)] * 4,
        out_specs=[
            rows_at(STEP, HID),
            rows_at(STEP, 2 * HID),
            whole(4, ROWS, W),
            whole(4, ROWS, W),
            whole(HID, W),
            whole(8, W),
        ],
        scratch=[pltpu.VMEM((W, 2 * HID), BF16)], name="feed",
    )


def mid_body(a, b, d, f, c, res, gains, dres, low):
    dm = a[...].astype(F32) + b[...].astype(F32) + d[...].astype(F32) + f[...].astype(F32)
    r = res[...]
    inv = lax.rsqrt(jnp.mean(r * r, axis=-1, keepdims=True) + EPS)
    n = r * inv
    e = dm * gains[1:2, :]
    out = c[...].astype(F32) + inv * (e - n * jnp.mean(e * n, axis=-1, keepdims=True))
    dres[...] = out
    low[...] = out.astype(BF16)


def last_body(a, b, d, f, x, dres, gains, out):
    da = a[...].astype(F32) + b[...].astype(F32) + d[...].astype(F32) + f[...].astype(F32)
    r = x[...].astype(F32)
    inv = lax.rsqrt(jnp.mean(r * r, axis=-1, keepdims=True) + EPS)
    n = r * inv
    e = da * gains[0:1, :]
    out[...] = (dres[...] + inv * (e - n * jnp.mean(e * n, axis=-1, keepdims=True))).astype(BF16)


def back_body(
    sc, l0, l1, l2, l3, l4, l5, l6, l7, wo, qk_r, v_r, probs, cosine, sine, acted_t, att_t, w_slab, gains, sums,
    out, b0, b1, b2, b3, columns, dots, edge,
):
    lows = (l0, l1, l2, l3, l4, l5, l6, l7)
    i, g = sc[0], sc[1]
    place = lax.broadcasted_iota(jnp.int32, (256, W), 1) - lax.broadcasted_iota(jnp.int32, (256, W), 0)
    chosen = jnp.where(place == i * OUT, 1.0, 0.0).astype(BF16)
    @pl.loop(0, MICRO)
    def _(m):
        part = pl.ds(pl.multiple_of(m * POS, POS), POS)
        rows = jnp.concatenate([lows[b][part, :] for b in range(8)], 0)
        datt = lax.dot_general(rows, wo[...], NT, preferred_element_type=F32).astype(BF16)
        chosen_rows = lax.dot_general(rows, chosen, NT, preferred_element_type=F32).astype(BF16)
        qk = qk_r[m]
        keys = qk[:, HG:]
        v = v_r[m][:, :HEAD_SIZE]
        dq = []
        dk = jnp.zeros((HEAD_SIZE, LEN), F32)
        dv = jnp.zeros((HEAD_SIZE, LEN), F32)
        for h in range(3):
            da = datt[:, h * HEAD_SIZE : (h + 1) * HEAD_SIZE]
            q = qk[:, h * HEAD_SIZE : (h + 1) * HEAD_SIZE]
            low = probs[m, h]
            p = low.astype(F32)
            dp = lax.dot_general(da, v, NT, preferred_element_type=F32)
            delta = jnp.sum(p * dp, axis=-1, keepdims=True)
            ds = (p * (dp - delta)).astype(BF16)
            dq.append(jnp.dot(ds, keys, preferred_element_type=F32))
            dk = dk + lax.dot_general(q, ds, TN, preferred_element_type=F32)
            dv = dv + lax.dot_general(da, low, TN, preferred_element_type=F32)
        dqk = jnp.concatenate(dq + [jnp.transpose(dk)], 1) * SCALE
        dqk = rotate(dqk, cosine[...], sine[...], -1.0)
        dvt = jnp.transpose(jnp.concatenate([dv, jnp.zeros((HEAD_SIZE, LEN), F32)], 0))
        full = jnp.concatenate([dqk, dvt], 1).astype(BF16)
        for b in range(8):
            at = pl.ds(pl.multiple_of(b * ROWS + m * POS, POS), POS)
            out[at, :] = full[b * POS : (b + 1) * POS, :]
            columns[at, :] = chosen_rows[b * POS : (b + 1) * POS, :]

    blocks = (b0, b1, b2, b3)
    for k in range(4):
        z = g ^ k
        start = pl.multiple_of(z * 288, 32)
        y = jnp.dot(acted_t[pl.ds(start, 288), :], out[...], preferred_element_type=F32)
        yo = jnp.dot(att_t[pl.ds(start, 288), :], columns[...], preferred_element_type=F32)
        y2 = jnp.concatenate([y[:, :QKV], yo[:, : BACK - QKV]], 1)
        blocks[k][:288, :] = y2.astype(BF16)
        dot = jnp.sum(y * w_slab[pl.ds(start, 288), :].astype(F32), axis=-1, keepdims=True)
        dots[z] = jnp.transpose(jnp.broadcast_to(dot, (288, 128)))[:8, :]
    one = jnp.concatenate([dots[z][0:1, :] for z in range(4)], 1) / gains[0:1, :]
    two = sums[0:1, :] / gains[1:2, :]
    for z in range(4):
        full = one if z < 2 else two
        at = (z % 2) * 576
        rows = jnp.concatenate([full[:, at + 72 * c : at + 72 * (c + 1)] for c in range(8)], 0)
        rows = jnp.concatenate([rows, jnp.zeros((8, BACK - 72), F32)], 1)
        edge[z] = jnp.concatenate([rows, jnp.zeros((EDGE - 288 - 8, BACK), F32)], 0)
    for k in range(4):
        blocks[k][288:, :] = edge[g ^ k].astype(BF16)


def split_back_body(a, b, d, out):
    rows = a[...].astype(F32) + b[...].astype(F32) + d[...].astype(F32)
    for h in range(8):
        block = [rows[h * CHUNK : (h + 1) * CHUNK, :], rows[288 + h : 289 + h, :], jnp.zeros((3, BACK), F32)]
        out[h] = jnp.concatenate(block, 0).astype(BF16)


def grads_body(sc, grad_gu, grad_dn, b0, b1, b2, b3):
    g = sc[1]
    for k, block in enumerate((b0, b1, b2, b3)):
        z = g ^ k
        block[:288, :] = grad_gu[pl.ds(pl.multiple_of(z * 288, 32), 288), :]
        start = pl.multiple_of(z * SUB, 32)
        block[288 : 288 + SUB, :] = grad_dn[pl.ds(start, SUB), :768]
        block[288 + SUB :, :HID] = grad_dn[pl.ds(start, SUB // 2), 768:]
        block[288 + SUB :, HID:] = grad_dn[pl.ds(pl.multiple_of(start + SUB // 2, 16), SUB // 2), 768:]


def transpose_body(src, out):
    for n in range(ALL // 256):
        for m in range(W // 384):
            block = src[n * 256 : (n + 1) * 256, m * 384 : (m + 1) * 384]
            out[m * 384 : (m + 1) * 384, n * 256 : (n + 1) * 256] = jnp.transpose(block)


def transpose(value):
    return call(transpose_body, [sds((W, ALL), BF16)], value, name="transpose")[0]


def onward_body(rows, weight, even, odd):
    dims = NT if weight.shape[0] == W else (((1,), (0,)), ((), ()))
    for n in range(4):
        part = rows[n * 2 * ROWS : (n + 1) * 2 * ROWS, :]
        y = lax.dot_general(part, weight[...], dims, preferred_element_type=F32).astype(BF16)
        out = even if n < 2 else odd
        out[2 * (n % 2)] = y[:ROWS]
        out[2 * (n % 2) + 1] = y[ROWS:]


def onward(rows, weight, name):
    return call(onward_body, [sds((4, ROWS, W), BF16)] * 2, rows, weight, name=name)


def split_feed_body(a, b, d, out, down):
    rows = a[...].astype(F32) + b[...].astype(F32) + d[...].astype(F32)
    for h in range(8):
        out[h] = rows[h * CHUNK : (h + 1) * CHUNK, :].astype(BF16)
    right = jnp.concatenate([rows[288 + SUB :, :HID], rows[288 + SUB :, HID:]], 0)
    store_rows(down, jnp.concatenate([rows[288 : 288 + SUB, :], right], 1))


def split_back_body(a, b, d, out):
    rows = a[...].astype(F32) + b[...].astype(F32) + d[...].astype(F32)
    for h in range(8):
        block = [rows[h * CHUNK : (h + 1) * CHUNK, :], rows[288 + h : 289 + h, :], jnp.zeros((3, BACK), F32)]
        out[h] = jnp.concatenate(block, 0).astype(BF16)


def unpack_back_body(src, q, k, v, o, gains):
    parts = [src[h].astype(F32) for h in range(8)]
    rows = [p[:CHUNK, :] for p in parts]
    store_rows(q, jnp.concatenate([p[:, :HG] for p in rows[:KEY_HEADS]], 1))
    store_rows(k, jnp.concatenate([p[:, HG:QK] for p in rows[:KEY_HEADS]], 1))
    store_rows(v, jnp.concatenate([p[:, QK:QKV] for p in rows[:KEY_HEADS]], 1))
    store_rows(o, jnp.concatenate([p[:, QKV : QKV + OUT] for p in rows], 1))
    gains[...] = jnp.broadcast_to(sum(p[CHUNK : CHUNK + 1, :128] for p in parts), (8, 128))


def unpack_hidden_body(src, gate, up):
    for n, out in enumerate((gate, up)):
        parts = [
            src[h, :, n * HID + z * SUB : n * HID + (z + 1) * SUB].astype(F32)
            for z in range(4)
            for h in range(8)
        ]
        store_rows(out, jnp.concatenate(parts, 1))


def fast_local(inputs, segments, wq, wk, wv, wo, wg, wu, wd, gain_pair, cotangent):
    i = lax.axis_index("ctx").astype(jnp.int32)
    g = lax.axis_index("grp").astype(jnp.int32)
    r = g * 8 + i
    sc = jnp.stack([i, g])
    x_own = inputs.reshape(ROWS, W)
    c_own = cotangent.reshape(ROWS, W)
    order = Order()

    q2, k2, v2, gate2, up2 = (w.reshape(-1, 128) for w in (wq, wk, wv, wg, wu))
    placed = lax.dynamic_update_slice(jnp.zeros((1, W), BF16), gain_pair[None, :], (0, (r % 16) * 72))
    packed = order.then(
        call(
            pack_body,
            [sds((8, 40, SLAB + 2 * HID), BF16)],
            *late([q2, k2, v2, gate2, up2]), placed,
            scratch=[pltpu.VMEM(a.shape, F32) for a in (q2, k2, v2, gate2, up2)], name="pack",
        )
    )[0]
    packed = lax.all_to_all(packed, "ctx", 0, 0, tiled=True)

    x_late, seg_late, wo, wd, i_late, c_late = order((x_own, segments, wo, wd, i, c_own))
    o_own = wo.reshape(-1, 128)
    o_one, o_two = pz(o_own, 1), pz(o_own, 2)
    c_near = pc(c_late, 2), pc(c_late, 4)
    seg = jnp.broadcast_to(seg_late.reshape(ROWS, 1).astype(BF16), (ROWS, 128))
    x_sent = order.then(jnp.concatenate([x_late, seg], 1))
    d_own = order.then(order(wd).reshape(SUB, W))
    packed, o_one, o_two = order.wait((packed, o_one, o_two))

    slab, feed = order.then(
        call(unpack_body, [sds((8, 40, SLAB), BF16), sds((288, 2 * HID), BF16)], packed, name="unpack")
    )
    s_one, s_two = pz(slab, 1), pz(slab, 2)
    xs = first_ctx(order(x_sent))

    i_late = order(i_late)
    rel = jnp.array(RELATIVE, jnp.int32)
    positions = ((i_late ^ rel)[:, None] * POS + jnp.arange(POS, dtype=jnp.int32)[None, :]).reshape(LEN)
    half = HEAD_SIZE // 2
    freq = THETA ** (-jnp.arange(half, dtype=F32) * 2.0 / HEAD_SIZE)
    angle = positions.astype(F32)[:, None] * freq[None, :]
    cosine = jnp.tile(jnp.cos(angle), (1, 4))
    sine = jnp.sin(angle)
    sine = jnp.concatenate([-sine, sine, -sine, sine], 1)
    pcol = jnp.broadcast_to(positions.astype(F32)[:, None], (LEN, 128))
    prow = jnp.broadcast_to(positions.astype(F32)[None, :], (8, LEN))
    cosine, sine, pcol, prow = order.then((cosine, sine, pcol, prow))

    c_near = order.wait(c_near)
    s_one = order.wait(s_one)
    o_three = pz(order(o_two), 1)
    s_two = order.wait(s_two)
    s_three = pz(s_two, 1)
    o_three = order.wait(o_three)
    o_sent = order.then(jnp.stack([o_own, o_one, o_two, o_three]))
    d_one, d_two = pz(order(d_own), 1), pz(order(d_own), 2)
    s_three = order.wait(s_three)
    os = first_ctx(order(o_sent))
    xs = order.wait(both_cores(order.wait(xs)))
    xs, slabs = order((xs, (slab, s_one, s_two, s_three)))

    anywhere = pl.BlockSpec(memory_space=pl.ANY)
    vmem = pl.BlockSpec(memory_space=pltpu.VMEM)
    held = [
        sds((MICRO, LEN, QK), BF16),
        sds((MICRO, LEN, 128), BF16),
        sds((ALL, W), BF16),
        sds((MICRO, 3, LEN, LEN), BF16),
        sds((ALL, W), BF16),
    ]
    att, gains, w_slab, qk, v, acted, probs, call_x = order.then(
        call(
            attend_body,
            [sds((LEN, 2 * HG), BF16), sds((8, W), F32), sds((W, SLAB), BF16)]
            + [hbm(o.shape, o.dtype) for o in held],
            sc, *late(xs), *late(slabs), cosine, sine, pcol, prow,
            out_specs=[vmem] * 3 + [anywhere] * 5,
            scratch=[pltpu.VMEM(o.shape, o.dtype) for o in held]
            + [pltpu.VMEM((8, ROWS, 128), BF16), pltpu.VMEM((MICRO, LEN, HG), BF16), pltpu.SemaphoreType.DMA((5,))],
            name="attend",
        )
    )
    att, d_one, d_two = order.wait((att, d_one, d_two))
    heads = first_ctx(att)
    os = order.wait(os)
    g_one, g_two = pz(order(feed), 1), pz(order(feed), 2)
    os = order.wait(both_cores(os))
    w_out = order.then(
        call(
            output_weight_body, [sds((W, W), BF16)], sc, *late(os),
            scratch=[pltpu.VMEM((8, 4, wo.size // 128, 128), F32)], name="output_weight",
        )
    )[0]
    d_three = order.wait(pz(d_two, 1))
    acted_t = order.then(transpose(order(acted)))
    heads[1], heads[2] = order.wait((heads[1], heads[2]))
    heads = order.wait(both_cores(order.wait(heads)))
    g_two = order.wait(g_two)
    g_three = pz(g_two, 1)
    cs = [c_late, *c_near, pc(order(c_late), 6)]
    g_three, d_three = order.wait((g_three, d_three))

    att_full, mixed, res_own = order.then(run_project(sc, *late([call_x]), late(heads), w_out, gains))
    wo_own = order.then(lax.dynamic_slice(order(w_out), (jnp.minimum(i, KEY_HEADS - 1) * HG, 0), (HG, W)))
    call_c = order.then(join(late(order(both_cores(order.wait(cs))))))
    feeds = order((feed, g_one, g_two, g_three, d_own, d_one, d_two, d_three))
    hidden, dgu, pm, pe, down, dots_two = order.then(run_feed(sc, mixed, call_c, feeds))

    got = pc(pe, 1)
    grad_gu = order.then(lax.dot_general(order(mixed), dgu, TN, preferred_element_type=F32).astype(BF16))
    terms = send_ctx(order.then(scatter_ctx(pm, order(got))))
    grad_dn = order.then(lax.dot_general(order(hidden), call_c, TN, preferred_element_type=F32).astype(BF16))
    feed_blocks = order.then(
        call(grads_body, [hbm((FEED, 2 * HID), BF16)] * 4, sc, grad_gu, grad_dn, name="grads")
    )
    feed_far = pz(feed_blocks[3], 1)
    att_t = order.then(transpose(order(att_full)))
    feed_mid = order.then(add_low(feed_blocks[2], order(feed_far)))
    feed_terms = (feed_blocks[0], pz(after(feed_blocks[1], feed_mid), 1), pz(feed_mid, 2))
    dres, low = order.then(
        call(
            mid_body, [hbm((ROWS, W), F32), hbm((ROWS, W), BF16)],
            *order(terms), *late([c_own, res_own]), gains, name="mid",
        )
    )
    lows = first_ctx(low)

    om_p, oe_p = order.then(onward(order(hidden), down, "outward"))
    out_got = pc(oe_p, 1)
    out_terms = send_ctx(order.then(scatter_ctx(om_p, order(out_got))))
    lows = both_cores(order(lows))

    dqkv, *slab_blocks = order.then(
        call(
            back_body,
            [sds((ALL, SLAB), BF16)] + [sds((EDGE, BACK), BF16)] * 4,
            sc, *late(order(lows)), wo_own, qk, v, probs, cosine, sine, acted_t, att_t, w_slab, gains, dots_two,
            scratch=[
                pltpu.VMEM((ALL, 256), BF16),
                pltpu.VMEM((4, 8, 288), F32),
                pltpu.VMEM((4, EDGE - 288, BACK), F32),
            ],
            name="back",
        )
    )
    slab_far = pz(slab_blocks[3], 1)
    hid_sum, grad_down = order.then(
        call(
            split_feed_body, [sds((8, CHUNK, 2 * HID), BF16), sds((864, 128), F32)],
            *order(feed_terms), name="split_feed",
        )
    )
    hid_sum = lax.all_to_all(hid_sum, "ctx", 0, 0, tiled=True)
    dam, dae = order.then(onward(order(dqkv), w_slab, "inward"))
    in_got = pc(dae, 1)
    slab_mid = order.then(add_low(slab_blocks[2], order(slab_far)))
    slab_terms = (slab_blocks[0], pz(after(slab_blocks[1], slab_mid), 1), pz(slab_mid, 2))
    in_terms = send_ctx(order.then(scatter_ctx(dam, order(in_got))))

    outputs = order.then((res_own + sum(t.astype(F32) for t in order(out_terms))).astype(BF16))
    grad_gate, grad_up = order.then(
        call(unpack_hidden_body, [sds((864, 128), F32), sds((864, 128), F32)], order(hid_sum), name="unpack_hidden")
    )
    slab = order.then(call(split_back_body, [sds((8, 40, BACK), BF16)], *order(slab_terms), name="split_back"))[0]
    slab = lax.all_to_all(slab, "ctx", 0, 0, tiled=True)
    input_grad = order.then(
        call(last_body, [sds((ROWS, W), BF16)], *late([*order(in_terms), x_own, dres]), gains, name="last")
    )[0]
    grad_q, grad_k, grad_v, grad_out, grad_gains = call(
        unpack_back_body,
        [sds((324, 128), F32), sds((108, 128), F32), sds((108, 128), F32), sds((324, 128), F32), sds((8, 128), F32)],
        order(slab), name="unpack_back",
    )
    grad_gains = grad_gains[0, :72]

    shape = (MICRO, 1, POS, W)
    return (
        outputs.reshape(shape),
        input_grad.reshape(shape),
        grad_q.reshape(-1),
        grad_k.reshape(-1),
        grad_v.reshape(-1),
        grad_out.reshape(-1),
        grad_gate.reshape(-1),
        grad_up.reshape(-1),
        grad_down.reshape(-1),
        grad_gains,
    )


def solution(mesh):
    in_specs = (
        P(None, "grp", "ctx", None),
        P(None, "grp", "ctx"),
        P(("grp", "ctx")),
        P(("grp", "ctx")),
        P(("grp", "ctx")),
        P(("grp", "ctx")),
        P(("grp", "ctx")),
        P(("grp", "ctx")),
        P(("grp", "ctx")),
        P(("grp", "ctx")),
        P(None, "grp", "ctx", None),
    )
    out_specs = (
        P(None, "grp", "ctx", None),
        P(None, "grp", "ctx", None),
        P(("grp", "ctx")),
        P(("grp", "ctx")),
        P(("grp", "ctx")),
        P(("grp", "ctx")),
        P(("grp", "ctx")),
        P(("grp", "ctx")),
        P(("grp", "ctx")),
        P(("grp", "ctx")),
    )
    fits = (mesh.shape["ctx"], mesh.shape["grp"]) == (8, 4)
    return jax.shard_map(
        fast_local if fits else local,
        mesh=mesh,
        in_specs=in_specs,
        out_specs=out_specs,
        check_vma=False,
    )
```
